32 devices in a mesh: batch: 4 (over x, core), seq: 8 (over z, y).
Axes of the slice: x: 2, y: 2, z: 4, core: 2. Of those that a mesh axis runs over, the one named last changes fastest.
Arguments:
- block_in: bfloat16 [8, 2048, 1536], P('batch', 'seq'), may hold values from -6 to 6
- lengths: int32 [8], replicated, may hold values from 512 to 2048, as said below
- norm_gain: bfloat16 [1536], P(('batch', 'seq')), may hold values from 0.5 to 1.5
- in_weight: bfloat16 [1536, 6448], P(('batch', 'seq')), may hold values from -0.15625 to 0.15625
- conv_weight: bfloat16 [4, 3328], P(None, ('batch', 'seq')), may hold values from -3 to 3
- conv_bias: bfloat16 [3328], P(('batch', 'seq')), may hold values from -3 to 3
- step_bias: float32 [48], replicated, may hold values from -8 to -3
- decay_log: float32 [48], replicated, may hold values from 0 to 2.77
- skip_gain: float32 [48], replicated, may hold values from 0.5 to 1.5
- out_gain: bfloat16 [3072], P(('batch', 'seq')), may hold values from 0.5 to 1.5
- out_weight: bfloat16 [3072, 1536], P(('batch', 'seq')), may hold values from -0.109375 to 0.109375
- grad_out: bfloat16 [8, 2048, 1536], P('batch', 'seq'), may hold values from -6 to 6
Outputs:
- block_out: bfloat16 [8, 2048, 1536], P('batch', 'seq')
- grad_in: bfloat16 [8, 2048, 1536], P('batch', 'seq')
- grad_norm_gain: float32 [1536], P(('batch', 'seq'))
- grad_in_weight: float32 [1536, 6448], P(('batch', 'seq'))
- grad_conv_weight: float32 [4, 3328], P(None, ('batch', 'seq'))
- grad_conv_bias: float32 [3328], P(('batch', 'seq'))
- grad_step_bias: float32 [48], replicated
- grad_decay_log: float32 [48], replicated
- grad_skip_gain: float32 [48], replicated
- grad_out_gain: float32 [3072], P(('batch', 'seq'))
- grad_out_weight: float32 [3072, 1536], P(('batch', 'seq'))
- rms_stats: float32 [3], replicated
The draws below stay inside these ranges and needn't reach their ends.
Inputs may be any that keep to these rules, and one draw needn't show every extreme that they name: `lengths`: among the 2 slots of each batch index, one drawn from the seed has length 2048.
All inputs are finite; a program needn't handle non-finite values.
Results may differ from the reference program's by a relative error of at most 0.0064.
Values may be sent and summed in bfloat16 or wider, within the bound.
No kernel may reach another device: no remote copies, remote signals or barrier semaphores. Data moves between devices by JAX's collectives and lax.ppermute only.
A program may use at most 256 MiB of HBM per device.

```python
import jax
import jax.numpy as jnp
from jax import lax

D = 1536
H = 48
P_SIZE = 64
NS = 128
CONV = 4
SPAN = 256
L = 2048
SLOT_DEV = 2
Q = 256
E = 3072
CH = 3328
PROJ = 6448
SLOTS = 8


def draw_lengths(key, part):
    key = jax.random.fold_in(key, 11)
    drawn_lengths = jax.random.randint(jax.random.fold_in(key, 1), (SLOTS,), L // 4, L + 1)
    groups = SLOTS // SLOT_DEV
    chosen = jax.random.randint(jax.random.fold_in(key, 2), (groups,), 0, SLOT_DEV)
    short_group = jax.random.randint(jax.random.fold_in(key, 3), (), 0, groups)
    slot_index = jnp.arange(SLOTS, dtype=jnp.int32)
    slot_rank = slot_index % SLOT_DEV
    group_index = slot_index // SLOT_DEV
    chosen_each = jnp.repeat(chosen, SLOT_DEV, total_repeat_length=SLOTS)
    longest = slot_rank == chosen_each
    shortest = (group_index == short_group) & (slot_rank == (chosen_each + 1) % SLOT_DEV)
    shaped = jnp.where(shortest, L // 4, drawn_lengths)
    return jnp.where(longest, L, shaped).astype(jnp.int32)


def block_scale(own_key, dims, split, smallest, top_value):
    gain = 1.0
    for position, blocks in split:
        draws = jax.random.uniform(jax.random.fold_in(jax.random.fold_in(own_key, 6), position), (blocks,), jnp.float32, smallest / len(split), top_value / len(split))
        gain = gain * jnp.repeat(jnp.exp(draws), dims[position] // blocks).reshape((-1,) + (1,) * (len(dims) - 1 - position))
    return gain


def gaussian(key, dims, width, limit, shards=(), held_as=jnp.bfloat16):
    entries = jax.random.normal(key, dims, jnp.float32) * width
    if len(shards) > 0:
        entries = block_scale(key, dims, shards, -0.22, 0.18) * entries
    return jnp.clip(entries, min=-limit, max=limit).astype(held_as)


def setup_inputs(seed: int = 0) -> dict:
    key_list = jax.random.split(jax.random.key(seed), 13)
    block_in = gaussian(key_list[0], (SLOTS, L, D), 1.0, 6.0, ((0, 4), (1, 8)))
    lengths = draw_lengths(jax.random.fold_in(key_list[12], 71), 0)
    norm_gain = jnp.clip(1.0 + 0.1 * jax.random.normal(key_list[2], (D,), jnp.float32), 0.5, 1.5).astype(jnp.bfloat16)
    in_weight = gaussian(key_list[3], (D, PROJ), D ** -0.5, 0.15625, ((0, 32),))
    conv_weight = gaussian(key_list[4], (CONV, CH), CONV ** -0.5, 3.0, ((1, 32),))
    conv_bias = gaussian(key_list[5], (CH,), 0.5, 3.0, ((0, 32),))
    step_bias = jnp.clip(jax.random.uniform(key_list[6], (H,), jnp.float32, -8.0, -3.0), -8.0, -3.0)
    decay_log = jnp.clip(jax.random.uniform(key_list[7], (H,), jnp.float32, 0.0, 2.77), 0.0, 2.77)
    skip_gain = jnp.clip(jax.random.uniform(key_list[8], (H,), jnp.float32, 0.5, 1.5), 0.5, 1.5)
    out_gain = jnp.clip(1.0 + 0.1 * jax.random.normal(key_list[9], (E,), jnp.float32), 0.5, 1.5).astype(jnp.bfloat16)
    out_weight = gaussian(key_list[10], (E, D), E ** -0.5, 0.109375, ((0, 32),))
    grad_out = gaussian(key_list[11], (SLOTS, L, D), 1.0, 6.0, ((0, 4), (1, 8)))
    return dict(block_in=block_in, lengths=lengths, norm_gain=norm_gain, in_weight=in_weight, conv_weight=conv_weight, conv_bias=conv_bias, step_bias=step_bias, decay_log=decay_log, skip_gain=skip_gain, out_gain=out_gain, out_weight=out_weight, grad_out=grad_out)


EPSILON = 1e-05
PRECISE = lax.Precision.HIGHEST

@jax.custom_vjp
def low(v):
    return lax.optimization_barrier(v.astype(jnp.bfloat16)).astype(jnp.float32)

@jax.custom_vjp
def low_back(v):
    return v

def low_keep(v):
    return (low(v), None)

def low_pass(kept, grad):
    return (grad,)

def back_keep(v):
    return (v, None)

def back_low(kept, grad):
    return (low(grad),)
low.defvjp(low_keep, low_pass)
low_back.defvjp(back_keep, back_low)

def pre_norm(residual, gain_vec):
    inv_scale = lax.rsqrt(lax.optimization_barrier(jnp.mean(residual * residual, axis=-1, keepdims=True)) + EPSILON)
    return residual * inv_scale * gain_vec

def gate_norm(ssm_out, gate_in, gain_vec):
    gated_out = ssm_out * jax.nn.silu(gate_in)
    inv_scale = lax.rsqrt(lax.optimization_barrier(jnp.mean(gated_out * gated_out, axis=-1, keepdims=True)) + EPSILON)
    return gated_out * inv_scale * gain_vec

def conv_apply(padded, weight, bias_vec, row_count):
    running = bias_vec
    for offset in range(CONV):
        running = running + weight[offset] * padded[..., offset:offset + row_count, :]
    return jax.nn.silu(running)

def unpack_slot(conv_out, step_raw, step_bias, decay_log):
    row_count = conv_out.shape[0]
    heads_in = conv_out[:, :E].reshape(row_count, H, P_SIZE)
    write_vec = conv_out[:, E:E + NS]
    read_vec = conv_out[:, E + NS:]
    step_size = jax.nn.softplus(step_raw + step_bias)
    log_decay = -step_size * jnp.exp(decay_log)
    return (heads_in, write_vec, read_vec, step_size, log_decay)

def intra_part(heads_in, write_vec, read_vec, step_size, log_decay):
    row_count = heads_in.shape[0]
    cumulative = jnp.cumsum(log_decay, axis=0)
    causal = jnp.arange(row_count)[:, None] >= jnp.arange(row_count)[None, :]
    differ = cumulative[:, None, :] - cumulative[None, :, :]
    segment = jnp.exp(jnp.where(causal[:, :, None], differ, -jnp.inf))
    intersection = jnp.dot(read_vec, write_vec.T, precision=PRECISE)
    mixing = segment * intersection[:, :, None] * step_size[None, :, :]
    inner_out = jnp.einsum('tsh,shp->thp', mixing, heads_in, precision=PRECISE)
    tail_weight = jnp.exp(cumulative[-1][None, :] - cumulative) * step_size
    fresh_state = jnp.einsum('sh,shp,sn->hpn', tail_weight, heads_in, write_vec, precision=PRECISE)
    return (cumulative, inner_out, fresh_state)

def finish_part(carry_state, cumulative, read_vec, inner_out, fresh_state):
    from_state = jnp.exp(cumulative)[:, :, None] * jnp.einsum('tn,hpn->thp', read_vec, carry_state, precision=PRECISE)
    next_state = jnp.exp(cumulative[-1])[:, None, None] * carry_state + fresh_state
    return (next_state, inner_out + from_state)

def block_forward(params, residual, valid_mask):
    norm_gain, in_weight, conv_weight, conv_bias, step_bias, decay_log, skip_gain, out_gain, out_weight = params
    normed = low(pre_norm(residual, norm_gain))
    projected = low_back(jnp.dot(normed, in_weight, precision=PRECISE))
    gate_in = projected[:, :E]
    conv_in = projected[:, E:E + CH]
    step_raw = projected[:, E + CH:]
    padded = jnp.concatenate([jnp.zeros((CONV - 1, CH), jnp.float32), conv_in], axis=0)
    conv_out = conv_apply(padded, conv_weight, conv_bias, L)
    heads_in, write_vec, read_vec, step_size, log_decay = unpack_slot(conv_out, step_raw, step_bias, decay_log)
    block_rows = min(Q, SPAN)
    blocks = L // block_rows

    def span_step(carry_state, slot_item):
        heads_part, write_part, read_part, step_part, decay_part = slot_item
        cumulative, inner_out, fresh_state = intra_part(heads_part, write_part, read_part, step_part, decay_part)
        return finish_part(carry_state, cumulative, read_part, inner_out, fresh_state)
    _, mixed_out = lax.scan(jax.checkpoint(span_step), jnp.zeros((H, P_SIZE, NS), jnp.float32), (heads_in.reshape(blocks, block_rows, H, P_SIZE), write_vec.reshape(blocks, block_rows, NS), read_vec.reshape(blocks, block_rows, NS), step_size.reshape(blocks, block_rows, H), log_decay.reshape(blocks, block_rows, H)))
    ssm_out = (mixed_out.reshape(L, H, P_SIZE) + skip_gain[:, None] * heads_in).reshape(L, E)
    mixer_in = low(gate_norm(ssm_out, gate_in, out_gain))
    mixer_out = jnp.dot(mixer_in, out_weight, precision=PRECISE)
    return (valid_mask * (residual + mixer_out), mixer_out)

def reference(block_in, lengths, norm_gain, in_weight, conv_weight, conv_bias, step_bias, decay_log, skip_gain, out_gain, out_weight, grad_out):
    params = tuple((entry.astype(jnp.float32) for entry in (norm_gain, in_weight, conv_weight, conv_bias, step_bias, decay_log, skip_gain, out_gain, out_weight)))
    positions = jnp.arange(L, dtype=jnp.int32)

    def per_slot(hop_carry, slot_item):
        stat_sums, grad_sums = hop_carry
        slot_in, slot_grad, length = slot_item
        residual = slot_in.astype(jnp.float32)
        cotangent = slot_grad.astype(jnp.float32)
        valid_mask = (positions < length).astype(jnp.float32)[:, None]

        def forward(weights, inputs):
            return block_forward(weights, inputs, valid_mask)
        block_value, pull_back, mixer_out = jax.vjp(forward, params, residual, has_aux=True)
        grad_params, grad_resid = pull_back(cotangent)
        local_sums = jnp.stack([jnp.sum(valid_mask * residual * residual), jnp.sum(valid_mask * mixer_out * mixer_out), jnp.sum(block_value * block_value)])
        grad_sums = jax.tree.map(lambda running, addend: running + addend, grad_sums, grad_params)
        return ((stat_sums + local_sums, grad_sums), (block_value.astype(jnp.bfloat16), grad_resid.astype(jnp.bfloat16)))
    start = (jnp.zeros((3,), jnp.float32), jax.tree.map(jnp.zeros_like, params))
    (stat_sums, grad_sums), (block_out, grad_in) = lax.scan(per_slot, start, (block_in, grad_out, lengths))
    token_total = jnp.sum(lengths).astype(jnp.float32) * D
    rms_stats = jnp.sqrt(stat_sums / token_total)
    g_norm, g_in_w, g_conv_w, g_conv_b, g_step, g_decay, g_skip, g_out_gain, g_out_w = grad_sums
    return (block_out, grad_in, g_norm, g_in_w, g_conv_w, g_conv_b, g_step, g_decay, g_skip, g_out_gain, g_out_w, rms_stats)
```

```python
import functools

import jax
import jax.numpy as jnp
from jax import lax
from jax.experimental import pallas as pl
from jax.experimental.pallas import tpu as pltpu
from jax.sharding import Mesh
from jax.sharding import PartitionSpec as P

H = 48
P_SIZE = 64
NS = 128
CONV = 4
SPAN = 256
E = 3072
CH = 3328

HC = H // 2
EC = E // 2
HALO = 8
OWN = EC
STEP = EC + NS
OTHER = EC + 2 * NS
WIDE = EC + 3 * NS
BACK = EC + 2 * NS

EPSILON = 1e-05
BF16 = jnp.bfloat16
F32 = jnp.float32
VMEM_LIMIT = 56 * 1024 * 1024


def others(piece, axis):
    size = lax.axis_size(axis)
    here = lax.axis_index(axis)
    moved = []
    for step in range(1, size):
        route = [(i, (i + step) % size) for i in range(size)]
        moved.append((lax.rem(here - step + size, size), lax.ppermute(piece, axis, route)))
    return moved


def place(buffer, piece, index):
    return lax.dynamic_update_slice(buffer, piece, index)


def by_index(axis, mine, other):
    first = lax.axis_index(axis) == 0
    return jnp.where(first, jnp.stack([mine, other]), jnp.stack([other, mine]))


def swapped(piece, axis):
    return lax.ppermute(piece, axis, [(0, 1), (1, 0)])


def gather_chips(pieces, inner):
    _, rows, columns = pieces.shape
    nx, nz, ny = lax.axis_size("x"), lax.axis_size("z"), lax.axis_size("y")
    ix, iz, iy = lax.axis_index("x"), lax.axis_index("z"), lax.axis_index("y")
    line = jnp.zeros((2, nz, rows, columns), pieces.dtype)
    line = place(line, pieces[:, None], (0, iz, 0, 0))
    for index, moved in others(pieces, "z"):
        line = place(line, moved[:, None], (0, index, 0, 0))
    if inner:
        whole = jnp.zeros((nx, nz, ny, 2, rows, columns), pieces.dtype)
    else:
        whole = jnp.zeros((nx, 2, nz, ny, rows, columns), pieces.dtype)
    for half, (first, second) in enumerate((("y", "x"), ("x", "y"))):
        held = [((ix, iy), line[half])]
        for axis in (first, second):
            more = []
            for (at_x, at_y), piece in held:
                for index, moved in others(piece, axis):
                    more.append(((index, at_y) if axis == "x" else (at_x, index), moved))
            held = held + more
        for (at_x, at_y), piece in held:
            if inner:
                whole = place(whole, piece[None, :, None, None], (at_x, 0, at_y, half, 0, 0))
            else:
                whole = place(whole, piece[None, None, :, None], (at_x, half, 0, at_y, 0, 0))
    return whole


def take(value, index, axis):
    return lax.dynamic_index_in_dim(value, index, axis, keepdims=False)


def add_up(mine, moved):
    total = mine.astype(F32)
    for piece in moved:
        total = total + piece.astype(F32)
    return total


def sent_to(value, axis, dim):
    size = lax.axis_size(axis)
    here = lax.axis_index(axis)
    moved = []
    for step in range(1, size):
        route = [(i, (i + step) % size) for i in range(size)]
        moved.append(lax.ppermute(take(value, lax.rem(here + step, size), dim), axis, route))
    return take(value, here, dim), moved


def scatter_chips(whole, inner):
    shares = []
    for half, (first, second) in enumerate((("x", "y"), ("y", "x"))):
        part = whole[:, :, :, half] if inner else whole[:, half]
        for axis in (first, second):
            dim = 0 if axis == "x" else (2 if axis == first or first == "y" else 1)
            if axis == "y":
                dim = part.ndim - 3
            mine, moved = sent_to(part, axis, dim)
            part = add_up(mine, moved).astype(whole.dtype)
        mine, moved = sent_to(part, "z", 0)
        shares.append(add_up(mine, moved))
    return jnp.stack(shares)


def sum_everywhere(value):
    for axis in ("core", "x", "y", "z"):
        size = lax.axis_size(axis)
        step = 1
        while step < size:
            route = [(i, i ^ step) for i in range(size)]
            value = value + lax.ppermute(value, axis, route)
            step *= 2
    return value


def gather_small(piece):
    count = piece.shape[0]
    sizes = [lax.axis_size(a) for a in ("x", "core", "z", "y")]
    held = piece.reshape(1, 1, 1, 1, count)
    for dim, axis in ((2, "z"), (3, "y"), (0, "x"), (1, "core")):
        dims = list(held.shape)
        dims[dim] = lax.axis_size(axis)
        zero = (0,) * 5
        wide = jnp.zeros(dims, piece.dtype)
        at = list(zero)
        at[dim] = lax.axis_index(axis)
        wide = place(wide, held, at)
        for index, moved in others(held, axis):
            at = list(zero)
            at[dim] = index
            wide = place(wide, moved, at)
        held = wide
    return held.reshape(sizes[0] * sizes[1] * sizes[2] * sizes[3], count)


def nn(a, b):
    return lax.dot_general(a, b, (((1,), (0,)), ((), ())), preferred_element_type=F32)


def nt(a, b):
    return lax.dot_general(a, b, (((1,), (1,)), ((), ())), preferred_element_type=F32)


def tn(a, b):
    return lax.dot_general(a, b, (((0,), (0,)), ((), ())), preferred_element_type=F32)


def pieces_of(value, count):
    parts = []
    rest = value
    for index in range(count):
        part = rest.astype(BF16)
        parts.append(part)
        if index < count - 1:
            rest = rest - part.astype(F32)
    return parts


def head_map():
    row = lax.broadcasted_iota(jnp.int32, (NS, EC), 0)
    lane = lax.broadcasted_iota(jnp.int32, (NS, EC), 1)
    inside = (lane >= row * P_SIZE) & (lane < row * P_SIZE + P_SIZE)
    return jnp.where(inside, 1.0, 0.0).astype(BF16)


def spread(value, heads, count=2):
    return sum(nn(part, heads) for part in pieces_of(value, count))


def gathered_heads(value, heads, count=2):
    return sum(nt(part, heads) for part in pieces_of(value, count))


def triangle(kind):
    row = lax.broadcasted_iota(jnp.int32, (SPAN, SPAN), 0)
    col = lax.broadcasted_iota(jnp.int32, (SPAN, SPAN), 1)
    keep = {"ge": row >= col, "gt": row > col, "le": row <= col}[kind]
    return jnp.where(keep, 1.0, 0.0)


def exact_sum(matrix, value):
    low = matrix.astype(BF16)
    return sum(nn(low, part) for part in pieces_of(value, 3))


def sigmoid(v):
    return 1.0 / (1.0 + jnp.exp(-v))


def softplus(v):
    return jnp.maximum(v, 0.0) + jnp.log1p(jnp.exp(-jnp.abs(v)))


def call(kernel, grid, in_specs, out_specs, out_shape, scratch=(), flops=0, moved=0, **more):
    return pl.pallas_call(
        kernel,
        grid=grid,
        in_specs=in_specs,
        out_specs=out_specs,
        out_shape=out_shape,
        scratch_shapes=list(scratch),
        compiler_params=pltpu.CompilerParams(vmem_limit_bytes=VMEM_LIMIT),
        cost_estimate=pl.CostEstimate(flops=flops, bytes_accessed=moved, transcendentals=0),
        **more,
    )


def shape(*dims, dtype=F32):
    return jax.ShapeDtypeStruct(dims, dtype)


def fixed(*dims):
    return pl.BlockSpec(dims, lambda *_: (0,) * len(dims))


def conv_kernel(rows, nz, proj, taps, heads_par, x_out, bc_out, step_out, cum_out, state_out, local_out, total_out):
    heads = head_map()
    spans = rows // SPAN
    lower = triangle("ge")
    state = jnp.zeros((NS, EC), F32)
    total = jnp.zeros((1, NS), F32)
    core_one = heads_par[3:4, :] > 0.5
    for span in range(spans):
        start = HALO + span * SPAN

        def activated(first, width):
            running = taps[4:5, first : first + width]
            for k in range(CONV):
                at = start - (CONV - 1) + k
                running = running + taps[k : k + 1, first : first + width] * proj[0, at : at + SPAN, first : first + width]
            return running * sigmoid(running)

        own = activated(OWN, NS)
        other = activated(OTHER, NS)
        write = jnp.where(core_one, other, own).astype(BF16)
        read = jnp.where(core_one, own, other).astype(BF16)
        here = slice(span * SPAN, span * SPAN + SPAN)
        bc_out[0, here, :NS] = write
        bc_out[0, here, NS:] = read
        raw = proj[0, start : start + SPAN, STEP : STEP + NS] + heads_par[0:1, :]
        step = softplus(raw)
        cum = exact_sum(lower, -step * heads_par[1:2, :])
        step_out[0, here] = step
        cum_out[0, here] = cum
        last = cum[SPAN - 1 : SPAN]
        tail = jnp.exp(last - cum) * step
        local_out[0, span] = state.astype(BF16)
        decay = spread(jnp.broadcast_to(jnp.exp(last), (8, NS)), heads)[0:1]
        wide = EC // 2
        fresh = []
        for half in range(2):
            cols = slice(half * wide, half * wide + wide)
            x = activated(half * wide, wide)
            x_out[0, here, cols] = x.astype(BF16)
            tail_wide = sum(nn(part, heads[:, cols]) for part in pieces_of(tail, 2))
            fresh.append(tn(write, (x * tail_wide).astype(BF16)))
        state = state * decay + jnp.concatenate(fresh, axis=1)
        total = total + last
    depth = NS // nz
    for group in range(nz):
        state_out[group, 0] = state[group * depth : (group + 1) * depth].astype(BF16)
    total_out[0] = jnp.broadcast_to(total, (8, NS))


def intra_kernel(x_ref, bc_ref, step_ref, cum_ref, heads_par, out_ref, xs_ref, cross_ref, cumt_ref):
    heads = head_map()
    step_wide = spread(step_ref[0], heads)
    xs_ref[...] = (x_ref[0].astype(F32) * step_wide).astype(BF16)
    cum = cum_ref[0]
    cumt_ref[...] = cum.T
    cross_ref[...] = nt(bc_ref[0, :, NS:], bc_ref[0, :, :NS]) * triangle("ge")
    skip = spread(jnp.broadcast_to(heads_par[2:3, :], (8, NS)), heads, 3)[0:1]
    out_ref[0] = x_ref[0].astype(F32) * skip
    low = lax.broadcasted_iota(jnp.int32, (SPAN, NS), 1) < P_SIZE

    def pair(p, carry):
        lanes = pl.ds(pl.multiple_of(p * NS, NS), NS)
        xs = xs_ref[:, lanes]
        made = []
        for j in range(2):
            h = 2 * p + j
            col = pltpu.roll(cum, lax.rem(NS - h, NS), 1)[:, 0:1]
            row = cumt_ref[pl.ds(h, 1), :]
            mix = jnp.exp(jnp.minimum(col - row, 0.0)) * cross_ref[...]
            made.append(nn(mix.astype(BF16), xs))
        out_ref[0, :, lanes] += jnp.where(low, made[0], made[1])
        return carry

    lax.fori_loop(0, HC // 2, pair, 0)


def span_state(state_ref, local_ref, before, heads):
    whole = jnp.concatenate([state_ref[g, 0] for g in range(state_ref.shape[0])], axis=0)
    decay = spread(jnp.broadcast_to(jnp.exp(before), (8, NS)), heads)[0:1]
    return whole.astype(F32) * decay + local_ref[0, 0].astype(F32)


def finish_kernel(part_ref, bc_ref, cum_ref, before_ref, state_ref, local_ref, gate_ref, dmix_ref, gain_ref, out_ref, sums_ref):
    heads = head_map()
    state = span_state(state_ref, local_ref, before_ref[0, 0, 0:1], heads).astype(BF16)
    grown = spread(jnp.exp(cum_ref[0]), heads)
    y = part_ref[0] + grown * nn(bc_ref[0, :, NS:], state)
    out_ref[0] = y
    gate = gate_ref[0]
    gated = y * gate * sigmoid(gate)
    squares = jnp.sum(gated * gated, axis=1, keepdims=True)
    slopes = jnp.sum(gated * gain_ref[0:1, :] * dmix_ref[0], axis=1, keepdims=True)
    lane = lax.broadcasted_iota(jnp.int32, (SPAN, NS), 1)
    sums_ref[0] = jnp.where(lane == 0, squares, jnp.where(lane == 1, slopes, 0.0))


def gate_kernel(
    spans, nz, y_ref, gate_ref, dmix_ref, sums_ref, gain_ref, bc_ref, cum_ref,
    mix_out, dy_out, dgate_out, ggain_out, state_out, local_out, run_ref,
):
    step = pl.program_id(1)
    heads = head_map()
    squares = sums_ref[0, :, 0:1]
    slopes = sums_ref[0, :, 1:2]
    scale = lax.rsqrt(squares / E + EPSILON)
    y = y_ref[0]
    gate = gate_ref[0]
    soft = sigmoid(gate)
    silu = gate * soft
    gated = y * silu
    gain = gain_ref[0:1, :]
    dmix = dmix_ref[0]
    mix_out[0] = (gated * scale * gain).astype(BF16)
    dgated = scale * (gain * dmix - gated * (scale * scale * slopes / E))
    dy = dgated * silu
    dy_out[0] = dy.astype(BF16)
    dgate_out[0] = (dgated * y * (soft * (1.0 + gate * (1.0 - soft)))).astype(BF16)

    @pl.when((step == 0) & (pl.program_id(0) == 0))
    def _():
        ggain_out[...] = jnp.zeros_like(ggain_out)

    ggain_out[...] += jnp.broadcast_to(jnp.sum(gated * scale * dmix, axis=0, keepdims=True), (8, EC))

    @pl.when(step == 0)
    def _():
        run_ref[...] = jnp.zeros_like(run_ref)

    cum = cum_ref[0]
    grown = spread(jnp.exp(cum), heads)
    fresh = tn(bc_ref[0, :, NS:], (dy * grown).astype(BF16))
    local_out[0, 0] = run_ref[...].astype(BF16)
    run_ref[...] = fresh + run_ref[...] * grown[SPAN - 1 : SPAN]

    @pl.when(step == spans - 1)
    def _():
        depth = NS // nz
        for group in range(nz):
            state_out[group, 0] = run_ref[group * depth : (group + 1) * depth].astype(BF16)


def back_kernel(
    x_ref, bc_ref, step_ref, cum_ref, before_ref, dy_ref, state_ref, local_ref,
    dxs_out, dbc_out, dcum_out, xs_ref, cross_ref, dcross_ref, cumt_ref, rows_ref,
):
    heads = head_map()
    cum = cum_ref[0]
    xs_ref[...] = (x_ref[0].astype(F32) * spread(step_ref[0], heads)).astype(BF16)
    cumt_ref[...] = cum.T
    write = bc_ref[0, :, :NS]
    read = bc_ref[0, :, NS:]
    mask = triangle("le")
    cross_ref[...] = nt(write, read) * mask
    dcross_ref[...] = jnp.zeros_like(dcross_ref)
    rows_ref[...] = jnp.zeros_like(rows_ref)
    lane = lax.broadcasted_iota(jnp.int32, (SPAN, NS), 1)
    low = lane < P_SIZE

    def pair(p, cols):
        lanes = pl.ds(pl.multiple_of(p * NS, NS), NS)
        xs = xs_ref[:, lanes]
        dy = dy_ref[0, :, lanes]
        made = []
        for j in range(2):
            h = 2 * p + j
            col = pltpu.roll(cum, lax.rem(NS - h, NS), 1)[:, 0:1]
            row = cumt_ref[pl.ds(h, 1), :]
            decay = jnp.exp(jnp.minimum(row - col, 0.0))
            xs_one = jnp.where(low if j == 0 else ~low, xs, jnp.zeros_like(xs))
            slope = nt(xs_one, dy) * decay
            dcross_ref[...] += slope
            cross = cross_ref[...]
            weight = slope * cross
            rows_ref[pl.ds(h, 1), :] = jnp.sum(weight, axis=0, keepdims=True)
            cols = jnp.where(lane == h, jnp.sum(weight, axis=1, keepdims=True), cols)
            made.append(nn((decay * cross).astype(BF16), dy))
        dxs_out[0, :, lanes] = jnp.where(low, made[0], made[1])
        return cols

    cols = lax.fori_loop(0, HC // 2, pair, jnp.zeros((SPAN, NS), F32))
    dcross = (dcross_ref[...] * mask).astype(BF16)
    state = span_state(state_ref, local_ref, before_ref[0, 0, 0:1], heads).astype(BF16)
    grown = spread(jnp.exp(cum), heads)
    dye = dy_ref[0].astype(F32) * grown
    inter = gathered_heads(dye * nn(read, state), heads)
    dbc_out[0, :, :NS] = nn(dcross, read)
    dbc_out[0, :, NS:] = tn(dcross, write) + nt(dye.astype(BF16), state)
    dcum_out[0] = rows_ref[...].T - cols + inter


def close_kernel(
    rows, nz, x_ref, bc_ref, step_ref, cum_ref, dy_ref, proj_ref, taps, heads_par, dxs_ref, dbc_ref, dcum_ref,
    state_ref, local_ref, back_ref, blocal_ref, dproj_out, dbc_out, gtaps_out, ghead_out, dpre_ref,
):
    heads = head_map()
    spans = rows // SPAN
    upper = triangle("le")
    below = triangle("gt")
    whole_in = jnp.concatenate([state_ref[g, 0] for g in range(nz)], axis=0).astype(F32)
    whole_back = jnp.concatenate([back_ref[g, 0] for g in range(nz)], axis=0).astype(F32)
    lasts = [cum_ref[0, (c + 1) * SPAN - 1 : (c + 1) * SPAN] for c in range(spans)]
    skip = spread(jnp.broadcast_to(heads_par[2:3, :], (8, NS)), heads, 3)[0:1]
    real = lax.broadcasted_iota(jnp.int32, (SPAN, NS), 1) < HC
    dpre_ref[:HALO] = jnp.zeros((HALO, EC), F32)
    dpre_ref[HALO + rows :] = jnp.zeros((HALO, EC), F32)
    zero_row = jnp.zeros((1, NS), F32)
    gbias, gdecay, gskip = zero_row, zero_row, zero_row
    for span in range(spans):
        here = slice(span * SPAN, span * SPAN + SPAN)
        before = sum(lasts[:span], zero_row)
        after = sum(lasts[span + 1 :], zero_row)
        both = spread(jnp.exp(jnp.concatenate([before, after, lasts[span], jnp.zeros((5, NS), F32)], axis=0)), heads)
        state = whole_in * both[0:1] + local_ref[0, span].astype(F32)
        back = whole_back * both[1:2] + blocal_ref[0, span].astype(F32)
        back_low = back.astype(BF16)
        at_last = gathered_heads(
            jnp.broadcast_to(jnp.sum(state * back, axis=0, keepdims=True) * both[2:3], (8, EC)), heads
        )[0:1]
        write = bc_ref[0, here, :NS]
        cum = cum_ref[0, here]
        step = step_ref[0, here]
        x = x_ref[0, here].astype(F32)
        dy = dy_ref[0, here].astype(F32)
        tail = spread(jnp.exp(lasts[span] - cum), heads)
        step_wide = spread(step, heads)
        from_back = tail * nn(write, back_low)
        dxs = dxs_ref[0, here] + from_back
        dstep = gathered_heads(x * dxs, heads)
        moved = step * gathered_heads(x * from_back, heads)
        dbc_out[0, here, :NS] = dbc_ref[0, here, :NS] + nt((x * tail * step_wide).astype(BF16), back_low)
        dbc_out[0, here, NS:] = dbc_ref[0, here, NS:]
        dlog = exact_sum(upper, dcum_ref[0, here]) + exact_sum(below, moved) + at_last
        raw = proj_ref[0, HALO + span * SPAN : HALO + span * SPAN + SPAN, STEP : STEP + NS] + heads_par[0:1, :]
        draw = jnp.where(real, (dstep - heads_par[1:2, :] * dlog) * sigmoid(raw), 0.0)
        dproj_out[0, HALO + span * SPAN : HALO + span * SPAN + SPAN, STEP : STEP + NS] = draw.astype(BF16)
        gbias = gbias + jnp.sum(draw, axis=0, keepdims=True)
        gdecay = gdecay + jnp.sum(jnp.where(real, dlog * (-step * heads_par[1:2, :]), 0.0), axis=0, keepdims=True)
        gskip = gskip + gathered_heads(jnp.broadcast_to(jnp.sum(dy * x, axis=0, keepdims=True), (8, EC)), heads, 3)[0:1]
        dx = dxs * step_wide + skip * dy
        start = HALO + span * SPAN
        pre = taps[4:5, :EC]
        for k in range(CONV):
            at = start - (CONV - 1) + k
            pre = pre + taps[k : k + 1, :EC] * proj_ref[0, at : at + SPAN, :EC]
        soft = sigmoid(pre)
        dpre_ref[start : start + SPAN] = dx * (soft * (1.0 + pre * (1.0 - soft)))
    conv_back(rows, dpre_ref, proj_ref, taps, 0, EC, dproj_out, 0, gtaps_out)
    dproj_out[0, :HALO, STEP : STEP + NS] = jnp.zeros((HALO, NS), BF16)
    ghead_out[0] = jnp.concatenate([gbias, gdecay, gskip, jnp.zeros((5, NS), F32)], axis=0)


def conv_back(rows, dpre_ref, proj_ref, taps, first, width, dproj_out, out_first, gtaps_out):
    sums = [jnp.zeros((1, width), F32)] * (CONV + 1)
    blocks = [(0, HALO)] + [(HALO + s * SPAN, SPAN) for s in range(rows // SPAN)]
    for start, count in blocks:
        running = jnp.zeros((count, width), F32)
        for k in range(CONV):
            at = start + (CONV - 1) - k
            running = running + taps[k : k + 1, first : first + width] * dpre_ref[at : at + count]
        dproj_out[0, start : start + count, out_first : out_first + width] = running.astype(BF16)
        if count == SPAN:
            dpre = dpre_ref[start : start + count]
            for k in range(CONV):
                at = start - (CONV - 1) + k
                sums[k] = sums[k] + jnp.sum(dpre * proj_ref[0, at : at + count, first : first + width], axis=0, keepdims=True)
            sums[CONV] = sums[CONV] + jnp.sum(dpre, axis=0, keepdims=True)
    gtaps_out[0, :, :width] = jnp.concatenate(sums + [jnp.zeros((3, width), F32)], axis=0)


def own_kernel(rows, dproj_in, mine_ref, came_ref, proj_ref, taps, dproj_out, gtaps_out, dpre_ref):
    dpre_ref[:HALO] = jnp.zeros((HALO, NS), F32)
    dpre_ref[HALO + rows :] = jnp.zeros((HALO, NS), F32)
    for span in range(rows // SPAN):
        start = HALO + span * SPAN
        pre = taps[4:5, :]
        for k in range(CONV):
            at = start - (CONV - 1) + k
            pre = pre + taps[k : k + 1, :] * proj_ref[0, at : at + SPAN]
        soft = sigmoid(pre)
        here = slice(span * SPAN, span * SPAN + SPAN)
        dconv = mine_ref[0, here] + came_ref[0, here]
        dpre_ref[start : start + SPAN] = dconv * (soft * (1.0 + pre * (1.0 - soft)))
    conv_back(rows, dpre_ref, proj_ref, taps, 0, NS, dproj_out, 0, gtaps_out)


def dot(a, b):
    return jnp.dot(a, b, preferred_element_type=F32)


def shards(
    block_in,
    lengths,
    norm_gain,
    in_weight,
    conv_weight,
    conv_bias,
    step_bias,
    decay_log,
    skip_gain,
    out_gain,
    out_weight,
    grad_out,
):
    slot_count, row_count, features = block_in.shape
    nx, nz, ny = lax.axis_size("x"), lax.axis_size("z"), lax.axis_size("y")
    ix, iz, iy = lax.axis_index("x"), lax.axis_index("z"), lax.axis_index("y")
    core = lax.axis_index("core")
    rows = ny * row_count
    spans = rows // SPAN
    deep = in_weight.shape[0]
    thin = out_weight.shape[0]

    def half_of(value, width, which):
        parts = value.reshape(value.shape[:-1] + (nx, 2, width // (2 * nx)))
        chosen = take(parts, which, value.ndim)
        return chosen.reshape(value.shape[:-1] + (width // 2,))

    def rows_of(block):
        send = take(block, 1 - iy, 0)
        keep = take(block, iy, 0)
        mine = by_index("y", keep, swapped(send, "y")).reshape(rows, features)
        return mine, by_index("core", mine, swapped(mine, "core"))

    own_in, all_in = rows_of(block_in)
    before_rows = lax.ppermute(all_in[:, rows - HALO :], "z", [(i, i + 1) for i in range(nz - 1)])
    own_grad, all_grad = rows_of(grad_out)

    def in_part(which):
        heads_in = half_of(in_weight[:, E : 2 * E], E, which)
        write = in_weight[:, 2 * E : 2 * E + NS]
        read = in_weight[:, 2 * E + NS : E + CH]
        first = which == 0
        steps = jnp.pad(half_of(in_weight[:, E + CH :], H, which), ((0, 0), (0, NS - HC)))
        scan_part = jnp.concatenate(
            [heads_in, jnp.where(first, write, read), steps, jnp.where(first, read, write)], axis=1
        )
        return scan_part, half_of(in_weight[:, :E], E, which)

    my_scan, my_gate = in_part(core)
    its_scan, its_gate = in_part(1 - core)
    scan_pieces = by_index("core", my_scan, swapped(its_scan, "core"))
    gate_pieces = by_index("core", my_gate, swapped(its_gate, "core"))
    small = jnp.concatenate([norm_gain, conv_weight.reshape(-1), conv_bias, out_gain])
    small_count = small.shape[0]
    small = gather_small(jnp.pad(small, (0, -small_count % 1024)))
    scan_weight = gather_chips(scan_pieces, False).reshape(features, WIDE)
    gate_weight = gather_chips(gate_pieces, False).reshape(features, EC)
    back_weight = gather_chips(out_weight.reshape(2, thin // 2, features), True).reshape(EC, features)

    chan = CH // (2 * nx * nz * ny)
    gain_in = small[:, :deep].reshape(1, features).astype(F32)
    taps_all = small[:, deep : deep + CONV * chan].reshape(-1, CONV, chan).transpose(1, 0, 2).reshape(CONV, CH)
    at = deep + CONV * chan
    bias_all = small[:, at : at + chan].reshape(1, CH)
    gain_out_all = small[:, at + chan : at + chan + thin].reshape(E)
    taps_all = jnp.concatenate([taps_all, bias_all, jnp.zeros((3, CH), BF16)], axis=0).astype(F32)
    own_taps = jnp.where(core == 0, taps_all[:, E : E + NS], taps_all[:, E + NS :])
    other_taps = jnp.where(core == 0, taps_all[:, E + NS :], taps_all[:, E : E + NS])
    taps = jnp.concatenate(
        [half_of(taps_all[:, :E], E, core), own_taps, jnp.zeros((8, NS), F32), other_taps], axis=1
    )
    gain_out = jnp.broadcast_to(half_of(gain_out_all, E, core).astype(F32), (8, EC))

    def head_row(value):
        return jnp.pad(half_of(value, H, core), (0, NS - HC))

    heads_par = jnp.stack(
        [
            head_row(step_bias),
            head_row(jnp.exp(decay_log)),
            head_row(skip_gain),
            jnp.full((NS,), core, F32),
        ]
        + [jnp.zeros((NS,), F32)] * 4
    )

    positions = iz * rows + jnp.arange(rows, dtype=jnp.int32)
    slot_lengths = jnp.stack(
        [take(lengths, (ix * 2 + s) * slot_count + iy, 0) for s in range(2)]
    )
    all_valid = positions[None, :] < slot_lengths[:, None]
    own_valid = (positions < take(slot_lengths, core, 0)).astype(F32)[:, None]

    def scaled(value):
        wide = value.astype(F32)
        return wide * lax.rsqrt(jnp.mean(wide * wide, axis=-1, keepdims=True) + EPSILON)

    joined = jnp.concatenate([before_rows, all_in], axis=1)
    normed = (scaled(joined) * gain_in).astype(BF16)
    tall = HALO + rows
    proj = dot(normed.reshape(2 * tall, features), scan_weight).reshape(2, tall, WIDE)
    d_mix = jnp.where(all_valid[:, :, None], all_grad, jnp.zeros_like(all_grad))

    whole_row = lambda *dims: pl.BlockSpec((1,) + dims, lambda s: (s,) + (0,) * len(dims))
    x, bc, step, cum, state_part, local, total = call(
        functools.partial(conv_kernel, rows, nz),
        (2,),
        [whole_row(tall, WIDE), fixed(8, WIDE), fixed(8, NS)],
        [
            whole_row(rows, EC), whole_row(rows, 2 * NS), whole_row(rows, NS), whole_row(rows, NS),
            pl.BlockSpec((nz, 1, NS // nz, EC), lambda s: (0, s, 0, 0)), whole_row(spans, NS, EC), whole_row(8, NS),
        ],
        [
            shape(2, rows, EC, dtype=BF16), shape(2, rows, 2 * NS, dtype=BF16), shape(2, rows, NS), shape(2, rows, NS),
            shape(nz, 2, NS // nz, EC, dtype=BF16), shape(2, spans, NS, EC, dtype=BF16), shape(2, 8, NS),
        ],
        flops=2 * 2 * rows * EC * NS * 3,
        moved=2 * (tall * WIDE * 4 + rows * EC * 2),
    )(proj, taps, heads_par)

    totals = jnp.zeros((nz, 2, NS), F32)
    totals = place(totals, total[None, :, 0], (iz, 0, 0))
    for index, moved in others(total, "z"):
        totals = place(totals, moved[None, :, 0], (index, 0, 0))
    decays = jnp.exp(totals)[:, :, :HC]
    decays = jnp.broadcast_to(decays[..., None], decays.shape + (P_SIZE,)).reshape(nz, 2, 1, EC)

    def exchange(value):
        return lax.all_to_all(value, "z", 0, 0, tiled=True)

    ends = exchange(state_part).astype(F32)
    running = jnp.zeros_like(ends[0])
    starts = []
    for k in range(nz):
        starts.append(running.astype(BF16))
        running = running * decays[k] + ends[k]
    state_in = exchange(jnp.stack(starts))

    in_span = lambda *dims: pl.BlockSpec((1, SPAN) + dims, lambda s, c: (s, c) + (0,) * len(dims))
    local_span = pl.BlockSpec((1, 1, NS, EC), lambda s, c: (s, c, 0, 0))
    state_spec = pl.BlockSpec((nz, 1, NS // nz, EC), lambda s, c: (0, s, 0, 0))
    before_spec = pl.BlockSpec((1, 1, 8, NS), lambda s, c: (s, c, 0, 0))
    part = call(
        intra_kernel,
        (2, spans),
        [in_span(EC), in_span(2 * NS), in_span(NS), in_span(NS), fixed(8, NS)],
        in_span(EC),
        shape(2, rows, EC),
        [
            pltpu.VMEM((SPAN, EC), BF16), pltpu.VMEM((SPAN, SPAN), F32), pltpu.VMEM((NS, SPAN), F32),
        ],
        flops=2 * rows * SPAN * EC * 2 * 6,
        moved=2 * rows * EC * 6,
    )(x, bc, step, cum, heads_par)

    gate = dot(normed[:, HALO:].reshape(2 * rows, features), gate_weight).reshape(2, rows, EC)
    d_mixer_in = lax.dot_general(
        d_mix.reshape(2 * rows, features), back_weight, (((1,), (1,)), ((), ())), preferred_element_type=F32
    ).reshape(2, rows, EC)
    span_ends = cum.reshape(2, spans, SPAN, NS)[:, :, SPAN - 1]
    before = jnp.cumsum(span_ends, axis=1) - span_ends
    before = jnp.broadcast_to(before[:, :, None], (2, spans, 8, NS))
    ssm_out, sums = call(
        finish_kernel,
        (2, spans),
        [
            in_span(EC), in_span(2 * NS), in_span(NS), before_spec, state_spec, local_span, in_span(EC), in_span(EC),
            fixed(8, EC),
        ],
        [in_span(EC), in_span(NS)],
        [shape(2, rows, EC), shape(2, rows, NS)],
        flops=2 * 2 * rows * EC * NS * 3,
        moved=2 * rows * EC * 16,
    )(part, bc, cum, before, state_in, local, gate, d_mixer_in, gain_out)
    sums = sums + swapped(sums, "core")

    rev = lambda *dims: pl.BlockSpec((1, SPAN) + dims, lambda s, c: (s, spans - 1 - c) + (0,) * len(dims))
    rev_local = pl.BlockSpec((1, 1, NS, EC), lambda s, c: (s, spans - 1 - c, 0, 0))
    mixer_in, d_ssm, d_gate, g_gain_out, back_part, back_local = call(
        functools.partial(gate_kernel, spans, nz),
        (2, spans),
        [rev(EC), rev(EC), rev(EC), rev(NS), fixed(8, EC), rev(2 * NS), rev(NS)],
        [rev(EC), rev(EC), rev(EC), fixed(8, EC), state_spec, rev_local],
        [
            shape(2, rows, EC, dtype=BF16), shape(2, rows, EC, dtype=BF16), shape(2, rows, EC, dtype=BF16), shape(8, EC),
            shape(nz, 2, NS // nz, EC, dtype=BF16), shape(2, spans, NS, EC, dtype=BF16),
        ],
        [pltpu.VMEM((NS, EC), F32)],
        flops=2 * 2 * rows * EC * NS * 3,
        moved=2 * rows * EC * 18,
    )(ssm_out, gate, d_mixer_in, sums, gain_out, bc, cum)

    tails = exchange(back_part).astype(F32)
    running = jnp.zeros_like(tails[0])
    backs = [None] * nz
    for k in reversed(range(nz)):
        backs[k] = running.astype(BF16)
        running = running * decays[k] + tails[k]
    back_in = exchange(jnp.stack(backs))

    flat_mix = mixer_in.reshape(2 * rows, EC)
    flat_dmix = d_mix.reshape(2 * rows, features)
    g_out = lax.dot_general(flat_mix, flat_dmix, (((0,), (0,)), ((), ())), preferred_element_type=BF16)
    g_out = scatter_chips(g_out.reshape(nx, nz, ny, 2, thin // 2, features), True).reshape(thin, features)
    flat_normed = normed.reshape(2 * tall, features)
    g_gate = lax.dot_general(
        normed[:, HALO:].reshape(2 * rows, features), d_gate.reshape(2 * rows, EC), (((0,), (0,)), ((), ())),
        preferred_element_type=BF16,
    )
    g_gate = scatter_chips(g_gate.reshape(nx, 2, nz, ny, deep, EC), False)

    mixer_part = dot(flat_mix, back_weight).reshape(2, rows, features)
    mixer_out = take(mixer_part, core, 0) + swapped(take(mixer_part, 1 - core, 0), "core")
    residual = own_in.astype(F32)
    block_value = own_valid * (residual + mixer_out)
    local_sums = jnp.stack(
        [
            jnp.sum(own_valid * residual * residual),
            jnp.sum(own_valid * mixer_out * mixer_out),
            jnp.sum(block_value * block_value),
        ]
    )

    def slots_of(value):
        parts = value.reshape(ny, row_count, features)
        return by_index("y", take(parts, iy, 0), swapped(take(parts, 1 - iy, 0), "y"))

    block_out = slots_of(block_value.astype(BF16))

    dxs, d_bc, d_cum = call(
        back_kernel,
        (2, spans),
        [in_span(EC), in_span(2 * NS), in_span(NS), in_span(NS), before_spec, in_span(EC), state_spec, local_span],
        [in_span(EC), in_span(2 * NS), in_span(NS)],
        [shape(2, rows, EC), shape(2, rows, 2 * NS), shape(2, rows, NS)],
        [
            pltpu.VMEM((SPAN, EC), BF16), pltpu.VMEM((SPAN, SPAN), F32), pltpu.VMEM((SPAN, SPAN), F32),
            pltpu.VMEM((NS, SPAN), F32), pltpu.VMEM((NS, SPAN), F32),
        ],
        flops=2 * rows * SPAN * EC * 2 * 16,
        moved=2 * rows * EC * 10,
    )(x, bc, step, cum, before, d_ssm, state_in, local)

    slot_state = pl.BlockSpec((nz, 1, NS // nz, EC), lambda s: (0, s, 0, 0))
    d_proj, d_bc, g_taps, g_heads = call(
        functools.partial(close_kernel, rows, nz),
        (2,),
        [
            whole_row(rows, EC), whole_row(rows, 2 * NS), whole_row(rows, NS), whole_row(rows, NS), whole_row(rows, EC),
            whole_row(tall, WIDE), fixed(8, WIDE), fixed(8, NS), whole_row(rows, EC), whole_row(rows, 2 * NS),
            whole_row(rows, NS), slot_state, whole_row(spans, NS, EC), slot_state, whole_row(spans, NS, EC),
        ],
        [whole_row(tall, BACK), whole_row(rows, 2 * NS), whole_row(8, EC), whole_row(8, NS)],
        [shape(2, tall, BACK, dtype=BF16), shape(2, rows, 2 * NS), shape(2, 8, EC), shape(2, 8, NS)],
        [pltpu.VMEM((HALO + rows + HALO, EC), F32)],
        flops=2 * 2 * rows * EC * NS * 8,
        moved=2 * rows * EC * 16,
    )(x, bc, step, cum, d_ssm, proj, taps, heads_par, dxs, d_bc, d_cum, state_in, local, back_in, back_local)

    bc_parts = d_bc.reshape(2, rows, 2, NS)
    mine = jnp.where(core == 0, d_bc[:, :, :NS], d_bc[:, :, NS:])
    theirs = jnp.where(core == 0, d_bc[:, :, NS:], d_bc[:, :, :NS])
    column = pl.BlockSpec((1, tall, NS), lambda s: (s, 0, OWN // NS))
    d_proj, g_own = call(
        functools.partial(own_kernel, rows),
        (2,),
        [pl.BlockSpec(memory_space=pl.ANY), whole_row(rows, NS), whole_row(rows, NS), column, fixed(8, NS)],
        [column, whole_row(8, NS)],
        [shape(2, tall, BACK, dtype=BF16), shape(2, 8, NS)],
        [pltpu.VMEM((HALO + rows + HALO, NS), F32)],
        input_output_aliases={0: 0},
    )(d_proj, mine, swapped(theirs, "core"), proj, own_taps)

    flat_dproj = d_proj.reshape(2 * tall, BACK)
    g_scan = lax.dot_general(flat_normed, flat_dproj, (((0,), (0,)), ((), ())), preferred_element_type=BF16)
    g_scan = scatter_chips(g_scan.reshape(nx, 2, nz, ny, deep, BACK), False)

    d_normed = lax.dot_general(
        flat_dproj, scan_weight[:, :BACK], (((1,), (1,)), ((), ())), preferred_element_type=F32
    ).reshape(2, tall, features)
    d_normed_gate = lax.dot_general(
        d_gate.reshape(2 * rows, EC), gate_weight, (((1,), (1,)), ((), ())), preferred_element_type=F32
    ).reshape(2, rows, features)
    d_normed = jnp.concatenate([d_normed[:, :HALO], d_normed[:, HALO:] + d_normed_gate], axis=1)
    d_own = take(d_normed, core, 0) + swapped(take(d_normed, 1 - core, 0), "core")
    returned = lax.ppermute(d_own[:HALO], "z", [(i + 1, i) for i in range(nz - 1)])
    d_own = jnp.concatenate([d_own[HALO:tall - HALO], d_own[tall - HALO :] + returned], axis=0)

    _, pull_norm = jax.vjp(lambda value, gain: scaled(value) * gain, residual, gain_in)
    d_resid, g_gain_in = pull_norm(d_own)
    grad_in = slots_of((own_valid * own_grad.astype(F32) + d_resid).astype(BF16))

    def spread_half(value, width):
        parts = value.reshape(value.shape[:-1] + (nx, 1, width // (2 * nx)))
        zero = jnp.zeros_like(parts)
        first = core == 0
        both = jnp.concatenate([jnp.where(first, parts, zero), jnp.where(first, zero, parts)], axis=-2)
        return both.reshape(value.shape[:-1] + (width,))

    taps_sum = jnp.sum(g_taps, axis=0)
    own_sum = jnp.sum(g_own, axis=0)
    nothing = jnp.zeros_like(own_sum)
    taps_sum = jnp.concatenate(
        [
            spread_half(taps_sum, E),
            jnp.where(core == 0, own_sum, nothing),
            jnp.where(core == 0, nothing, own_sum),
        ],
        axis=1,
    )
    head_sum = spread_half(jnp.sum(g_heads, axis=0)[:3, :HC], H)
    packed = jnp.concatenate(
        [
            taps_sum[: CONV + 1].reshape(-1),
            spread_half(g_gain_out[0], E),
            g_gain_in.reshape(-1),
            head_sum.reshape(-1),
            local_sums,
        ]
    )
    count = packed.shape[0]
    packed = sum_everywhere(jnp.pad(packed, (0, -count % 1024)).reshape(-1, NS)).reshape(-1)
    place_at = [0]
    for size in ((CONV + 1) * CH, E, features, 3 * H, 3):
        place_at.append(place_at[-1] + size)
    device = ((ix * 2 + core) * nz + iz) * ny + iy
    taps_total = packed[: place_at[1]].reshape(CONV + 1, CH)
    taps_mine = lax.dynamic_slice_in_dim(taps_total, device * chan, chan, 1)
    gain_out_mine = lax.dynamic_slice_in_dim(packed[place_at[1] : place_at[2]], device * thin, thin)
    gain_in_mine = lax.dynamic_slice_in_dim(packed[place_at[2] : place_at[3]], device * deep, deep)
    head_total = packed[place_at[3] : place_at[4]].reshape(3, H)
    valid_sums = packed[place_at[4] : place_at[5]]

    def row_share(value):
        return take(value, core, 0), swapped(take(value, 1 - core, 0), "core")

    scan_mine, scan_came = row_share(g_scan)
    gate_mine, gate_came = row_share(g_gate)

    def both_halves(mine_part, came_part):
        pair = by_index("core", mine_part, came_part)
        width = mine_part.shape[-1]
        return pair.reshape(2, deep, nx, width // nx).transpose(1, 2, 0, 3).reshape(deep, 2 * width)

    own_pair = by_index("core", scan_mine[:, OWN:STEP], scan_came[:, OWN:STEP])
    g_in_weight = jnp.concatenate(
        [
            both_halves(gate_mine, gate_came),
            both_halves(scan_mine[:, :EC], scan_came[:, :EC]),
            own_pair[0],
            own_pair[1],
            both_halves(scan_mine[:, STEP : STEP + HC], scan_came[:, STEP : STEP + HC]),
        ],
        axis=1,
    )
    token_total = jnp.sum(lengths).astype(F32) * features
    rms_stats = jnp.sqrt(valid_sums / token_total)
    return (
        block_out,
        grad_in,
        gain_in_mine,
        g_in_weight,
        taps_mine[:CONV],
        taps_mine[CONV],
        head_total[0],
        head_total[1],
        head_total[2],
        gain_out_mine,
        g_out,
        rms_stats,
    )


def solution(mesh):
    nb, ns = mesh.shape["batch"], mesh.shape["seq"]
    fine = Mesh(mesh.devices.reshape(nb // 2, 2, ns // 2, 2), ("x", "core", "z", "y"))
    batch, seq = ("x", "core"), ("z", "y")
    every = batch + seq
    act = P(batch, seq, None)
    return jax.shard_map(
        shards,
        mesh=fine,
        in_specs=(
            act, P(), P(every), P(every, None), P(None, every), P(every), P(), P(), P(), P(every), P(every, None), act,
        ),
        out_specs=(
            act, act, P(every), P(every, None), P(None, every), P(every), P(), P(), P(), P(every), P(every, None), P(),
        ),
        check_vma=False,
    )
```

```python
import functools
import types

import jax
import jax.numpy as jnp
from jax import lax
from jax.experimental import pallas as pl
from jax.experimental.pallas import tpu as pltpu
from jax.sharding import Mesh
from jax.sharding import PartitionSpec as P

H = 48
P_SIZE = 64
NS = 128
CONV = 4
SPAN = 256
E = 3072
CH = 3328

HC = H // 2
EC = E // 2
HALO = 16
OWN = EC
STEP = EC + NS
OTHER = EC + 2 * NS
WIDE = EC + 3 * NS
BACK = EC + 2 * NS

EPSILON = 1e-05
BF16 = jnp.bfloat16
VM = 60
F32 = jnp.float32


def settle(live):
    live.__dict__.update(lax.optimization_barrier(dict(live.__dict__)))


def others(piece, axis):
    size = lax.axis_size(axis)
    here = lax.axis_index(axis)
    moved = []
    for step in range(1, size):
        route = [(i, (i + step) % size) for i in range(size)]
        moved.append((lax.rem(here - step + size, size), lax.ppermute(piece, axis, route)))
    return moved


def everyone(piece, axis):
    return [(lax.axis_index(axis), piece)] + others(piece, axis)


def shared(value, axes):
    count = 1
    for axis in axes:
        count *= lax.axis_size(axis)
    return lax.all_to_all(jnp.broadcast_to(value, (count,) + value.shape), axes, 0, 0, tiled=True)


def by_index(axis, mine, other):
    first = lax.axis_index(axis) == 0
    return jnp.where(first, jnp.stack([mine, other]), jnp.stack([other, mine]))


def swapped(piece, axis):
    return lax.ppermute(piece, axis, [(0, 1), (1, 0)])


def take(value, index, axis):
    return lax.dynamic_index_in_dim(value, index, axis, keepdims=False)


def copy_plan(items):
    values, scalars, plan = [], [], []
    for piece, source, out, target in items:
        known = [i for i, v in enumerate(values) if v is piece]
        if not known:
            values.append(piece)
            known = [len(values) - 1]
        at = []
        for index in target:
            if index is None or isinstance(index, int):
                at.append(index)
            else:
                scalars.append(index)
                at.append((len(scalars) - 1,))
        plan.append((known[0], source, out, at))
    return values, jnp.stack(scalars).astype(jnp.int32), plan


def copy_all(plan, table, inputs, results, sems):
    copies = []
    for number, (known, source, out, at) in enumerate(plan):
        here = tuple(slice(None) if i is None else i for i in source)
        there = tuple(slice(None) if i is None else (table[i[0]] if isinstance(i, tuple) else i) for i in at)
        origin = inputs[known].at[here] if here else inputs[known]
        copies.append(pltpu.make_async_copy(origin, results[out].at[there], sems.at[number]))
    for copy in copies:
        copy.start()
    for copy in copies:
        copy.wait()


ANYWHERE = pl.BlockSpec(memory_space=pltpu.HBM)
NO_COST = pl.CostEstimate(flops=0, bytes_accessed=1024, transcendentals=0)


def assemble(outs, items, dtype):
    values, table, plan = copy_plan(items)
    count = len(values)

    def kernel(table_ref, *refs):
        copy_all(plan, table_ref, refs[:count], refs[count:-1], refs[-1])

    return pl.pallas_call(
        kernel,
        in_specs=[pl.BlockSpec(memory_space=pltpu.SMEM)] + [ANYWHERE] * count,
        out_specs=[pl.BlockSpec(memory_space=pltpu.VMEM)] * len(outs),
        out_shape=[jax.ShapeDtypeStruct(dims, dtype) for dims in outs],
        scratch_shapes=[pltpu.SemaphoreType.DMA((len(plan),))],
        compiler_params=pltpu.CompilerParams(vmem_limit_bytes=16 * 1024 * 1024),
        cost_estimate=NO_COST,
    )(table, *values)


ORDERS = (("y", "x"), ("x", "y"))


def join_line(everybody):
    _, rows, columns = everybody[0][1].shape
    items = [(piece, (half,), half, (index,)) for index, piece in everybody for half in range(2)]
    return assemble([(len(everybody), rows, columns)] * 2, items, everybody[0][1].dtype)


def plane_first(line):
    return [everyone(line[half], ORDERS[half][0]) for half in range(2)]


def plane_stack(held):
    items, outs = [], []
    for half, pieces in enumerate(held):
        outs.append((len(pieces),) + pieces[0][1].shape)
        items += [(piece, (), half, (index,)) for index, piece in pieces]
    return assemble(outs, items, held[0][0][1].dtype)


def plane_second(both):
    return [everyone(both[half], ORDERS[half][1]) for half in range(2)]


def plane_items(held, inner):
    nx, ny = lax.axis_size("x"), lax.axis_size("y")
    _, nz, rows, columns = held[0][0][1].shape
    dims = (nx, nz, ny, 2, rows, columns) if inner else (nx, 2, nz, ny, rows, columns)
    items = []
    for half, pieces in enumerate(held):
        for index, piece in pieces:
            for k in range(piece.shape[0]):
                at_x, at_y = (index, k) if half == 0 else (k, index)
                items.append((piece, (k,), 0, (at_x, None, at_y, half) if inner else (at_x, half, None, at_y)))
    return dims, items


def cut(value, axis, dim):
    size = lax.axis_size(axis)
    here = lax.axis_index(axis)
    return take(value, here, dim), [take(value, lax.rem(here + step, size), dim) for step in range(1, size)]


def move(held, axis):
    mine, going = held
    size = lax.axis_size(axis)
    came = []
    for step, piece in enumerate(going, 1):
        came.append(lax.ppermute(piece, axis, [(i, (i + step) % size) for i in range(size)]))
    return mine, came


def add_up(held):
    mine, came = held
    total = mine.astype(F32)
    for piece in came:
        total = total + piece.astype(F32)
    return total


def cut_first(whole, inner):
    return [
        cut(whole[:, :, :, half] if inner else whole[:, half], axis, 0 if axis == "x" else 2)
        for half, (_, axis) in enumerate(ORDERS)
    ]


def move_first(held):
    return [move(one, axis) for one, (_, axis) in zip(held, ORDERS)]


def cut_second(held):
    return [cut(add_up(one).astype(BF16), axis, 0 if axis == "x" else 1) for one, (axis, _) in zip(held, ORDERS)]


def move_second(held):
    return [move(one, axis) for one, (axis, _) in zip(held, ORDERS)]


def cut_line(held):
    return cut(jnp.stack([add_up(one).astype(BF16) for one in held]), "z", 1)


def sum_everywhere(value):
    for axis in ("core", "x", "z", "y"):
        size = lax.axis_size(axis)
        step = 1
        while step < size:
            route = [(i, i ^ step) for i in range(size)]
            value = value + lax.ppermute(value, axis, route)
            step *= 2
    return value


def nn(a, b):
    return lax.dot_general(a, b, (((1,), (0,)), ((), ())), preferred_element_type=F32)


def nt(a, b):
    return lax.dot_general(a, b, (((1,), (1,)), ((), ())), preferred_element_type=F32)


def tn(a, b):
    return lax.dot_general(a, b, (((0,), (0,)), ((), ())), preferred_element_type=F32)


def pieces_of(value, count):
    parts = []
    rest = value
    for index in range(count):
        part = rest.astype(BF16)
        parts.append(part)
        if index < count - 1:
            rest = rest - part.astype(F32)
    return parts


PIECE = 32


def nt_fine(a, b):
    a_high, a_low = pieces_of(a, 2)
    b_high, b_low = pieces_of(b, 2)
    return nt(jnp.concatenate([a_high, a_low, a_high], axis=1), jnp.concatenate([b_high, b_high, b_low], axis=1))


def head_map():
    row = lax.rem(lax.broadcasted_iota(jnp.int32, (NS, EC), 0), PIECE)
    lane = lax.broadcasted_iota(jnp.int32, (NS, EC), 1)
    inside = (lane >= row * P_SIZE) & (lane < row * P_SIZE + P_SIZE)
    return jnp.where(inside, 1.0, 0.0).astype(BF16)


def head_sums():
    row = lax.broadcasted_iota(jnp.int32, (EC, NS), 0)
    lane = lax.broadcasted_iota(jnp.int32, (EC, NS), 1)
    inside = (row >= lane * P_SIZE) & (row < lane * P_SIZE + P_SIZE)
    return jnp.where(inside, 1.0, 0.0).astype(BF16)


def packed(value):
    lane = lax.broadcasted_iota(jnp.int32, value.shape, 1)
    high, mid, low = (p.astype(F32) for p in pieces_of(jnp.where(lane < HC, value, 0.0), 3))
    return (high + pltpu.roll(mid, PIECE, 1) + pltpu.roll(low, 2 * PIECE, 1)).astype(BF16)


def spread(value, heads):
    return nn(packed(value), heads)


def gathered_heads(value, sums, count=1):
    return sum(nn(part, sums) for part in pieces_of(value, count))


def triangle(kind):
    row = lax.broadcasted_iota(jnp.int32, (SPAN, SPAN), 0)
    col = lax.broadcasted_iota(jnp.int32, (SPAN, SPAN), 1)
    keep = {"ge": row >= col, "gt": row > col, "le": row <= col}[kind]
    return jnp.where(keep, 1.0, 0.0)


def exact_sum(matrix, value):
    low = matrix.astype(BF16)
    return sum(nn(low, part) for part in pieces_of(value, 3))


def sigmoid(v):
    return 0.5 * jnp.tanh(0.5 * v) + 0.5


def softplus(v):
    return jnp.maximum(v, 0.0) + jnp.log1p(jnp.exp(-jnp.abs(v)))


def call(kernel, grid, in_specs, out_specs, out_shape, scratch=(), vmem=VM, **more):
    return pl.pallas_call(
        kernel,
        grid=grid,
        in_specs=in_specs,
        out_specs=out_specs,
        out_shape=out_shape,
        scratch_shapes=list(scratch),
        compiler_params=pltpu.CompilerParams(vmem_limit_bytes=vmem * 1024 * 1024),
        cost_estimate=NO_COST,
        **more,
    )


def shape(*dims, dtype=F32):
    return jax.ShapeDtypeStruct(dims, dtype)


def fixed(*dims):
    return pl.BlockSpec(dims, lambda *_: (0,) * len(dims))


def conv_kernel(rows, nz, proj, taps, heads_par, x_out, bc_out, step_out, cum_out, state_out, local_out):
    heads = head_map()
    spans = rows // SPAN
    lower = triangle("ge")
    state = jnp.zeros((NS, EC), F32)
    total = jnp.zeros((1, NS), F32)
    core_one = heads_par[3:4, :] > 0.5
    for span in range(spans):
        start = HALO + span * SPAN

        def activated(first, width):
            running = taps[4:5, first : first + width]
            for k in range(CONV):
                at = start - (CONV - 1) + k
                running = running + taps[k : k + 1, first : first + width] * proj[0, at : at + SPAN, first : first + width]
            return running * sigmoid(running)

        own = activated(OWN, NS)
        other = activated(OTHER, NS)
        write_full = jnp.where(core_one, other, own)
        write = write_full.astype(BF16)
        here = slice(span * SPAN, span * SPAN + SPAN)
        bc_out[0, here, :NS] = write_full
        bc_out[0, here, NS:] = jnp.where(core_one, own, other)
        raw = proj[0, start : start + SPAN, STEP : STEP + NS] + heads_par[0:1, :]
        step = softplus(raw)
        cum = exact_sum(lower, -step * heads_par[1:2, :])
        step_out[0, here] = step
        cum_out[0, here] = cum
        last = cum[SPAN - 1 : SPAN]
        tail_low = packed(jnp.exp(last - cum) * step)
        local_out[0, span] = state.astype(BF16)
        decay = spread(jnp.broadcast_to(jnp.exp(last), (8, NS)), heads)[0:1]
        wide = EC // 2
        fresh = []
        for half in range(2):
            cols = slice(half * wide, half * wide + wide)
            x = activated(half * wide, wide)
            x_out[0, here, cols] = x
            fresh.append(tn(write, (x * nn(tail_low, heads[:, cols])).astype(BF16)))
        state = state * decay + jnp.concatenate(fresh, axis=1)
        total = total + last
    depth = NS // nz
    for group in range(nz):
        state_out[group, 0, :, :EC] = state[group * depth : (group + 1) * depth].astype(BF16)
    row = lax.broadcasted_iota(jnp.int32, (depth, NS), 0)
    high, mid, low = (part.astype(F32) for part in pieces_of(total, 3))
    total_rows = jnp.where(row == 0, high, jnp.where(row == 1, mid, jnp.where(row == 2, low, 0.0))).astype(BF16)
    for group in range(nz):
        state_out[group, 0, :, EC:] = total_rows


def intra_kernel(x_ref, bc_ref, step_ref, cum_ref, heads_par, out_ref, xs_ref, cross_ref, cumt_ref):
    heads = head_map()
    step_wide = spread(step_ref[0], heads)
    xs_ref[...] = (x_ref[0] * step_wide).astype(BF16)
    cum = cum_ref[0]
    cumt_ref[...] = cum.T
    cross_ref[...] = nt_fine(bc_ref[0, :, NS:], bc_ref[0, :, :NS]) * triangle("ge")
    skip = spread(jnp.broadcast_to(heads_par[2:3, :], (8, NS)), heads)[0:1]
    out_ref[0] = x_ref[0] * skip
    low = lax.broadcasted_iota(jnp.int32, (SPAN, NS), 1) < P_SIZE

    def pair(p, carry):
        lanes = pl.ds(pl.multiple_of(p * NS, NS), NS)
        xs = xs_ref[:, lanes]
        made = []
        for j in range(2):
            h = 2 * p + j
            col = pltpu.roll(cum, lax.rem(NS - h, NS), 1)[:, 0:1]
            row = cumt_ref[pl.ds(h, 1), :]
            mix = jnp.exp(jnp.minimum(col - row, 0.0)) * cross_ref[...]
            made.append(nn(mix.astype(BF16), xs))
        out_ref[0, :, lanes] += jnp.where(low, made[0], made[1])
        return carry

    lax.fori_loop(0, HC // 2, pair, 0)


def span_state(state_ref, local_ref, before, heads):
    whole = jnp.concatenate([state_ref[g, 0] for g in range(state_ref.shape[0])], axis=0)
    decay = spread(jnp.broadcast_to(jnp.exp(before), (8, NS)), heads)[0:1]
    return whole.astype(F32) * decay + local_ref[0, 0].astype(F32)


def finish_kernel(part_ref, bc_ref, cum_ref, before_ref, state_ref, local_ref, gate_ref, dmix_ref, gain_ref, out_ref, sums_ref):
    heads = head_map()
    state = span_state(state_ref, local_ref, before_ref[0, 0, 0:1], heads).astype(BF16)
    grown = spread(jnp.exp(cum_ref[0]), heads)
    y = part_ref[0] + grown * nn(bc_ref[0, :, NS:].astype(BF16), state)
    out_ref[0] = y
    gate = gate_ref[0]
    gated = y * gate * sigmoid(gate)
    squares = jnp.sum(gated * gated, axis=1, keepdims=True)
    slopes = jnp.sum(gated * gain_ref[0:1, :] * dmix_ref[0], axis=1, keepdims=True)
    lane = lax.broadcasted_iota(jnp.int32, (SPAN, NS), 1)
    sums_ref[0] = jnp.where(lane == 0, squares, jnp.where(lane == 1, slopes, 0.0))


def gate_kernel(
    spans, nz, y_ref, gate_ref, dmix_ref, sums_ref, gain_ref, bc_ref, cum_ref,
    mix_out, dy_out, dgate_out, ggain_out, state_out, local_out, run_ref,
):
    step = pl.program_id(1)
    heads = head_map()
    squares = sums_ref[0, :, 0:1]
    slopes = sums_ref[0, :, 1:2]
    scale = lax.rsqrt(squares / E + EPSILON)
    y = y_ref[0]
    gate = gate_ref[0]
    soft = sigmoid(gate)
    silu = gate * soft
    gated = y * silu
    gain = gain_ref[0:1, :]
    dmix = dmix_ref[0]
    mix_out[0] = (gated * scale * gain).astype(BF16)
    dgated = scale * (gain * dmix - gated * (scale * scale * slopes / E))
    dy = dgated * silu
    dy_out[0] = dy
    dgate_out[0] = (dgated * y * (soft * (1.0 + gate * (1.0 - soft)))).astype(BF16)

    @pl.when((step == 0) & (pl.program_id(0) == 0))
    def _():
        ggain_out[...] = jnp.zeros_like(ggain_out)

    ggain_out[...] += jnp.broadcast_to(jnp.sum(gated * scale * dmix, axis=0, keepdims=True), (8, EC))

    @pl.when(step == 0)
    def _():
        run_ref[...] = jnp.zeros_like(run_ref)

    cum = cum_ref[0]
    grown = spread(jnp.exp(cum), heads)
    fresh = tn(bc_ref[0, :, NS:].astype(BF16), (dy * grown).astype(BF16))
    local_out[0, 0] = run_ref[...].astype(BF16)
    run_ref[...] = fresh + run_ref[...] * grown[SPAN - 1 : SPAN]

    @pl.when(step == spans - 1)
    def _():
        depth = NS // nz
        for group in range(nz):
            state_out[group, 0] = run_ref[group * depth : (group + 1) * depth].astype(BF16)


def back_kernel(kept, x_ref, bc_ref, step_ref, cum_ref, before_ref, dy_ref, state_ref, local_ref, *refs):
    dxs_out, dbc_out, dcum_out, dstep_out, cross_ref, dcross_ref, cumt_ref, rows_ref = refs[kept:]
    heads = head_map()
    sums = head_sums()
    cum = cum_ref[0]
    step = step_ref[0]
    cumt_ref[...] = cum.T
    write = bc_ref[0, :, :NS].astype(BF16)
    read = bc_ref[0, :, NS:].astype(BF16)
    mask = triangle("le")
    cross_ref[...] = nt_fine(bc_ref[0, :, :NS], bc_ref[0, :, NS:]) * mask
    dcross_ref[...] = jnp.zeros_like(dcross_ref)
    rows_ref[...] = jnp.zeros_like(rows_ref)
    lane = lax.broadcasted_iota(jnp.int32, (SPAN, NS), 1)
    low = lane < P_SIZE

    def pair(p, cols):
        lanes = pl.ds(pl.multiple_of(p * NS, NS), NS)
        x_high, x_low = (part.astype(F32) for part in pieces_of(x_ref[0, :, lanes], 2))
        dy, dy_low = pieces_of(dy_ref[0, :, lanes], 2)
        right = jnp.concatenate([dy, dy, dy_low], axis=1)
        made = []
        for j in range(2):
            h = 2 * p + j
            col = pltpu.roll(cum, lax.rem(NS - h, NS), 1)[:, 0:1]
            step_col = pltpu.roll(step, lax.rem(NS - h, NS), 1)[:, 0:1]
            row = cumt_ref[pl.ds(h, 1), :]
            decay = jnp.exp(jnp.minimum(row - col, 0.0))
            mine = low if j == 0 else ~low
            high = jnp.where(mine, x_high, 0.0).astype(BF16)
            rest = jnp.where(mine, x_low, 0.0).astype(BF16)
            slope = nt(jnp.concatenate([high, rest, high], axis=1), right) * decay
            cross = cross_ref[...]
            cols = jnp.where(lane == h, jnp.sum(slope * cross, axis=1, keepdims=True), cols)
            slope = slope * step_col
            dcross_ref[...] += slope
            rows_ref[pl.ds(h, 1), :] = jnp.sum(slope * cross, axis=0, keepdims=True)
            made.append(nn((decay * cross).astype(BF16), dy))
        dxs_out[0, :, lanes] = jnp.where(low, made[0], made[1])
        return cols

    cols = lax.fori_loop(0, HC // 2, pair, jnp.zeros((SPAN, NS), F32))
    dcross = (dcross_ref[...] * mask).astype(BF16)
    state = span_state(state_ref, local_ref, before_ref[0, 0, 0:1], heads).astype(BF16)
    grown = spread(jnp.exp(cum), heads)
    dye = dy_ref[0] * grown
    inter = gathered_heads(dye * nn(read, state), sums)
    dstep_out[0] = cols
    dbc_out[0, :, :NS] = nn(dcross, read)
    dbc_out[0, :, NS:] = tn(dcross, write) + nt(dye.astype(BF16), state)
    dcum_out[0] = rows_ref[...].T - step * cols + inter


def close_kernel(
    rows, nz, x_ref, bc_ref, step_ref, cum_ref, dy_ref, proj_ref, taps, heads_par, dxs_ref, dbc_ref, dcum_ref, dstep_ref,
    state_ref, local_ref, back_ref, blocal_ref, dproj_out, mine_out, theirs_out, gtaps_out, ghead_out, dpre_ref,
):
    core_one = heads_par[3:4, :] > 0.5
    heads = head_map()
    sums = head_sums()
    spans = rows // SPAN
    upper = triangle("le")
    below = triangle("gt")
    whole_in = jnp.concatenate([state_ref[g, 0] for g in range(nz)], axis=0).astype(F32)
    whole_back = jnp.concatenate([back_ref[g, 0] for g in range(nz)], axis=0).astype(F32)
    lasts = [cum_ref[0, (c + 1) * SPAN - 1 : (c + 1) * SPAN] for c in range(spans)]
    skip = spread(jnp.broadcast_to(heads_par[2:3, :], (8, NS)), heads)[0:1]
    real = lax.broadcasted_iota(jnp.int32, (SPAN, NS), 1) < HC
    dpre_ref[:HALO] = jnp.zeros((HALO, EC), F32)
    dpre_ref[HALO + rows :] = jnp.zeros((HALO, EC), F32)
    zero_row = jnp.zeros((1, NS), F32)
    gbias, gdecay, gskip = zero_row, zero_row, zero_row
    for span in range(spans):
        here = slice(span * SPAN, span * SPAN + SPAN)
        before = sum(lasts[:span], zero_row)
        after = sum(lasts[span + 1 :], zero_row)
        both = spread(jnp.exp(jnp.concatenate([before, after, lasts[span], jnp.zeros((5, NS), F32)], axis=0)), heads)
        state = whole_in * both[0:1] + local_ref[0, span].astype(F32)
        back = whole_back * both[1:2] + blocal_ref[0, span].astype(F32)
        back_low = back.astype(BF16)
        at_last = gathered_heads(
            jnp.broadcast_to(jnp.sum(state * back, axis=0, keepdims=True) * both[2:3], (8, EC)), sums, 2
        )[0:1]
        write = bc_ref[0, here, :NS].astype(BF16)
        cum = cum_ref[0, here]
        step = step_ref[0, here]
        x = x_ref[0, here]
        dy = dy_ref[0, here]
        tail = spread(jnp.exp(lasts[span] - cum), heads)
        step_wide = spread(step, heads)
        from_back = tail * nn(write, back_low)
        dxs = dxs_ref[0, here] + from_back
        later = gathered_heads(x * from_back, sums)
        dstep = dstep_ref[0, here] + later
        moved = step * later
        dwrite = dbc_ref[0, here, :NS] + nt((x * tail * step_wide).astype(BF16), back_low)
        dread = dbc_ref[0, here, NS:]
        mine_out[0, here] = jnp.where(core_one, dread, dwrite)
        theirs_out[0, here] = jnp.where(core_one, dwrite, dread)
        dlog = exact_sum(upper, dcum_ref[0, here]) + exact_sum(below, moved) + at_last
        raw = proj_ref[0, HALO + span * SPAN : HALO + span * SPAN + SPAN, STEP : STEP + NS] + heads_par[0:1, :]
        draw = jnp.where(real, (dstep - heads_par[1:2, :] * dlog) * sigmoid(raw), 0.0)
        dproj_out[0, HALO + span * SPAN : HALO + span * SPAN + SPAN, STEP : STEP + NS] = draw.astype(BF16)
        gbias = gbias + jnp.sum(draw, axis=0, keepdims=True)
        gdecay = gdecay + jnp.sum(jnp.where(real, dlog * (-step * heads_par[1:2, :]), 0.0), axis=0, keepdims=True)
        gskip = gskip + gathered_heads(jnp.broadcast_to(jnp.sum(dy * x, axis=0, keepdims=True), (8, EC)), sums, 3)[0:1]
        dx = dxs * step_wide + skip * dy
        start = HALO + span * SPAN
        pre = taps[4:5, :EC]
        for k in range(CONV):
            at = start - (CONV - 1) + k
            pre = pre + taps[k : k + 1, :EC] * proj_ref[0, at : at + SPAN, :EC]
        soft = sigmoid(pre)
        dpre_ref[start : start + SPAN] = dx * (soft * (1.0 + pre * (1.0 - soft)))
    conv_back(rows, dpre_ref, proj_ref, taps, 0, EC, dproj_out, 0, gtaps_out)
    dproj_out[0, :HALO, STEP : STEP + NS] = jnp.zeros((HALO, NS), BF16)
    ghead_out[0] = jnp.concatenate([gbias, gdecay, gskip, jnp.zeros((5, NS), F32)], axis=0)


def conv_back(rows, dpre_ref, proj_ref, taps, first, width, dproj_out, out_first, gtaps_out):
    sums = [jnp.zeros((1, width), F32)] * (CONV + 1)
    blocks = [(0, HALO)] + [(HALO + s * SPAN, SPAN) for s in range(rows // SPAN)]
    for start, count in blocks:
        running = jnp.zeros((count, width), F32)
        for k in range(CONV):
            at = start + (CONV - 1) - k
            running = running + taps[k : k + 1, first : first + width] * dpre_ref[at : at + count]
        dproj_out[0, start : start + count, out_first : out_first + width] = running.astype(BF16)
        if count == SPAN:
            dpre = dpre_ref[start : start + count]
            for k in range(CONV):
                at = start - (CONV - 1) + k
                sums[k] = sums[k] + jnp.sum(dpre * proj_ref[0, at : at + count, first : first + width], axis=0, keepdims=True)
            sums[CONV] = sums[CONV] + jnp.sum(dpre, axis=0, keepdims=True)
    gtaps_out[0, :, :width] = jnp.concatenate(sums + [jnp.zeros((3, width), F32)], axis=0)


def own_kernel(rows, dproj_in, mine_ref, came_ref, proj_ref, taps, dproj_out, gtaps_out, dpre_ref):
    dpre_ref[:HALO] = jnp.zeros((HALO, NS), F32)
    dpre_ref[HALO + rows :] = jnp.zeros((HALO, NS), F32)
    for span in range(rows // SPAN):
        start = HALO + span * SPAN
        pre = taps[4:5, :]
        for k in range(CONV):
            at = start - (CONV - 1) + k
            pre = pre + taps[k : k + 1, :] * proj_ref[0, at : at + SPAN]
        soft = sigmoid(pre)
        here = slice(span * SPAN, span * SPAN + SPAN)
        dconv = mine_ref[0, here] + came_ref[0, here]
        dpre_ref[start : start + SPAN] = dconv * (soft * (1.0 + pre * (1.0 - soft)))
    conv_back(rows, dpre_ref, proj_ref, taps, 0, NS, dproj_out, 0, gtaps_out)


def outer_kernel(halo, a_ref, b_ref, out_ref):
    slots, _, width = a_ref.shape
    left = a_ref[...][:, halo:].reshape(-1, width)
    right = b_ref[...].reshape(left.shape[0], -1)
    out_ref[...] = tn(left, right).astype(BF16)


def outer(a, b, halo=0):
    slots, tall, left = a.shape
    rows, right = b.shape[1:]
    tile = 256
    return call(
        functools.partial(outer_kernel, halo),
        (left // tile,),
        [pl.BlockSpec((slots, tall, tile), lambda i: (0, 0, i)), fixed(slots, rows, right)],
        pl.BlockSpec((tile, right), lambda i: (i, 0)),
        shape(left, right, dtype=BF16),
    )(a, b)


def rows_kernel(turned, halo, a_ref, b_ref, out_ref):
    value = a_ref[0, halo:]
    out_ref[0] = (nt if turned else nn)(value, b_ref[...])


def by_rows(a, b, turned=False, halo=0):
    slots, tall, depth = a.shape
    right = b.shape[0 if turned else 1]
    return call(
        functools.partial(rows_kernel, turned, halo),
        (slots,),
        [pl.BlockSpec((1, tall, depth), lambda s: (s, 0, 0)), fixed(*b.shape)],
        pl.BlockSpec((1, tall - halo, right), lambda s: (s, 0, 0)),
        shape(slots, tall - halo, right),
    )(a, b)


def by_rows_of(a, held, inner, turned=False, halo=0):
    dims, items = plane_items(held, inner)
    wide = dims[-1]
    deep = EC if inner else dims[0] * dims[1] * dims[2] * dims[3] * dims[4]
    if dims[4] % 16:
        whole = assemble([dims], items, BF16)[0].reshape(deep, wide)
        return by_rows(a, whole, turned, halo), whole
    values, table, plan = copy_plan(items)
    count = len(values)
    slots, tall, depth = a.shape
    right = deep if turned else wide

    def kernel(table_ref, a_ref, *refs):
        pieces, out_ref, whole_ref, held_ref, sems, whole_sem = refs[:count], *refs[count:]
        store = pltpu.make_async_copy(held_ref, whole_ref, whole_sem)

        @pl.when(pl.program_id(0) == 0)
        def _():
            copy_all(plan, table_ref, pieces, [held_ref], sems)
            store.start()

        matrix = held_ref[...].reshape(deep, wide)
        out_ref[0] = (nt if turned else nn)(a_ref[0, halo:], matrix)

        @pl.when(pl.program_id(0) == slots - 1)
        def _():
            store.wait()

    out, whole = call(
        kernel,
        (slots,),
        [pl.BlockSpec(memory_space=pltpu.SMEM), pl.BlockSpec((1, tall, depth), lambda s: (s, 0, 0))]
        + [ANYWHERE] * count,
        [pl.BlockSpec((1, tall - halo, right), lambda s: (s, 0, 0)), ANYWHERE],
        [shape(slots, tall - halo, right), shape(*dims, dtype=BF16)],
        [pltpu.VMEM(dims, BF16), pltpu.SemaphoreType.DMA((len(plan),)), pltpu.SemaphoreType.DMA],
    )(table, a, *values)
    return out, whole.reshape(deep, wide)


def normed_kernel(core_ref, dproj_ref, dgate_ref, scan_ref, gate_ref, own_ref, other_ref):
    scan, gate = scan_ref[...], gate_ref[...]
    core = core_ref[0]
    for slot, out_ref in ((core, own_ref), (1 - core, other_ref)):
        out_ref[:HALO] = nt(dproj_ref[slot, :HALO], scan)
        out_ref[HALO:] = nt(dproj_ref[slot, HALO:], scan) + nt(dgate_ref[slot], gate)


SMALL = pl.BlockSpec(memory_space=pltpu.SMEM)


def to_normed(core, d_proj, d_gate, scan_weight, gate_weight):
    slots, tall, _ = d_proj.shape
    features = gate_weight.shape[0]
    tile = 256
    return call(
        normed_kernel,
        (features // tile,),
        [
            SMALL, fixed(slots, tall, BACK), fixed(slots, tall - HALO, EC),
            pl.BlockSpec((tile, BACK), lambda i: (i, 0)), pl.BlockSpec((tile, EC), lambda i: (i, 0)),
        ],
        [pl.BlockSpec((tall, tile), lambda i: (0, i))] * 2,
        [shape(tall, features)] * 2,
    )(core.reshape(1), d_proj, d_gate, scan_weight, gate_weight)


def two_kernel(core_ref, a_ref, b_ref, own_ref, other_ref):
    core = core_ref[0]
    own_ref[...] = nn(a_ref[core], b_ref[...])
    other_ref[...] = nn(a_ref[1 - core], b_ref[...])


def two_slots(core, a, b):
    slots, rows, depth = a.shape
    right = b.shape[1]
    tile = 256
    return call(
        two_kernel,
        (right // tile,),
        [SMALL, fixed(slots, rows, depth), pl.BlockSpec((depth, tile), lambda i: (0, i))],
        [pl.BlockSpec((rows, tile), lambda i: (0, i))] * 2,
        [shape(rows, right)] * 2,
    )(core.reshape(1), a, b)


def valid_rows(bounds_ref, count):
    row = lax.broadcasted_iota(jnp.int32, (count, 1), 0) + pl.program_id(0) * count + bounds_ref[0]
    return jnp.where(row < bounds_ref[1], 1.0, 0.0)


def block_kernel(bounds_ref, in_ref, own_ref, came_ref, out_ref, sums_ref):
    valid = valid_rows(bounds_ref, SPAN)
    residual = in_ref[...].astype(F32)
    mixed = own_ref[...] + came_ref[...]
    value = valid * (residual + mixed)
    out_ref[...] = value.astype(BF16)
    lane = lax.broadcasted_iota(jnp.int32, (8, NS), 1)
    total = jnp.zeros((8, NS), F32)
    for number, part in enumerate((valid * residual * residual, valid * mixed * mixed, value * value)):
        part = jnp.sum(jnp.sum(part, axis=1, keepdims=True), axis=0, keepdims=True)
        total = jnp.where(lane == number, part, total)

    @pl.when(pl.program_id(0) == 0)
    def _():
        sums_ref[...] = jnp.zeros_like(sums_ref)

    sums_ref[...] += total


def block_rows(bounds, own_in, mixer_own, mixer_came):
    rows, features = own_in.shape
    tile = pl.BlockSpec((SPAN, features), lambda i: (i, 0))
    return call(
        block_kernel,
        (rows // SPAN,),
        [SMALL, tile, tile, tile],
        [tile, fixed(8, NS)],
        [shape(rows, features, dtype=BF16), shape(8, NS)],
    )(bounds, own_in, mixer_own, mixer_came)


def input_kernel(bounds_ref, in_ref, grad_ref, own_ref, came_ref, later_ref, across_ref, gain_ref, out_ref, gain_out):
    valid = valid_rows(bounds_ref, SPAN)
    at = pl.program_id(0)
    start = pl.multiple_of(HALO + at * SPAN, HALO)
    slope = own_ref[pl.ds(start, SPAN)] + came_ref[pl.ds(start, SPAN)]
    tail = jnp.where(at == pl.num_programs(0) - 1, later_ref[...] + across_ref[...], 0.0)
    slope = jnp.concatenate([slope[: SPAN - HALO], slope[SPAN - HALO :] + tail], axis=0)
    residual = in_ref[...].astype(F32)
    features = residual.shape[1]
    scale = lax.rsqrt(jnp.sum(residual * residual, axis=1, keepdims=True) / features + EPSILON)
    unit = residual * scale
    along = slope * gain_ref[...]
    mean = jnp.sum(along * unit, axis=1, keepdims=True) / features
    out_ref[...] = (valid * grad_ref[...].astype(F32) + scale * (along - unit * mean)).astype(BF16)

    @pl.when(at == 0)
    def _():
        gain_out[...] = jnp.zeros_like(gain_out)

    gain_out[...] += jnp.broadcast_to(jnp.sum(slope * unit, axis=0, keepdims=True), gain_out.shape)


def input_rows(bounds, own_in, own_grad, d_own, d_came, back_own, back_came, gain):
    rows, features = own_in.shape
    tile = pl.BlockSpec((SPAN, features), lambda i: (i, 0))
    return call(
        input_kernel,
        (rows // SPAN,),
        [
            SMALL, tile, tile, fixed(*d_own.shape), fixed(*d_came.shape), fixed(HALO, features), fixed(HALO, features),
            fixed(1, features),
        ],
        [tile, fixed(8, features)],
        [shape(rows, features, dtype=BF16), shape(8, features)],
    )(bounds, own_in, own_grad, d_own, d_came, back_own, back_came, gain)


def shards(
    block_in,
    lengths,
    norm_gain,
    in_weight,
    conv_weight,
    conv_bias,
    step_bias,
    decay_log,
    skip_gain,
    out_gain,
    out_weight,
    grad_out,
):
    slot_count, row_count, features = block_in.shape
    nx, nz, ny = lax.axis_size("x"), lax.axis_size("z"), lax.axis_size("y")
    ix, iz, iy = lax.axis_index("x"), lax.axis_index("z"), lax.axis_index("y")
    core = lax.axis_index("core")
    rows = ny * row_count
    spans = rows // SPAN
    deep = in_weight.shape[0]
    thin = out_weight.shape[0]

    def half_of(value, width, which):
        parts = value.reshape(value.shape[:-1] + (nx, 2, width // (2 * nx)))
        chosen = take(parts, which, value.ndim)
        return chosen.reshape(value.shape[:-1] + (width // 2,))

    def one_slot(block):
        return by_index("y", take(block, iy, 0), swapped(take(block, 1 - iy, 0), "y")).reshape(rows, features)

    def by_slots(value):
        parts = value.reshape(ny, row_count, features)
        return take(parts, iy, 0), take(parts, 1 - iy, 0)

    def exchange(value):
        return lax.all_to_all(value, "z", 0, 0, tiled=True)

    def scaled(value):
        wide = value.astype(F32)
        return wide * lax.rsqrt(jnp.mean(wide * wide, axis=-1, keepdims=True) + EPSILON)

    tall = HALO + rows
    own_length = take(lengths, (ix * 2 + core) * slot_count + iy, 0)
    bounds = jnp.stack([iz * rows, own_length]).astype(jnp.int32)
    live = types.SimpleNamespace()

    def columns_of(which):
        heads_in = half_of(in_weight[:, E : 2 * E], E, which)
        write = in_weight[:, 2 * E : 2 * E + NS]
        read = in_weight[:, 2 * E + NS : E + CH]
        first = which == 0
        steps = jnp.pad(half_of(in_weight[:, E + CH :], H, which), ((0, 0), (0, NS - HC)))
        gate = half_of(in_weight[:, :E], E, which)
        return jnp.concatenate(
            [heads_in, jnp.where(first, write, read), steps, jnp.where(first, read, write), gate], axis=1
        )

    live.mine = columns_of(core)
    live.came = swapped(columns_of(1 - core), "core")
    live.block_in, live.grad_out = block_in, grad_out
    live.small = jnp.concatenate([norm_gain, conv_weight.reshape(-1), conv_bias, out_gain])
    settle(live)

    pieces = by_index("core", live.mine, live.came)
    live.scan = everyone(pieces[:, :, :WIDE], "z")
    live.gate = pieces[:, :, WIDE:]
    live.own_in = one_slot(live.block_in)
    live.own_grad = one_slot(live.grad_out)
    live.small = shared(jnp.pad(live.small, (0, -live.small.shape[0] % 1024)).reshape(-1, NS), ("x", "core", "z", "y"))
    del live.mine, live.came, live.block_in, live.grad_out
    settle(live)

    live.scan = join_line(live.scan)
    settle(live)
    live.scan = plane_first(live.scan)
    last_rows = live.own_in[rows - HALO :]
    live.other_in = swapped(live.own_in, "core")
    live.before_own = lax.ppermute(last_rows, "z", [(i, i + 1) for i in range(nz - 1)])
    across = [(c * nz + i, (1 - c) * nz + i + 1) for c in range(2) for i in range(nz - 1)]
    live.before_other = lax.ppermute(last_rows, ("core", "z"), across)
    small = live.small.reshape(2 * nx * nz * ny, -1)
    chan = CH // (2 * nx * nz * ny)
    gain_in = small[:, :deep].reshape(1, features).astype(F32)
    taps_all = small[:, deep : deep + CONV * chan].reshape(-1, CONV, chan).transpose(1, 0, 2).reshape(CONV, CH)
    at = deep + CONV * chan
    bias_all = small[:, at : at + chan].reshape(1, CH)
    gain_out_all = small[:, at + chan : at + chan + thin].reshape(E)
    taps_all = jnp.concatenate([taps_all, bias_all, jnp.zeros((3, CH), BF16)], axis=0).astype(F32)
    own_taps = jnp.where(core == 0, taps_all[:, E : E + NS], taps_all[:, E + NS :])
    other_taps = jnp.where(core == 0, taps_all[:, E + NS :], taps_all[:, E : E + NS])
    taps = jnp.concatenate(
        [half_of(taps_all[:, :E], E, core), own_taps, jnp.zeros((8, NS), F32), other_taps], axis=1
    )
    gain_out = jnp.broadcast_to(half_of(gain_out_all, E, core).astype(F32), (8, EC))

    def head_row(value):
        return jnp.pad(half_of(value, H, core), (0, NS - HC))

    heads_par = jnp.stack(
        [
            head_row(step_bias),
            head_row(jnp.exp(decay_log)),
            head_row(skip_gain),
            jnp.full((NS,), core, F32),
        ]
        + [jnp.zeros((NS,), F32)] * 4
    )

    live.gain_in, live.taps, live.own_taps, live.gain_out, live.heads_par = gain_in, taps, own_taps, gain_out, heads_par
    del live.small
    settle(live)

    live.scan = plane_stack(live.scan)
    settle(live)
    live.scan = plane_second(live.scan)
    live.gate = everyone(live.gate, "z")
    joined = jnp.concatenate(
        [by_index("core", live.before_own, live.before_other), by_index("core", live.own_in, live.other_in)], axis=1
    )
    live.normed = (scaled(joined) * live.gain_in).astype(BF16)
    del live.before_own, live.before_other, live.other_in
    settle(live)

    live.gate = join_line(live.gate)
    settle(live)
    live.gate = plane_first(live.gate)
    live.other_grad = swapped(live.own_grad, "core")
    live.proj, live.scan_weight = by_rows_of(live.normed, live.scan, False)
    del live.scan
    settle(live)

    live.gate = plane_stack(live.gate)
    live.out_rows = out_weight.reshape(2, thin // 2, features)
    settle(live)
    live.gate = plane_second(live.gate)
    live.out_rows = everyone(live.out_rows, "z")
    proj, taps, heads_par = live.proj, live.taps, live.heads_par
    whole_row = lambda *dims: pl.BlockSpec((1,) + dims, lambda s: (s,) + (0,) * len(dims))
    x, bc, step, cum, state_part, local = call(
        functools.partial(conv_kernel, rows, nz),
        (2,),
        [whole_row(tall, WIDE), fixed(8, WIDE), fixed(8, NS)],
        [
            whole_row(rows, EC), whole_row(rows, 2 * NS), whole_row(rows, NS), whole_row(rows, NS),
            pl.BlockSpec((nz, 1, NS // nz, EC + NS), lambda s: (0, s, 0, 0)), whole_row(spans, NS, EC),
        ],
        [
            shape(2, rows, EC), shape(2, rows, 2 * NS), shape(2, rows, NS), shape(2, rows, NS),
            shape(nz, 2, NS // nz, EC + NS, dtype=BF16), shape(2, spans, NS, EC, dtype=BF16),
        ],
    )(proj, taps, heads_par)

    live.state_part, live.x, live.bc, live.step, live.cum, live.local = state_part, x, bc, step, cum, local
    settle(live)

    live.out_rows = join_line(live.out_rows)
    settle(live)
    live.ends = exchange(live.state_part)
    live.out_rows = plane_first(live.out_rows)
    x, bc, step, cum, heads_par = live.x, live.bc, live.step, live.cum, live.heads_par
    in_span = lambda *dims: pl.BlockSpec((1, SPAN) + dims, lambda s, c: (s, c) + (0,) * len(dims))
    local_span = pl.BlockSpec((1, 1, NS, EC), lambda s, c: (s, c, 0, 0))
    state_spec = pl.BlockSpec((nz, 1, NS // nz, EC), lambda s, c: (0, s, 0, 0))
    before_spec = pl.BlockSpec((1, 1, 8, NS), lambda s, c: (s, c, 0, 0))
    part = call(
        intra_kernel,
        (2, spans),
        [in_span(EC), in_span(2 * NS), in_span(NS), in_span(NS), fixed(8, NS)],
        in_span(EC),
        shape(2, rows, EC),
        [
            pltpu.VMEM((SPAN, EC), BF16), pltpu.VMEM((SPAN, SPAN), F32), pltpu.VMEM((NS, SPAN), F32),
        ],
    )(x, bc, step, cum, heads_par)

    live.part = part
    del live.state_part
    settle(live)

    decays = jnp.exp(jnp.sum(live.ends[:, :, :3, EC : EC + HC].astype(F32), axis=2))
    live.decays = jnp.broadcast_to(decays[..., None], decays.shape + (P_SIZE,)).reshape(nz, 2, 1, EC)
    ends = live.ends[..., :EC].astype(F32)
    running = jnp.zeros_like(ends[0])
    starts = []
    for k in range(nz):
        starts.append(running.astype(BF16))
        running = running * live.decays[k] + ends[k]
    live.starts = jnp.stack(starts)
    live.out_rows = plane_stack(live.out_rows)
    del live.ends
    settle(live)
    live.state_in = exchange(live.starts)
    live.out_rows = plane_second(live.out_rows)
    live.gate, live.gate_weight = by_rows_of(live.normed, live.gate, False, halo=HALO)

    positions = iz * rows + jnp.arange(rows, dtype=jnp.int32)
    slot_lengths = jnp.stack(
        [take(lengths, (ix * 2 + s) * slot_count + iy, 0) for s in range(2)]
    )
    all_valid = positions[None, :] < slot_lengths[:, None]

    all_grad = by_index("core", live.own_grad, live.other_grad)
    live.d_mix = jnp.where(all_valid[:, :, None], all_grad, jnp.zeros_like(all_grad))
    del live.starts, live.other_grad
    settle(live)

    d_mixer_in, live.back_weight = by_rows_of(live.d_mix, live.out_rows, True, turned=True)
    span_ends = live.cum.reshape(2, spans, SPAN, NS)[:, :, SPAN - 1]
    before = jnp.cumsum(span_ends, axis=1) - span_ends
    live.before = jnp.broadcast_to(before[:, :, None], (2, spans, 8, NS))
    part, bc, cum, before, state_in, local, gate, gain_out = (
        live.part, live.bc, live.cum, live.before, live.state_in, live.local, live.gate, live.gain_out
    )
    ssm_out, sums = call(
        finish_kernel,
        (2, spans),
        [
            in_span(EC), in_span(2 * NS), in_span(NS), before_spec, state_spec, local_span, in_span(EC), in_span(EC),
            fixed(8, EC),
        ],
        [in_span(EC), in_span(NS)],
        [shape(2, rows, EC), shape(2, rows, NS)],
    )(part, bc, cum, before, state_in, local, gate, d_mixer_in, gain_out)
    sums = sums + swapped(sums, "core")
    rev = lambda *dims: pl.BlockSpec((1, SPAN) + dims, lambda s, c: (s, spans - 1 - c) + (0,) * len(dims))
    rev_local = pl.BlockSpec((1, 1, NS, EC), lambda s, c: (s, spans - 1 - c, 0, 0))
    mixer_in, d_ssm, d_gate, g_gain_out, back_part, back_local = call(
        functools.partial(gate_kernel, spans, nz),
        (2, spans),
        [rev(EC), rev(EC), rev(EC), rev(NS), fixed(8, EC), rev(2 * NS), rev(NS)],
        [rev(EC), rev(EC), rev(EC), fixed(8, EC), state_spec, rev_local],
        [
            shape(2, rows, EC, dtype=BF16), shape(2, rows, EC), shape(2, rows, EC, dtype=BF16), shape(8, EC),
            shape(nz, 2, NS // nz, EC, dtype=BF16), shape(2, spans, NS, EC, dtype=BF16),
        ],
        [pltpu.VMEM((NS, EC), F32)],
    )(ssm_out, gate, d_mixer_in, sums, gain_out, bc, cum)
    live.mixer_in, live.d_ssm, live.d_gate, live.back_part, live.back_local = mixer_in, d_ssm, d_gate, back_part, back_local
    live.g_gain_out = g_gain_out
    del live.part, live.gate, live.out_rows, live.gain_out
    settle(live)

    live.tails = exchange(live.back_part)
    live.out_sums = outer(live.mixer_in, live.d_mix)
    live.gate_sums = outer(live.normed, live.d_gate, HALO)
    live.mixer_own, live.mixer_part = two_slots(core, live.mixer_in, live.back_weight)
    del live.back_part, live.d_mix, live.mixer_in, live.back_weight
    settle(live)

    tails = live.tails.astype(F32)
    running = jnp.zeros_like(tails[0])
    backs = [None] * nz
    for k in reversed(range(nz)):
        backs[k] = running.astype(BF16)
        running = running * live.decays[k] + tails[k]
    live.backs = jnp.stack(backs)
    live.out_sums = cut_first(live.out_sums.reshape(nx, nz, ny, 2, thin // 2, features), True)
    live.gate_sums = cut_first(live.gate_sums.reshape(nx, 2, nz, ny, deep, EC), False)
    del live.tails, live.decays
    settle(live)
    live.back_in = exchange(live.backs)
    live.out_sums = move_first(live.out_sums)

    def back_call(slot, kept):
        one = lambda *dims: pl.BlockSpec((1, SPAN) + dims, lambda c: (slot, c) + (0,) * len(dims))
        anywhere = [pl.BlockSpec(memory_space=pl.ANY)] * len(kept)
        return call(
            functools.partial(back_kernel, len(kept)),
            (spans,),
            [
                one(EC), one(2 * NS), one(NS), one(NS), pl.BlockSpec((1, 1, 8, NS), lambda c: (slot, c, 0, 0)), one(EC),
                pl.BlockSpec((nz, 1, NS // nz, EC), lambda c: (0, slot, 0, 0)),
                pl.BlockSpec((1, 1, NS, EC), lambda c: (slot, c, 0, 0)),
            ]
            + anywhere,
            [one(EC), one(2 * NS), one(NS), one(NS)],
            [shape(2, rows, EC), shape(2, rows, 2 * NS), shape(2, rows, NS), shape(2, rows, NS)],
            [
                pltpu.VMEM((SPAN, SPAN), F32), pltpu.VMEM((SPAN, SPAN), F32), pltpu.VMEM((NS, SPAN), F32),
                pltpu.VMEM((NS, SPAN), F32),
            ],
            input_output_aliases={8 + i: i for i in range(len(kept))},
        )(live.x, live.bc, live.step, live.cum, live.before, live.d_ssm, live.state_in, live.local, *kept)

    live.first_slot = back_call(0, ())
    del live.backs
    settle(live)

    live.gate_sums = move_first(live.gate_sums)
    live.mixer_part = swapped(live.mixer_part, "core")
    live.dxs, live.d_bc, live.d_cum, live.d_step = back_call(1, live.first_slot)
    del live.first_slot, live.before
    settle(live)

    live.out_sums = cut_second(live.out_sums)
    live.gate_sums = cut_second(live.gate_sums)
    settle(live)
    live.out_sums = move_second(live.out_sums)
    live.gate_sums = move_second(live.gate_sums)
    slot_state = pl.BlockSpec((nz, 1, NS // nz, EC), lambda s: (0, s, 0, 0))
    d_proj, mine, theirs, g_taps, g_heads = call(
        functools.partial(close_kernel, rows, nz),
        (2,),
        [
            whole_row(rows, EC), whole_row(rows, 2 * NS), whole_row(rows, NS), whole_row(rows, NS), whole_row(rows, EC),
            whole_row(tall, WIDE), fixed(8, WIDE), fixed(8, NS), whole_row(rows, EC), whole_row(rows, 2 * NS),
            whole_row(rows, NS), whole_row(rows, NS), slot_state, whole_row(spans, NS, EC), slot_state,
            whole_row(spans, NS, EC),
        ],
        [whole_row(tall, BACK), whole_row(rows, NS), whole_row(rows, NS), whole_row(8, EC), whole_row(8, NS)],
        [shape(2, tall, BACK, dtype=BF16), shape(2, rows, NS), shape(2, rows, NS), shape(2, 8, EC), shape(2, 8, NS)],
        [pltpu.VMEM((HALO + rows + HALO, EC), F32)],
    )(live.x, live.bc, live.step, live.cum, live.d_ssm, live.proj, live.taps, live.heads_par, live.dxs, live.d_bc, live.d_cum, live.d_step, live.state_in, live.local, live.back_in, live.back_local)

    live.d_proj, live.bc_mine, live.bc_theirs, live.g_taps, live.g_heads = d_proj, mine, theirs, g_taps, g_heads
    del live.x, live.bc, live.step, live.cum, live.d_ssm, live.taps, live.heads_par, live.dxs, live.d_bc, live.d_cum
    live.block_out, live.stats = block_rows(bounds, live.own_in, live.mixer_own, live.mixer_part)
    del live.d_step, live.state_in, live.local, live.back_in, live.back_local, live.mixer_own, live.mixer_part
    settle(live)

    live.out_sums = cut_line(live.out_sums)
    live.block_keep, live.block_send = by_slots(live.block_out)
    del live.block_out
    settle(live)
    live.out_sums = move(live.out_sums, "z")
    live.block_send = swapped(live.block_send, "y")
    mine, theirs, d_proj, proj, own_taps = (
        live.bc_mine, swapped(live.bc_theirs, "core"), live.d_proj, live.proj, live.own_taps
    )
    column = pl.BlockSpec((1, tall, NS), lambda s: (s, 0, OWN // NS))
    d_proj, g_own = call(
        functools.partial(own_kernel, rows),
        (2,),
        [pl.BlockSpec(memory_space=pl.ANY), whole_row(rows, NS), whole_row(rows, NS), column, fixed(8, NS)],
        [column, whole_row(8, NS)],
        [shape(2, tall, BACK, dtype=BF16), shape(2, 8, NS)],
        [pltpu.VMEM((HALO + rows + HALO, NS), F32)],
        input_output_aliases={0: 0},
    )(d_proj, mine, theirs, proj, own_taps)

    live.d_proj, live.g_own = d_proj, g_own
    live.scan_sums = outer(live.normed, d_proj)
    del live.bc_mine, live.bc_theirs, live.proj, live.own_taps, live.normed
    settle(live)

    live.scan_sums = cut_first(live.scan_sums.reshape(nx, 2, nz, ny, deep, BACK), False)
    live.gate_sums = cut_line(live.gate_sums)
    settle(live)
    live.scan_sums = move_first(live.scan_sums)
    live.gate_sums = move(live.gate_sums, "z")
    live.d_own, live.d_came = to_normed(core, live.d_proj, live.d_gate, live.scan_weight, live.gate_weight)
    del live.d_proj, live.d_gate, live.scan_weight, live.gate_weight
    settle(live)

    live.scan_sums = cut_second(live.scan_sums)
    halo_own, halo_came = live.d_own[:HALO], live.d_came[:HALO]
    settle(live)
    live.scan_sums = move_second(live.scan_sums)
    live.back_own = lax.ppermute(halo_own, "z", [(i + 1, i) for i in range(nz - 1)])
    across = [(c * nz + i + 1, (1 - c) * nz + i) for c in range(2) for i in range(nz - 1)]
    live.back_came = lax.ppermute(halo_came, ("core", "z"), across)
    live.d_came = swapped(live.d_came, "core")
    live.out_sums = add_up(live.out_sums)
    live.gate_sums = add_up(live.gate_sums)
    settle(live)

    live.scan_sums = cut_line(live.scan_sums)
    settle(live)
    live.scan_sums = move(live.scan_sums, "z")
    live.grad_in, g_gain_in = input_rows(
        bounds, live.own_in, live.own_grad, live.d_own, live.d_came, live.back_own, live.back_came, live.gain_in
    )

    def spread_half(value, width):
        parts = value.reshape(value.shape[:-1] + (nx, 1, width // (2 * nx)))
        zero = jnp.zeros_like(parts)
        first = core == 0
        both = jnp.concatenate([jnp.where(first, parts, zero), jnp.where(first, zero, parts)], axis=-2)
        return both.reshape(value.shape[:-1] + (width,))

    taps_sum = jnp.sum(live.g_taps, axis=0)
    own_sum = jnp.sum(live.g_own, axis=0)
    nothing = jnp.zeros_like(own_sum)
    taps_sum = jnp.concatenate(
        [
            spread_half(taps_sum, E),
            jnp.where(core == 0, own_sum, nothing),
            jnp.where(core == 0, nothing, own_sum),
        ],
        axis=1,
    )
    head_sum = spread_half(jnp.sum(live.g_heads, axis=0)[:3, :HC], H)
    packed = jnp.concatenate(
        [
            taps_sum[: CONV + 1].reshape(-1),
            spread_half(live.g_gain_out[0], E),
            g_gain_in[0],
            head_sum.reshape(-1),
            live.stats[0, :3],
        ]
    )
    live.packed = jnp.pad(packed, (0, -packed.shape[0] % 1024)).reshape(-1, NS)
    live.grad_keep, live.grad_send = by_slots(live.grad_in)
    del live.own_in, live.own_grad, live.d_own, live.d_came, live.g_taps, live.g_own, live.g_heads, live.grad_in
    del live.g_gain_out, live.gain_in, live.back_own, live.back_came, live.stats
    settle(live)

    packed = sum_everywhere(live.packed).reshape(-1)
    grad_in = by_index("y", live.grad_keep, swapped(live.grad_send, "y"))
    block_out = by_index("y", live.block_keep, live.block_send)
    g_out = live.out_sums.reshape(thin, features)

    def row_share(value):
        return take(value, core, 0), swapped(take(value, 1 - core, 0), "core")

    gate_mine, gate_came = row_share(live.gate_sums)
    scan_mine, scan_came = row_share(add_up(live.scan_sums))
    place_at = [0]
    for size in ((CONV + 1) * CH, E, features, 3 * H, 3):
        place_at.append(place_at[-1] + size)
    device = ((ix * 2 + core) * nz + iz) * ny + iy
    taps_total = packed[: place_at[1]].reshape(CONV + 1, CH)
    taps_mine = lax.dynamic_slice_in_dim(taps_total, device * chan, chan, 1)
    gain_out_mine = lax.dynamic_slice_in_dim(packed[place_at[1] : place_at[2]], device * thin, thin)
    gain_in_mine = lax.dynamic_slice_in_dim(packed[place_at[2] : place_at[3]], device * deep, deep)
    head_total = packed[place_at[3] : place_at[4]].reshape(3, H)
    valid_sums = packed[place_at[4] : place_at[5]]

    def both_halves(mine_part, came_part):
        pair = by_index("core", mine_part, came_part)
        width = mine_part.shape[-1]
        return pair.reshape(2, deep, nx, width // nx).transpose(1, 2, 0, 3).reshape(deep, 2 * width)

    own_pair = by_index("core", scan_mine[:, OWN:STEP], scan_came[:, OWN:STEP])
    g_in_weight = jnp.concatenate(
        [
            both_halves(gate_mine, gate_came),
            both_halves(scan_mine[:, :EC], scan_came[:, :EC]),
            own_pair[0],
            own_pair[1],
            both_halves(scan_mine[:, STEP : STEP + HC], scan_came[:, STEP : STEP + HC]),
        ],
        axis=1,
    )
    token_total = jnp.sum(lengths).astype(F32) * features
    rms_stats = jnp.sqrt(valid_sums / token_total)
    return (
        block_out,
        grad_in,
        gain_in_mine,
        g_in_weight,
        taps_mine[:CONV],
        taps_mine[CONV],
        head_total[0],
        head_total[1],
        head_total[2],
        gain_out_mine,
        g_out,
        rms_stats,
    )


def solution(mesh):
    nb, ns = mesh.shape["batch"], mesh.shape["seq"]
    fine = Mesh(mesh.devices.reshape(nb // 2, 2, ns // 2, 2), ("x", "core", "z", "y"))
    batch, seq = ("x", "core"), ("z", "y")
    every = batch + seq
    act = P(batch, seq, None)
    return jax.shard_map(
        shards,
        mesh=fine,
        in_specs=(
            act, P(), P(every), P(every, None), P(None, every), P(every), P(), P(), P(), P(every), P(every, None), act,
        ),
        out_specs=(
            act, act, P(every), P(every, None), P(None, every), P(every), P(), P(), P(), P(every), P(every, None), P(),
        ),
        check_vma=False,
    )
```

```python
import functools
import types

import jax
import jax.numpy as jnp
from jax import lax
from jax.experimental import pallas as pl
from jax.experimental.pallas import tpu as pltpu
from jax.sharding import Mesh
from jax.sharding import PartitionSpec as P

H = 48
P_SIZE = 64
NS = 128
CONV = 4
SPAN = 256
E = 3072
CH = 3328

HC = H // 2
EC = E // 2
HALO = 16
OWN = EC
STEP = EC + NS
OTHER = EC + 2 * NS
WIDE = EC + 3 * NS
BACK = EC + 2 * NS

EPSILON = 1e-05
BF16 = jnp.bfloat16
VM = 60
UNROLL = 6
F32 = jnp.float32


def settle(live):
    live.__dict__.update(lax.optimization_barrier(dict(live.__dict__)))


def others(piece, axis):
    size = lax.axis_size(axis)
    here = lax.axis_index(axis)
    moved = []
    for step in range(1, size):
        route = [(i, (i + step) % size) for i in range(size)]
        moved.append((lax.rem(here - step + size, size), lax.ppermute(piece, axis, route)))
    return moved


def everyone(piece, axis):
    return [(lax.axis_index(axis), piece)] + others(piece, axis)


def shared(value, axes):
    count = 1
    for axis in axes:
        count *= lax.axis_size(axis)
    return lax.all_to_all(jnp.broadcast_to(value, (count,) + value.shape), axes, 0, 0, tiled=True)


def by_index(axis, mine, other):
    first = lax.axis_index(axis) == 0
    return jnp.where(first, jnp.stack([mine, other]), jnp.stack([other, mine]))


def swapped(piece, axis):
    return lax.ppermute(piece, axis, [(0, 1), (1, 0)])


def take(value, index, axis):
    return lax.dynamic_index_in_dim(value, index, axis, keepdims=False)


def copy_plan(items):
    values, scalars, plan = [], [], []
    for piece, source, out, target in items:
        known = [i for i, v in enumerate(values) if v is piece]
        if not known:
            values.append(piece)
            known = [len(values) - 1]
        at = []
        for index in target:
            if index is None or isinstance(index, int):
                at.append(index)
            else:
                scalars.append(index)
                at.append((len(scalars) - 1,))
        plan.append((known[0], source, out, at))
    return values, jnp.stack(scalars).astype(jnp.int32), plan


def copy_all(plan, table, inputs, results, sems):
    copies = []
    for number, (known, source, out, at) in enumerate(plan):
        here = tuple(slice(None) if i is None else i for i in source)
        there = tuple(slice(None) if i is None else (table[i[0]] if isinstance(i, tuple) else i) for i in at)
        origin = inputs[known].at[here] if here else inputs[known]
        copies.append(pltpu.make_async_copy(origin, results[out].at[there], sems.at[number]))
    for copy in copies:
        copy.start()
    for copy in copies:
        copy.wait()


ANYWHERE = pl.BlockSpec(memory_space=pltpu.HBM)
NO_COST = pl.CostEstimate(flops=0, bytes_accessed=1024, transcendentals=0)


def assemble(outs, items, dtype):
    values, table, plan = copy_plan(items)
    count = len(values)

    def kernel(table_ref, *refs):
        copy_all(plan, table_ref, refs[:count], refs[count:-1], refs[-1])

    return pl.pallas_call(
        kernel,
        in_specs=[pl.BlockSpec(memory_space=pltpu.SMEM)] + [ANYWHERE] * count,
        out_specs=[pl.BlockSpec(memory_space=pltpu.VMEM)] * len(outs),
        out_shape=[jax.ShapeDtypeStruct(dims, dtype) for dims in outs],
        scratch_shapes=[pltpu.SemaphoreType.DMA((len(plan),))],
        compiler_params=pltpu.CompilerParams(vmem_limit_bytes=16 * 1024 * 1024),
        cost_estimate=NO_COST,
    )(table, *values)


ORDERS = (("y", "x"), ("x", "y"))


def join_line(everybody):
    _, rows, columns = everybody[0][1].shape
    items = [(piece, (half,), half, (index,)) for index, piece in everybody for half in range(2)]
    return assemble([(len(everybody), rows, columns)] * 2, items, everybody[0][1].dtype)


def plane_first(line):
    return [everyone(line[half], ORDERS[half][0]) for half in range(2)]


def plane_stack(held):
    items, outs = [], []
    for half, pieces in enumerate(held):
        outs.append((len(pieces),) + pieces[0][1].shape)
        items += [(piece, (), half, (index,)) for index, piece in pieces]
    return assemble(outs, items, held[0][0][1].dtype)


def plane_second(both):
    return [everyone(both[half], ORDERS[half][1]) for half in range(2)]


def plane_items(held, inner):
    nx, ny = lax.axis_size("x"), lax.axis_size("y")
    _, nz, rows, columns = held[0][0][1].shape
    dims = (nx, nz, ny, 2, rows, columns) if inner else (nx, 2, nz, ny, rows, columns)
    items = []
    for half, pieces in enumerate(held):
        for index, piece in pieces:
            for k in range(piece.shape[0]):
                at_x, at_y = (index, k) if half == 0 else (k, index)
                items.append((piece, (k,), 0, (at_x, None, at_y, half) if inner else (at_x, half, None, at_y)))
    return dims, items


def cut(value, axis, dim):
    size = lax.axis_size(axis)
    here = lax.axis_index(axis)
    return take(value, here, dim), [take(value, lax.rem(here + step, size), dim) for step in range(1, size)]


def move(held, axis):
    mine, going = held
    size = lax.axis_size(axis)
    came = []
    for step, piece in enumerate(going, 1):
        came.append(lax.ppermute(piece, axis, [(i, (i + step) % size) for i in range(size)]))
    return mine, came


def add_up(held):
    mine, came = held
    total = mine.astype(F32)
    for piece in came:
        total = total + piece.astype(F32)
    return total


def cut_first(whole, inner):
    return [
        cut(whole[:, :, :, half] if inner else whole[:, half], axis, 0 if axis == "x" else 2)
        for half, (_, axis) in enumerate(ORDERS)
    ]


def move_first(held):
    return [move(one, axis) for one, (_, axis) in zip(held, ORDERS)]


def cut_second(held):
    return [cut(add_up(one).astype(BF16), axis, 0 if axis == "x" else 1) for one, (axis, _) in zip(held, ORDERS)]


def move_second(held):
    return [move(one, axis) for one, (axis, _) in zip(held, ORDERS)]


def cut_line(held):
    return cut(jnp.stack([add_up(one).astype(BF16) for one in held]), "z", 1)


def sum_everywhere(value):
    for axis in ("core", "x", "z", "y"):
        size = lax.axis_size(axis)
        step = 1
        while step < size:
            route = [(i, i ^ step) for i in range(size)]
            value = value + lax.ppermute(value, axis, route)
            step *= 2
    return value


def nn(a, b):
    return lax.dot_general(a, b, (((1,), (0,)), ((), ())), preferred_element_type=F32)


def nt(a, b):
    return lax.dot_general(a, b, (((1,), (1,)), ((), ())), preferred_element_type=F32)


def tn(a, b):
    return lax.dot_general(a, b, (((0,), (0,)), ((), ())), preferred_element_type=F32)


def pieces_of(value, count):
    parts = []
    rest = value
    for index in range(count):
        part = rest.astype(BF16)
        parts.append(part)
        if index < count - 1:
            rest = rest - part.astype(F32)
    return parts


PIECE = 32


def nt_fine(a, b):
    a_high, a_low = pieces_of(a, 2)
    b_high, b_low = pieces_of(b, 2)
    return nt(jnp.concatenate([a_high, a_low, a_high], axis=1), jnp.concatenate([b_high, b_high, b_low], axis=1))


def head_map():
    row = lax.rem(lax.broadcasted_iota(jnp.int32, (NS, EC), 0), PIECE)
    lane = lax.broadcasted_iota(jnp.int32, (NS, EC), 1)
    inside = (lane >= row * P_SIZE) & (lane < row * P_SIZE + P_SIZE)
    return jnp.where(inside, 1.0, 0.0).astype(BF16)


def head_sums():
    row = lax.broadcasted_iota(jnp.int32, (EC, NS), 0)
    lane = lax.broadcasted_iota(jnp.int32, (EC, NS), 1)
    inside = (row >= lane * P_SIZE) & (row < lane * P_SIZE + P_SIZE)
    return jnp.where(inside, 1.0, 0.0).astype(BF16)


def packed(value):
    lane = lax.broadcasted_iota(jnp.int32, value.shape, 1)
    high, mid, low = (p.astype(F32) for p in pieces_of(jnp.where(lane < HC, value, 0.0), 3))
    return (high + pltpu.roll(mid, PIECE, 1) + pltpu.roll(low, 2 * PIECE, 1)).astype(BF16)


def spread(value, heads):
    return nn(packed(value), heads)


def gathered_heads(value, sums, count=1):
    return sum(nn(part, sums) for part in pieces_of(value, count))


def triangle(kind):
    row = lax.broadcasted_iota(jnp.int32, (SPAN, SPAN), 0)
    col = lax.broadcasted_iota(jnp.int32, (SPAN, SPAN), 1)
    keep = {"ge": row >= col, "gt": row > col, "le": row <= col}[kind]
    return jnp.where(keep, 1.0, 0.0)


def exact_sum(matrix, value):
    low = matrix.astype(BF16)
    return sum(nn(low, part) for part in pieces_of(value, 3))


def sigmoid(v):
    return 0.5 * jnp.tanh(0.5 * v) + 0.5


def softplus(v):
    return jnp.maximum(v, 0.0) + jnp.log1p(jnp.exp(-jnp.abs(v)))


def call(kernel, grid, in_specs, out_specs, out_shape, scratch=(), vmem=VM, **more):
    return pl.pallas_call(
        kernel,
        grid=grid,
        in_specs=in_specs,
        out_specs=out_specs,
        out_shape=out_shape,
        scratch_shapes=list(scratch),
        compiler_params=pltpu.CompilerParams(vmem_limit_bytes=vmem * 1024 * 1024),
        cost_estimate=NO_COST,
        **more,
    )


def shape(*dims, dtype=F32):
    return jax.ShapeDtypeStruct(dims, dtype)


def fixed(*dims):
    return pl.BlockSpec(dims, lambda *_: (0,) * len(dims))


def conv_kernel(rows, nz, proj, taps, heads_par, x_out, bc_out, step_out, cum_out, state_out, local_out):
    heads = head_map()
    spans = rows // SPAN
    lower = triangle("ge")
    state = jnp.zeros((NS, EC), F32)
    total = jnp.zeros((1, NS), F32)
    core_one = heads_par[3:4, :] > 0.5
    for span in range(spans):
        start = HALO + span * SPAN

        def activated(first, width):
            running = taps[4:5, first : first + width]
            for k in range(CONV):
                at = start - (CONV - 1) + k
                running = running + taps[k : k + 1, first : first + width] * proj[0, at : at + SPAN, first : first + width]
            return running * sigmoid(running)

        own = activated(OWN, NS)
        other = activated(OTHER, NS)
        write_full = jnp.where(core_one, other, own)
        write = write_full.astype(BF16)
        here = slice(span * SPAN, span * SPAN + SPAN)
        bc_out[0, here, :NS] = write_full
        bc_out[0, here, NS:] = jnp.where(core_one, own, other)
        raw = proj[0, start : start + SPAN, STEP : STEP + NS] + heads_par[0:1, :]
        step = softplus(raw)
        cum = exact_sum(lower, -step * heads_par[1:2, :])
        step_out[0, here] = step
        cum_out[0, here] = cum
        last = cum[SPAN - 1 : SPAN]
        tail_low = packed(jnp.exp(last - cum) * step)
        local_out[0, span] = state.astype(BF16)
        decay = spread(jnp.broadcast_to(jnp.exp(last), (8, NS)), heads)[0:1]
        wide = EC // 2
        fresh = []
        for half in range(2):
            cols = slice(half * wide, half * wide + wide)
            x = activated(half * wide, wide)
            x_out[0, here, cols] = x
            fresh.append(tn(write, (x * nn(tail_low, heads[:, cols])).astype(BF16)))
        state = state * decay + jnp.concatenate(fresh, axis=1)
        total = total + last
    depth = NS // nz
    for group in range(nz):
        state_out[group, 0, :, :EC] = state[group * depth : (group + 1) * depth].astype(BF16)
    row = lax.broadcasted_iota(jnp.int32, (depth, NS), 0)
    high, mid, low = (part.astype(F32) for part in pieces_of(total, 3))
    total_rows = jnp.where(row == 0, high, jnp.where(row == 1, mid, jnp.where(row == 2, low, 0.0))).astype(BF16)
    for group in range(nz):
        state_out[group, 0, :, EC:] = total_rows


def intra_kernel(x_ref, bc_ref, step_ref, cum_ref, heads_par, out_ref, xs_ref, cross_ref, cumt_ref):
    heads = head_map()
    step_wide = spread(step_ref[0], heads)
    xs_ref[...] = (x_ref[0] * step_wide).astype(BF16)
    cum = cum_ref[0]
    cumt_ref[...] = cum.T
    cross_ref[...] = nt_fine(bc_ref[0, :, NS:], bc_ref[0, :, :NS]) * triangle("ge")
    skip = spread(jnp.broadcast_to(heads_par[2:3, :], (8, NS)), heads)[0:1]
    out_ref[0] = x_ref[0] * skip
    low = lax.broadcasted_iota(jnp.int32, (SPAN, NS), 1) < P_SIZE

    def pair(p, carry):
        lanes = pl.ds(pl.multiple_of(p * NS, NS), NS)
        xs = xs_ref[:, lanes]
        made = []
        for j in range(2):
            h = 2 * p + j
            col = pltpu.roll(cum, lax.rem(NS - h, NS), 1)[:, 0:1]
            row = cumt_ref[pl.ds(h, 1), :]
            mix = jnp.exp(jnp.minimum(col - row, 0.0)) * cross_ref[...]
            made.append(nn(mix.astype(BF16), xs))
        out_ref[0, :, lanes] += jnp.where(low, made[0], made[1])
        return carry

    lax.fori_loop(0, HC // 2, pair, 0, unroll=UNROLL)


def span_state(state_ref, local_ref, before, heads):
    whole = jnp.concatenate([state_ref[g, 0] for g in range(state_ref.shape[0])], axis=0)
    decay = spread(jnp.broadcast_to(jnp.exp(before), (8, NS)), heads)[0:1]
    return whole.astype(F32) * decay + local_ref[0, 0].astype(F32)


def finish_kernel(part_ref, bc_ref, cum_ref, before_ref, state_ref, local_ref, gate_ref, dmix_ref, gain_ref, out_ref, sums_ref):
    heads = head_map()
    state = span_state(state_ref, local_ref, before_ref[0, 0, 0:1], heads).astype(BF16)
    grown = spread(jnp.exp(cum_ref[0]), heads)
    y = part_ref[0] + grown * nn(bc_ref[0, :, NS:].astype(BF16), state)
    out_ref[0] = y
    gate = gate_ref[0]
    gated = y * gate * sigmoid(gate)
    squares = jnp.sum(gated * gated, axis=1, keepdims=True)
    slopes = jnp.sum(gated * gain_ref[0:1, :] * dmix_ref[0], axis=1, keepdims=True)
    lane = lax.broadcasted_iota(jnp.int32, (SPAN, NS), 1)
    sums_ref[0] = jnp.where(lane == 0, squares, jnp.where(lane == 1, slopes, 0.0))


def gate_kernel(
    spans, nz, y_ref, gate_ref, dmix_ref, sums_ref, gain_ref, bc_ref, cum_ref,
    mix_out, dy_out, dgate_out, ggain_out, state_out, local_out, run_ref,
):
    step = pl.program_id(1)
    heads = head_map()
    squares = sums_ref[0, :, 0:1]
    slopes = sums_ref[0, :, 1:2]
    scale = lax.rsqrt(squares / E + EPSILON)
    y = y_ref[0]
    gate = gate_ref[0]
    soft = sigmoid(gate)
    silu = gate * soft
    gated = y * silu
    gain = gain_ref[0:1, :]
    dmix = dmix_ref[0]
    mix_out[0] = (gated * scale * gain).astype(BF16)
    dgated = scale * (gain * dmix - gated * (scale * scale * slopes / E))
    dy = dgated * silu
    dy_out[0] = dy
    dgate_out[0] = (dgated * y * (soft * (1.0 + gate * (1.0 - soft)))).astype(BF16)

    @pl.when((step == 0) & (pl.program_id(0) == 0))
    def _():
        ggain_out[...] = jnp.zeros_like(ggain_out)

    ggain_out[...] += jnp.broadcast_to(jnp.sum(gated * scale * dmix, axis=0, keepdims=True), (8, EC))

    @pl.when(step == 0)
    def _():
        run_ref[...] = jnp.zeros_like(run_ref)

    cum = cum_ref[0]
    grown = spread(jnp.exp(cum), heads)
    fresh = tn(bc_ref[0, :, NS:].astype(BF16), (dy * grown).astype(BF16))
    local_out[0, 0] = run_ref[...].astype(BF16)
    run_ref[...] = fresh + run_ref[...] * grown[SPAN - 1 : SPAN]

    @pl.when(step == spans - 1)
    def _():
        depth = NS // nz
        for group in range(nz):
            state_out[group, 0] = run_ref[group * depth : (group + 1) * depth].astype(BF16)


def back_kernel(kept, x_ref, bc_ref, step_ref, cum_ref, before_ref, dy_ref, state_ref, local_ref, *refs):
    dxs_out, dbc_out, dcum_out, dstep_out, cross_ref, dcross_ref, cumt_ref, rows_ref = refs[kept:]
    heads = head_map()
    sums = head_sums()
    cum = cum_ref[0]
    step = step_ref[0]
    cumt_ref[...] = cum.T
    write = bc_ref[0, :, :NS].astype(BF16)
    read = bc_ref[0, :, NS:].astype(BF16)
    mask = triangle("le")
    cross_ref[...] = nt_fine(bc_ref[0, :, :NS], bc_ref[0, :, NS:]) * mask
    dcross_ref[...] = jnp.zeros_like(dcross_ref)
    rows_ref[...] = jnp.zeros_like(rows_ref)
    lane = lax.broadcasted_iota(jnp.int32, (SPAN, NS), 1)
    low = lane < P_SIZE

    def pair(p, cols):
        lanes = pl.ds(pl.multiple_of(p * NS, NS), NS)
        x_high, x_low = (part.astype(F32) for part in pieces_of(x_ref[0, :, lanes], 2))
        dy, dy_low = pieces_of(dy_ref[0, :, lanes], 2)
        right = jnp.concatenate([dy, dy, dy_low], axis=1)
        made = []
        for j in range(2):
            h = 2 * p + j
            col = pltpu.roll(cum, lax.rem(NS - h, NS), 1)[:, 0:1]
            step_col = pltpu.roll(step, lax.rem(NS - h, NS), 1)[:, 0:1]
            row = cumt_ref[pl.ds(h, 1), :]
            decay = jnp.exp(jnp.minimum(row - col, 0.0))
            mine = low if j == 0 else ~low
            high = jnp.where(mine, x_high, 0.0).astype(BF16)
            rest = jnp.where(mine, x_low, 0.0).astype(BF16)
            slope = nt(jnp.concatenate([high, rest, high], axis=1), right) * decay
            cross = cross_ref[...]
            cols = jnp.where(lane == h, jnp.sum(slope * cross, axis=1, keepdims=True), cols)
            slope = slope * step_col
            dcross_ref[...] += slope
            rows_ref[pl.ds(h, 1), :] = jnp.sum(slope * cross, axis=0, keepdims=True)
            made.append(nn((decay * cross).astype(BF16), dy))
        dxs_out[0, :, lanes] = jnp.where(low, made[0], made[1])
        return cols

    cols = lax.fori_loop(0, HC // 2, pair, jnp.zeros((SPAN, NS), F32))
    dcross = (dcross_ref[...] * mask).astype(BF16)
    state = span_state(state_ref, local_ref, before_ref[0, 0, 0:1], heads).astype(BF16)
    grown = spread(jnp.exp(cum), heads)
    dye = dy_ref[0] * grown
    inter = gathered_heads(dye * nn(read, state), sums)
    dstep_out[0] = cols
    dbc_out[0, :, :NS] = nn(dcross, read)
    dbc_out[0, :, NS:] = tn(dcross, write) + nt(dye.astype(BF16), state)
    dcum_out[0] = rows_ref[...].T - step * cols + inter


def close_kernel(
    rows, nz, x_ref, bc_ref, step_ref, cum_ref, dy_ref, proj_ref, taps, heads_par, dxs_ref, dbc_ref, dcum_ref, dstep_ref,
    state_ref, local_ref, back_ref, blocal_ref, dproj_out, mine_out, theirs_out, gtaps_out, ghead_out, dpre_ref,
):
    core_one = heads_par[3:4, :] > 0.5
    heads = head_map()
    sums = head_sums()
    spans = rows // SPAN
    upper = triangle("le")
    below = triangle("gt")
    whole_in = jnp.concatenate([state_ref[g, 0] for g in range(nz)], axis=0).astype(F32)
    whole_back = jnp.concatenate([back_ref[g, 0] for g in range(nz)], axis=0).astype(F32)
    lasts = [cum_ref[0, (c + 1) * SPAN - 1 : (c + 1) * SPAN] for c in range(spans)]
    skip = spread(jnp.broadcast_to(heads_par[2:3, :], (8, NS)), heads)[0:1]
    real = lax.broadcasted_iota(jnp.int32, (SPAN, NS), 1) < HC
    dpre_ref[:HALO] = jnp.zeros((HALO, EC), F32)
    dpre_ref[HALO + rows :] = jnp.zeros((HALO, EC), F32)
    zero_row = jnp.zeros((1, NS), F32)
    gbias, gdecay, gskip = zero_row, zero_row, zero_row
    for span in range(spans):
        here = slice(span * SPAN, span * SPAN + SPAN)
        before = sum(lasts[:span], zero_row)
        after = sum(lasts[span + 1 :], zero_row)
        both = spread(jnp.exp(jnp.concatenate([before, after, lasts[span], jnp.zeros((5, NS), F32)], axis=0)), heads)
        state = whole_in * both[0:1] + local_ref[0, span].astype(F32)
        back = whole_back * both[1:2] + blocal_ref[0, span].astype(F32)
        back_low = back.astype(BF16)
        at_last = gathered_heads(
            jnp.broadcast_to(jnp.sum(state * back, axis=0, keepdims=True) * both[2:3], (8, EC)), sums, 2
        )[0:1]
        write = bc_ref[0, here, :NS].astype(BF16)
        cum = cum_ref[0, here]
        step = step_ref[0, here]
        x = x_ref[0, here]
        dy = dy_ref[0, here]
        tail = spread(jnp.exp(lasts[span] - cum), heads)
        step_wide = spread(step, heads)
        from_back = tail * nn(write, back_low)
        dxs = dxs_ref[0, here] + from_back
        later = gathered_heads(x * from_back, sums)
        dstep = dstep_ref[0, here] + later
        moved = step * later
        dwrite = dbc_ref[0, here, :NS] + nt((x * tail * step_wide).astype(BF16), back_low)
        dread = dbc_ref[0, here, NS:]
        mine_out[0, here] = jnp.where(core_one, dread, dwrite)
        theirs_out[0, here] = jnp.where(core_one, dwrite, dread)
        dlog = exact_sum(upper, dcum_ref[0, here]) + exact_sum(below, moved) + at_last
        raw = proj_ref[0, HALO + span * SPAN : HALO + span * SPAN + SPAN, STEP : STEP + NS] + heads_par[0:1, :]
        draw = jnp.where(real, (dstep - heads_par[1:2, :] * dlog) * sigmoid(raw), 0.0)
        dproj_out[0, HALO + span * SPAN : HALO + span * SPAN + SPAN, STEP : STEP + NS] = draw.astype(BF16)
        gbias = gbias + jnp.sum(draw, axis=0, keepdims=True)
        gdecay = gdecay + jnp.sum(jnp.where(real, dlog * (-step * heads_par[1:2, :]), 0.0), axis=0, keepdims=True)
        gskip = gskip + gathered_heads(jnp.broadcast_to(jnp.sum(dy * x, axis=0, keepdims=True), (8, EC)), sums, 3)[0:1]
        dx = dxs * step_wide + skip * dy
        start = HALO + span * SPAN
        pre = taps[4:5, :EC]
        for k in range(CONV):
            at = start - (CONV - 1) + k
            pre = pre + taps[k : k + 1, :EC] * proj_ref[0, at : at + SPAN, :EC]
        soft = sigmoid(pre)
        dpre_ref[start : start + SPAN] = dx * (soft * (1.0 + pre * (1.0 - soft)))
    conv_back(rows, dpre_ref, proj_ref, taps, 0, EC, dproj_out, 0, gtaps_out)
    dproj_out[0, :HALO, STEP : STEP + NS] = jnp.zeros((HALO, NS), BF16)
    ghead_out[0] = jnp.concatenate([gbias, gdecay, gskip, jnp.zeros((5, NS), F32)], axis=0)


def conv_back(rows, dpre_ref, proj_ref, taps, first, width, dproj_out, out_first, gtaps_out):
    sums = [jnp.zeros((1, width), F32)] * (CONV + 1)
    blocks = [(0, HALO)] + [(HALO + s * SPAN, SPAN) for s in range(rows // SPAN)]
    for start, count in blocks:
        running = jnp.zeros((count, width), F32)
        for k in range(CONV):
            at = start + (CONV - 1) - k
            running = running + taps[k : k + 1, first : first + width] * dpre_ref[at : at + count]
        dproj_out[0, start : start + count, out_first : out_first + width] = running.astype(BF16)
        if count == SPAN:
            dpre = dpre_ref[start : start + count]
            for k in range(CONV):
                at = start - (CONV - 1) + k
                sums[k] = sums[k] + jnp.sum(dpre * proj_ref[0, at : at + count, first : first + width], axis=0, keepdims=True)
            sums[CONV] = sums[CONV] + jnp.sum(dpre, axis=0, keepdims=True)
    gtaps_out[0, :, :width] = jnp.concatenate(sums + [jnp.zeros((3, width), F32)], axis=0)


def own_kernel(rows, dproj_in, mine_ref, came_ref, proj_ref, taps, dproj_out, gtaps_out, dpre_ref):
    dpre_ref[:HALO] = jnp.zeros((HALO, NS), F32)
    dpre_ref[HALO + rows :] = jnp.zeros((HALO, NS), F32)
    for span in range(rows // SPAN):
        start = HALO + span * SPAN
        pre = taps[4:5, :]
        for k in range(CONV):
            at = start - (CONV - 1) + k
            pre = pre + taps[k : k + 1, :] * proj_ref[0, at : at + SPAN]
        soft = sigmoid(pre)
        here = slice(span * SPAN, span * SPAN + SPAN)
        dconv = mine_ref[0, here] + came_ref[0, here]
        dpre_ref[start : start + SPAN] = dconv * (soft * (1.0 + pre * (1.0 - soft)))
    conv_back(rows, dpre_ref, proj_ref, taps, 0, NS, dproj_out, 0, gtaps_out)


def outer_kernel(halo, a_ref, b_ref, out_ref):
    slots, _, width = a_ref.shape
    left = a_ref[...][:, halo:].reshape(-1, width)
    right = b_ref[...].reshape(left.shape[0], -1)
    out_ref[...] = tn(left, right).astype(BF16)


def outer(a, b, halo=0):
    slots, tall, left = a.shape
    rows, right = b.shape[1:]
    tile = 256
    return call(
        functools.partial(outer_kernel, halo),
        (left // tile,),
        [pl.BlockSpec((slots, tall, tile), lambda i: (0, 0, i)), fixed(slots, rows, right)],
        pl.BlockSpec((tile, right), lambda i: (i, 0)),
        shape(left, right, dtype=BF16),
    )(a, b)


def outer_cut(a, b, inner, halo=0):
    nx, nz, ny = lax.axis_size("x"), lax.axis_size("z"), lax.axis_size("y")
    slots, tall, left = a.shape
    rows, right = b.shape[1:]
    deep = left // (2 * nx * nz * ny)
    if nx != 2 or nz % 2 or deep % 16:
        dims = (nx, nz, ny, 2, deep, right) if inner else (nx, 2, nz, ny, deep, right)
        return cut_first(outer(a, b, halo).reshape(dims), inner)
    tile = left // 4
    few = nz // 2

    def kernel(place_ref, a_ref, b_ref, stay0, go0, stay1, go1):
        at = pl.program_id(0)
        x = at // 2
        here = place_ref[0] == x
        low = place_ref[1] == 0
        part = a_ref[...][:, halo:].reshape(-1, tile)
        made = tn(part, b_ref[...].reshape(part.shape[0], -1)).astype(BF16)

        def split(value):
            return jnp.where(low, value[:, 0], value[:, 1]), jnp.where(low, value[:, 1], value[:, 0])

        if inner:
            made = made.reshape(few, ny, 2, deep, right)
            group = pl.ds((at % 2) * few, few)

            @pl.when(here)
            def _():
                stay0[group] = made[:, :, 0]

            @pl.when(jnp.logical_not(here))
            def _():
                go0[group] = made[:, :, 0]

            stay1[x, group], go1[x, group] = split(made[:, :, 1])
        else:
            made = made.reshape(nz, ny, deep, right)
            first = at % 2 == 0

            @pl.when(first & here)
            def _():
                stay0[...] = made

            @pl.when(first & jnp.logical_not(here))
            def _():
                go0[...] = made

            @pl.when(jnp.logical_not(first))
            def _():
                stay1[x], go1[x] = split(made)

    half0, half1 = (nz, ny, deep, right), (nx, nz, deep, right)
    stay0, go0, stay1, go1 = call(
        kernel,
        (4,),
        [
            pl.BlockSpec(memory_space=pltpu.SMEM), pl.BlockSpec((slots, tall, tile), lambda i: (0, 0, i)),
            fixed(slots, rows, right),
        ],
        [fixed(*half0), fixed(*half0), fixed(*half1), fixed(*half1)],
        [shape(*d, dtype=BF16) for d in (half0, half0, half1, half1)],
    )(jnp.stack([lax.axis_index("x"), lax.axis_index("y")]), a, b)
    return [(stay0, [go0]), (stay1, [go1])]


def rows_kernel(turned, halo, a_ref, b_ref, out_ref):
    value = a_ref[0, halo:]
    out_ref[0] = (nt if turned else nn)(value, b_ref[...])


def by_rows(a, b, turned=False, halo=0):
    slots, tall, depth = a.shape
    right = b.shape[0 if turned else 1]
    return call(
        functools.partial(rows_kernel, turned, halo),
        (slots,),
        [pl.BlockSpec((1, tall, depth), lambda s: (s, 0, 0)), fixed(*b.shape)],
        pl.BlockSpec((1, tall - halo, right), lambda s: (s, 0, 0)),
        shape(slots, tall - halo, right),
    )(a, b)


def by_rows_of(a, held, inner, turned=False, halo=0):
    dims, items = plane_items(held, inner)
    wide = dims[-1]
    deep = EC if inner else dims[0] * dims[1] * dims[2] * dims[3] * dims[4]
    if dims[4] % 16:
        whole = assemble([dims], items, BF16)[0].reshape(deep, wide)
        return by_rows(a, whole, turned, halo), whole
    values, table, plan = copy_plan(items)
    count = len(values)
    slots, tall, depth = a.shape
    right = deep if turned else wide

    def kernel(table_ref, a_ref, *refs):
        pieces, out_ref, whole_ref, held_ref, sems, whole_sem = refs[:count], *refs[count:]
        store = pltpu.make_async_copy(held_ref, whole_ref, whole_sem)

        @pl.when(pl.program_id(0) == 0)
        def _():
            copy_all(plan, table_ref, pieces, [held_ref], sems)
            store.start()

        matrix = held_ref[...].reshape(deep, wide)
        out_ref[0] = (nt if turned else nn)(a_ref[0, halo:], matrix)

        @pl.when(pl.program_id(0) == slots - 1)
        def _():
            store.wait()

    out, whole = call(
        kernel,
        (slots,),
        [pl.BlockSpec(memory_space=pltpu.SMEM), pl.BlockSpec((1, tall, depth), lambda s: (s, 0, 0))]
        + [ANYWHERE] * count,
        [pl.BlockSpec((1, tall - halo, right), lambda s: (s, 0, 0)), ANYWHERE],
        [shape(slots, tall - halo, right), shape(*dims, dtype=BF16)],
        [pltpu.VMEM(dims, BF16), pltpu.SemaphoreType.DMA((len(plan),)), pltpu.SemaphoreType.DMA],
    )(table, a, *values)
    return out, whole.reshape(deep, wide)


def normed_kernel(core_ref, dproj_ref, dgate_ref, scan_ref, gate_ref, own_ref, other_ref):
    scan, gate = scan_ref[...], gate_ref[...]
    core = core_ref[0]
    for slot, out_ref in ((core, own_ref), (1 - core, other_ref)):
        out_ref[:HALO] = nt(dproj_ref[slot, :HALO], scan)
        out_ref[HALO:] = nt(dproj_ref[slot, HALO:], scan) + nt(dgate_ref[slot], gate)


SMALL = pl.BlockSpec(memory_space=pltpu.SMEM)


def to_normed(core, d_proj, d_gate, scan_weight, gate_weight):
    slots, tall, _ = d_proj.shape
    features = gate_weight.shape[0]
    tile = 256
    return call(
        normed_kernel,
        (features // tile,),
        [
            SMALL, fixed(slots, tall, BACK), fixed(slots, tall - HALO, EC),
            pl.BlockSpec((tile, BACK), lambda i: (i, 0)), pl.BlockSpec((tile, EC), lambda i: (i, 0)),
        ],
        [pl.BlockSpec((tall, tile), lambda i: (0, i))] * 2,
        [shape(tall, features)] * 2,
    )(core.reshape(1), d_proj, d_gate, scan_weight, gate_weight)


def two_kernel(core_ref, a_ref, b_ref, own_ref, other_ref):
    core = core_ref[0]
    own_ref[...] = nn(a_ref[core], b_ref[...])
    other_ref[...] = nn(a_ref[1 - core], b_ref[...])


def two_slots(core, a, b):
    slots, rows, depth = a.shape
    right = b.shape[1]
    tile = 256
    return call(
        two_kernel,
        (right // tile,),
        [SMALL, fixed(slots, rows, depth), pl.BlockSpec((depth, tile), lambda i: (0, i))],
        [pl.BlockSpec((rows, tile), lambda i: (0, i))] * 2,
        [shape(rows, right)] * 2,
    )(core.reshape(1), a, b)


def valid_rows(bounds_ref, count):
    row = lax.broadcasted_iota(jnp.int32, (count, 1), 0) + pl.program_id(0) * count + bounds_ref[0]
    return jnp.where(row < bounds_ref[1], 1.0, 0.0)


def block_kernel(bounds_ref, in_ref, own_ref, came_ref, out_ref, sums_ref):
    valid = valid_rows(bounds_ref, SPAN)
    residual = in_ref[...].astype(F32)
    mixed = own_ref[...] + came_ref[...]
    value = valid * (residual + mixed)
    out_ref[...] = value.astype(BF16)
    lane = lax.broadcasted_iota(jnp.int32, (8, NS), 1)
    total = jnp.zeros((8, NS), F32)
    for number, part in enumerate((valid * residual * residual, valid * mixed * mixed, value * value)):
        part = jnp.sum(jnp.sum(part, axis=1, keepdims=True), axis=0, keepdims=True)
        total = jnp.where(lane == number, part, total)

    @pl.when(pl.program_id(0) == 0)
    def _():
        sums_ref[...] = jnp.zeros_like(sums_ref)

    sums_ref[...] += total


def block_rows(bounds, own_in, mixer_own, mixer_came):
    rows, features = own_in.shape
    tile = pl.BlockSpec((SPAN, features), lambda i: (i, 0))
    return call(
        block_kernel,
        (rows // SPAN,),
        [SMALL, tile, tile, tile],
        [tile, fixed(8, NS)],
        [shape(rows, features, dtype=BF16), shape(8, NS)],
    )(bounds, own_in, mixer_own, mixer_came)


def input_kernel(bounds_ref, in_ref, grad_ref, own_ref, came_ref, later_ref, across_ref, gain_ref, out_ref, gain_out):
    valid = valid_rows(bounds_ref, SPAN)
    at = pl.program_id(0)
    start = pl.multiple_of(HALO + at * SPAN, HALO)
    slope = own_ref[pl.ds(start, SPAN)] + came_ref[pl.ds(start, SPAN)]
    tail = jnp.where(at == pl.num_programs(0) - 1, later_ref[...] + across_ref[...], 0.0)
    slope = jnp.concatenate([slope[: SPAN - HALO], slope[SPAN - HALO :] + tail], axis=0)
    residual = in_ref[...].astype(F32)
    features = residual.shape[1]
    scale = lax.rsqrt(jnp.sum(residual * residual, axis=1, keepdims=True) / features + EPSILON)
    unit = residual * scale
    along = slope * gain_ref[...]
    mean = jnp.sum(along * unit, axis=1, keepdims=True) / features
    out_ref[...] = (valid * grad_ref[...].astype(F32) + scale * (along - unit * mean)).astype(BF16)

    @pl.when(at == 0)
    def _():
        gain_out[...] = jnp.zeros_like(gain_out)

    gain_out[...] += jnp.broadcast_to(jnp.sum(slope * unit, axis=0, keepdims=True), gain_out.shape)


def input_rows(bounds, own_in, own_grad, d_own, d_came, back_own, back_came, gain):
    rows, features = own_in.shape
    tile = pl.BlockSpec((SPAN, features), lambda i: (i, 0))
    return call(
        input_kernel,
        (rows // SPAN,),
        [
            SMALL, tile, tile, fixed(*d_own.shape), fixed(*d_came.shape), fixed(HALO, features), fixed(HALO, features),
            fixed(1, features),
        ],
        [tile, fixed(8, features)],
        [shape(rows, features, dtype=BF16), shape(8, features)],
    )(bounds, own_in, own_grad, d_own, d_came, back_own, back_came, gain)


def start_kernel(ends_ref, starts_out, decays_out):
    heads = head_map()
    nz, slots, depth, _ = starts_out.shape
    for slot in range(slots):
        running = jnp.zeros((depth, EC), F32)
        for k in range(nz):
            starts_out[k, slot] = running.astype(BF16)
            pieces = ends_ref[k, slot, :, EC:].astype(F32)
            total = pieces[0:1] + pieces[1:2] + pieces[2:3]
            decay = spread(jnp.broadcast_to(jnp.exp(total), (8, NS)), heads)
            decays_out[k, slot] = decay
            running = running * decay[0:1] + ends_ref[k, slot, :, :EC].astype(F32)


def start_states(ends):
    nz, slots, depth, _ = ends.shape
    return pl.pallas_call(
        start_kernel,
        out_shape=[shape(nz, slots, depth, EC, dtype=BF16), shape(nz, slots, 8, EC)],
        compiler_params=pltpu.CompilerParams(vmem_limit_bytes=VM * 1024 * 1024),
        cost_estimate=NO_COST,
    )(ends)


def later_kernel(tails_ref, decays_ref, backs_out):
    nz, slots, depth, _ = backs_out.shape
    for slot in range(slots):
        running = jnp.zeros((depth, EC), F32)
        for k in reversed(range(nz)):
            backs_out[k, slot] = running.astype(BF16)
            running = running * decays_ref[k, slot, 0:1] + tails_ref[k, slot].astype(F32)


def later_states(tails, decays):
    return pl.pallas_call(
        later_kernel,
        out_shape=shape(*tails.shape, dtype=BF16),
        compiler_params=pltpu.CompilerParams(vmem_limit_bytes=VM * 1024 * 1024),
        cost_estimate=NO_COST,
    )(tails, decays)


def shards(
    block_in,
    lengths,
    norm_gain,
    in_weight,
    conv_weight,
    conv_bias,
    step_bias,
    decay_log,
    skip_gain,
    out_gain,
    out_weight,
    grad_out,
):
    slot_count, row_count, features = block_in.shape
    nx, nz, ny = lax.axis_size("x"), lax.axis_size("z"), lax.axis_size("y")
    ix, iz, iy = lax.axis_index("x"), lax.axis_index("z"), lax.axis_index("y")
    core = lax.axis_index("core")
    rows = ny * row_count
    spans = rows // SPAN
    deep = in_weight.shape[0]
    thin = out_weight.shape[0]

    def half_of(value, width, which):
        parts = value.reshape(value.shape[:-1] + (nx, 2, width // (2 * nx)))
        chosen = take(parts, which, value.ndim)
        return chosen.reshape(value.shape[:-1] + (width // 2,))

    def one_slot(block):
        return by_index("y", take(block, iy, 0), swapped(take(block, 1 - iy, 0), "y")).reshape(rows, features)

    def by_slots(value):
        parts = value.reshape(ny, row_count, features)
        return take(parts, iy, 0), take(parts, 1 - iy, 0)

    def exchange(value):
        return lax.all_to_all(value, "z", 0, 0, tiled=True)

    def scaled(value):
        wide = value.astype(F32)
        return wide * lax.rsqrt(jnp.mean(wide * wide, axis=-1, keepdims=True) + EPSILON)

    tall = HALO + rows
    own_length = take(lengths, (ix * 2 + core) * slot_count + iy, 0)
    bounds = jnp.stack([iz * rows, own_length]).astype(jnp.int32)
    live = types.SimpleNamespace()

    def columns_of(which):
        heads_in = half_of(in_weight[:, E : 2 * E], E, which)
        write = in_weight[:, 2 * E : 2 * E + NS]
        read = in_weight[:, 2 * E + NS : E + CH]
        first = which == 0
        steps = jnp.pad(half_of(in_weight[:, E + CH :], H, which), ((0, 0), (0, NS - HC)))
        gate = half_of(in_weight[:, :E], E, which)
        return jnp.concatenate(
            [heads_in, jnp.where(first, write, read), steps, jnp.where(first, read, write), gate], axis=1
        )

    live.mine = columns_of(core)
    live.came = swapped(columns_of(1 - core), "core")
    live.block_in, live.grad_out = block_in, grad_out
    live.small = jnp.concatenate([norm_gain, conv_weight.reshape(-1), conv_bias, out_gain])
    settle(live)

    pieces = by_index("core", live.mine, live.came)
    live.scan = everyone(pieces[:, :, :WIDE], "z")
    live.gate = pieces[:, :, WIDE:]
    live.own_in = one_slot(live.block_in)
    live.own_grad = one_slot(live.grad_out)
    live.small = shared(jnp.pad(live.small, (0, -live.small.shape[0] % 1024)).reshape(-1, NS), ("x", "core", "z", "y"))
    del live.mine, live.came, live.block_in, live.grad_out
    settle(live)

    live.scan = join_line(live.scan)
    settle(live)
    live.scan = plane_first(live.scan)
    last_rows = live.own_in[rows - HALO :]
    live.other_in = swapped(live.own_in, "core")
    live.before_own = lax.ppermute(last_rows, "z", [(i, i + 1) for i in range(nz - 1)])
    across = [(c * nz + i, (1 - c) * nz + i + 1) for c in range(2) for i in range(nz - 1)]
    live.before_other = lax.ppermute(last_rows, ("core", "z"), across)
    small = live.small.reshape(2 * nx * nz * ny, -1)
    chan = CH // (2 * nx * nz * ny)
    gain_in = small[:, :deep].reshape(1, features).astype(F32)
    taps_all = small[:, deep : deep + CONV * chan].reshape(-1, CONV, chan).transpose(1, 0, 2).reshape(CONV, CH)
    at = deep + CONV * chan
    bias_all = small[:, at : at + chan].reshape(1, CH)
    gain_out_all = small[:, at + chan : at + chan + thin].reshape(E)
    taps_all = jnp.concatenate([taps_all, bias_all, jnp.zeros((3, CH), BF16)], axis=0).astype(F32)
    own_taps = jnp.where(core == 0, taps_all[:, E : E + NS], taps_all[:, E + NS :])
    other_taps = jnp.where(core == 0, taps_all[:, E + NS :], taps_all[:, E : E + NS])
    taps = jnp.concatenate(
        [half_of(taps_all[:, :E], E, core), own_taps, jnp.zeros((8, NS), F32), other_taps], axis=1
    )
    gain_out = jnp.broadcast_to(half_of(gain_out_all, E, core).astype(F32), (8, EC))

    def head_row(value):
        return jnp.pad(half_of(value, H, core), (0, NS - HC))

    heads_par = jnp.stack(
        [
            head_row(step_bias),
            head_row(jnp.exp(decay_log)),
            head_row(skip_gain),
            jnp.full((NS,), core, F32),
        ]
        + [jnp.zeros((NS,), F32)] * 4
    )

    live.gain_in, live.taps, live.own_taps, live.gain_out, live.heads_par = gain_in, taps, own_taps, gain_out, heads_par
    del live.small
    settle(live)

    live.scan = plane_stack(live.scan)
    settle(live)
    live.scan = plane_second(live.scan)
    live.gate = everyone(live.gate, "z")
    joined = jnp.concatenate(
        [by_index("core", live.before_own, live.before_other), by_index("core", live.own_in, live.other_in)], axis=1
    )
    live.normed = (scaled(joined) * live.gain_in).astype(BF16)
    del live.before_own, live.before_other, live.other_in
    settle(live)

    live.gate = join_line(live.gate)
    settle(live)
    live.gate = plane_first(live.gate)
    live.other_grad = swapped(live.own_grad, "core")
    live.proj, live.scan_weight = by_rows_of(live.normed, live.scan, False)
    del live.scan
    settle(live)

    live.gate = plane_stack(live.gate)
    live.out_rows = out_weight.reshape(2, thin // 2, features)
    settle(live)
    live.gate = plane_second(live.gate)
    live.out_rows = everyone(live.out_rows, "z")
    proj, taps, heads_par = live.proj, live.taps, live.heads_par
    whole_row = lambda *dims: pl.BlockSpec((1,) + dims, lambda s: (s,) + (0,) * len(dims))
    x, bc, step, cum, state_part, local = call(
        functools.partial(conv_kernel, rows, nz),
        (2,),
        [whole_row(tall, WIDE), fixed(8, WIDE), fixed(8, NS)],
        [
            whole_row(rows, EC), whole_row(rows, 2 * NS), whole_row(rows, NS), whole_row(rows, NS),
            pl.BlockSpec((nz, 1, NS // nz, EC + NS), lambda s: (0, s, 0, 0)), whole_row(spans, NS, EC),
        ],
        [
            shape(2, rows, EC), shape(2, rows, 2 * NS), shape(2, rows, NS), shape(2, rows, NS),
            shape(nz, 2, NS // nz, EC + NS, dtype=BF16), shape(2, spans, NS, EC, dtype=BF16),
        ],
    )(proj, taps, heads_par)

    live.state_part, live.x, live.bc, live.step, live.cum, live.local = state_part, x, bc, step, cum, local
    settle(live)

    live.out_rows = join_line(live.out_rows)
    settle(live)
    live.ends = exchange(live.state_part)
    live.out_rows = plane_first(live.out_rows)
    x, bc, step, cum, heads_par = live.x, live.bc, live.step, live.cum, live.heads_par
    in_span = lambda *dims: pl.BlockSpec((1, SPAN) + dims, lambda s, c: (s, c) + (0,) * len(dims))
    local_span = pl.BlockSpec((1, 1, NS, EC), lambda s, c: (s, c, 0, 0))
    state_spec = pl.BlockSpec((nz, 1, NS // nz, EC), lambda s, c: (0, s, 0, 0))
    before_spec = pl.BlockSpec((1, 1, 8, NS), lambda s, c: (s, c, 0, 0))
    part = call(
        intra_kernel,
        (2, spans),
        [in_span(EC), in_span(2 * NS), in_span(NS), in_span(NS), fixed(8, NS)],
        in_span(EC),
        shape(2, rows, EC),
        [
            pltpu.VMEM((SPAN, EC), BF16), pltpu.VMEM((SPAN, SPAN), F32), pltpu.VMEM((NS, SPAN), F32),
        ],
    )(x, bc, step, cum, heads_par)

    live.part = part
    del live.state_part
    settle(live)

    live.starts, live.decays = start_states(live.ends)
    live.out_rows = plane_stack(live.out_rows)
    del live.ends
    settle(live)
    live.state_in = exchange(live.starts)
    live.out_rows = plane_second(live.out_rows)
    live.gate, live.gate_weight = by_rows_of(live.normed, live.gate, False, halo=HALO)

    positions = iz * rows + jnp.arange(rows, dtype=jnp.int32)
    slot_lengths = jnp.stack(
        [take(lengths, (ix * 2 + s) * slot_count + iy, 0) for s in range(2)]
    )
    all_valid = positions[None, :] < slot_lengths[:, None]

    all_grad = by_index("core", live.own_grad, live.other_grad)
    live.d_mix = jnp.where(all_valid[:, :, None], all_grad, jnp.zeros_like(all_grad))
    del live.starts, live.other_grad
    settle(live)

    d_mixer_in, live.back_weight = by_rows_of(live.d_mix, live.out_rows, True, turned=True)
    span_ends = live.cum.reshape(2, spans, SPAN, NS)[:, :, SPAN - 1]
    before = jnp.cumsum(span_ends, axis=1) - span_ends
    live.before = jnp.broadcast_to(before[:, :, None], (2, spans, 8, NS))
    part, bc, cum, before, state_in, local, gate, gain_out = (
        live.part, live.bc, live.cum, live.before, live.state_in, live.local, live.gate, live.gain_out
    )
    ssm_out, sums = call(
        finish_kernel,
        (2, spans),
        [
            in_span(EC), in_span(2 * NS), in_span(NS), before_spec, state_spec, local_span, in_span(EC), in_span(EC),
            fixed(8, EC),
        ],
        [in_span(EC), in_span(NS)],
        [shape(2, rows, EC), shape(2, rows, NS)],
    )(part, bc, cum, before, state_in, local, gate, d_mixer_in, gain_out)
    sums = sums + swapped(sums, "core")
    rev = lambda *dims: pl.BlockSpec((1, SPAN) + dims, lambda s, c: (s, spans - 1 - c) + (0,) * len(dims))
    rev_local = pl.BlockSpec((1, 1, NS, EC), lambda s, c: (s, spans - 1 - c, 0, 0))
    mixer_in, d_ssm, d_gate, g_gain_out, back_part, back_local = call(
        functools.partial(gate_kernel, spans, nz),
        (2, spans),
        [rev(EC), rev(EC), rev(EC), rev(NS), fixed(8, EC), rev(2 * NS), rev(NS)],
        [rev(EC), rev(EC), rev(EC), fixed(8, EC), state_spec, rev_local],
        [
            shape(2, rows, EC, dtype=BF16), shape(2, rows, EC), shape(2, rows, EC, dtype=BF16), shape(8, EC),
            shape(nz, 2, NS // nz, EC, dtype=BF16), shape(2, spans, NS, EC, dtype=BF16),
        ],
        [pltpu.VMEM((NS, EC), F32)],
    )(ssm_out, gate, d_mixer_in, sums, gain_out, bc, cum)
    live.mixer_in, live.d_ssm, live.d_gate, live.back_part, live.back_local = mixer_in, d_ssm, d_gate, back_part, back_local
    live.g_gain_out = g_gain_out
    del live.part, live.gate, live.out_rows, live.gain_out
    settle(live)

    live.tails = exchange(live.back_part)
    live.out_sums = outer_cut(live.mixer_in, live.d_mix, True)
    live.gate_sums = outer_cut(live.normed, live.d_gate, False, HALO)
    live.mixer_own, live.mixer_part = two_slots(core, live.mixer_in, live.back_weight)
    del live.back_part, live.d_mix, live.mixer_in, live.back_weight
    settle(live)

    live.backs = later_states(live.tails, live.decays)
    del live.tails, live.decays
    settle(live)
    live.back_in = exchange(live.backs)
    live.out_sums = move_first(live.out_sums)

    def back_call(slot, kept):
        one = lambda *dims: pl.BlockSpec((1, SPAN) + dims, lambda c: (slot, c) + (0,) * len(dims))
        anywhere = [pl.BlockSpec(memory_space=pl.ANY)] * len(kept)
        return call(
            functools.partial(back_kernel, len(kept)),
            (spans,),
            [
                one(EC), one(2 * NS), one(NS), one(NS), pl.BlockSpec((1, 1, 8, NS), lambda c: (slot, c, 0, 0)), one(EC),
                pl.BlockSpec((nz, 1, NS // nz, EC), lambda c: (0, slot, 0, 0)),
                pl.BlockSpec((1, 1, NS, EC), lambda c: (slot, c, 0, 0)),
            ]
            + anywhere,
            [one(EC), one(2 * NS), one(NS), one(NS)],
            [shape(2, rows, EC), shape(2, rows, 2 * NS), shape(2, rows, NS), shape(2, rows, NS)],
            [
                pltpu.VMEM((SPAN, SPAN), F32), pltpu.VMEM((SPAN, SPAN), F32), pltpu.VMEM((NS, SPAN), F32),
                pltpu.VMEM((NS, SPAN), F32),
            ],
            input_output_aliases={8 + i: i for i in range(len(kept))},
        )(live.x, live.bc, live.step, live.cum, live.before, live.d_ssm, live.state_in, live.local, *kept)

    live.first_slot = back_call(0, ())
    del live.backs
    settle(live)

    live.gate_sums = move_first(live.gate_sums)
    live.mixer_part = swapped(live.mixer_part, "core")
    live.dxs, live.d_bc, live.d_cum, live.d_step = back_call(1, live.first_slot)
    del live.first_slot, live.before
    settle(live)

    live.out_sums = cut_second(live.out_sums)
    live.gate_sums = cut_second(live.gate_sums)
    settle(live)
    live.out_sums = move_second(live.out_sums)
    live.gate_sums = move_second(live.gate_sums)
    slot_state = pl.BlockSpec((nz, 1, NS // nz, EC), lambda s: (0, s, 0, 0))
    d_proj, mine, theirs, g_taps, g_heads = call(
        functools.partial(close_kernel, rows, nz),
        (2,),
        [
            whole_row(rows, EC), whole_row(rows, 2 * NS), whole_row(rows, NS), whole_row(rows, NS), whole_row(rows, EC),
            whole_row(tall, WIDE), fixed(8, WIDE), fixed(8, NS), whole_row(rows, EC), whole_row(rows, 2 * NS),
            whole_row(rows, NS), whole_row(rows, NS), slot_state, whole_row(spans, NS, EC), slot_state,
            whole_row(spans, NS, EC),
        ],
        [whole_row(tall, BACK), whole_row(rows, NS), whole_row(rows, NS), whole_row(8, EC), whole_row(8, NS)],
        [shape(2, tall, BACK, dtype=BF16), shape(2, rows, NS), shape(2, rows, NS), shape(2, 8, EC), shape(2, 8, NS)],
        [pltpu.VMEM((HALO + rows + HALO, EC), F32)],
    )(live.x, live.bc, live.step, live.cum, live.d_ssm, live.proj, live.taps, live.heads_par, live.dxs, live.d_bc, live.d_cum, live.d_step, live.state_in, live.local, live.back_in, live.back_local)

    live.d_proj, live.bc_mine, live.bc_theirs, live.g_taps, live.g_heads = d_proj, mine, theirs, g_taps, g_heads
    del live.x, live.bc, live.step, live.cum, live.d_ssm, live.taps, live.heads_par, live.dxs, live.d_bc, live.d_cum
    live.block_out, live.stats = block_rows(bounds, live.own_in, live.mixer_own, live.mixer_part)
    del live.d_step, live.state_in, live.local, live.back_in, live.back_local, live.mixer_own, live.mixer_part
    settle(live)

    live.out_sums = cut_line(live.out_sums)
    live.block_keep, live.block_send = by_slots(live.block_out)
    del live.block_out
    settle(live)
    live.out_sums = move(live.out_sums, "z")
    live.block_send = swapped(live.block_send, "y")
    mine, theirs, d_proj, proj, own_taps = (
        live.bc_mine, swapped(live.bc_theirs, "core"), live.d_proj, live.proj, live.own_taps
    )
    column = pl.BlockSpec((1, tall, NS), lambda s: (s, 0, OWN // NS))
    d_proj, g_own = call(
        functools.partial(own_kernel, rows),
        (2,),
        [pl.BlockSpec(memory_space=pl.ANY), whole_row(rows, NS), whole_row(rows, NS), column, fixed(8, NS)],
        [column, whole_row(8, NS)],
        [shape(2, tall, BACK, dtype=BF16), shape(2, 8, NS)],
        [pltpu.VMEM((HALO + rows + HALO, NS), F32)],
        input_output_aliases={0: 0},
    )(d_proj, mine, theirs, proj, own_taps)

    live.d_proj, live.g_own = d_proj, g_own
    live.scan_sums = outer_cut(live.normed, d_proj, False)
    del live.bc_mine, live.bc_theirs, live.proj, live.own_taps, live.normed
    settle(live)

    live.gate_sums = cut_line(live.gate_sums)
    settle(live)
    live.scan_sums = move_first(live.scan_sums)
    live.gate_sums = move(live.gate_sums, "z")
    live.d_own, live.d_came = to_normed(core, live.d_proj, live.d_gate, live.scan_weight, live.gate_weight)
    del live.d_proj, live.d_gate, live.scan_weight, live.gate_weight
    settle(live)

    live.scan_sums = cut_second(live.scan_sums)
    halo_own, halo_came = live.d_own[:HALO], live.d_came[:HALO]
    settle(live)
    live.scan_sums = move_second(live.scan_sums)
    live.back_own = lax.ppermute(halo_own, "z", [(i + 1, i) for i in range(nz - 1)])
    across = [(c * nz + i + 1, (1 - c) * nz + i) for c in range(2) for i in range(nz - 1)]
    live.back_came = lax.ppermute(halo_came, ("core", "z"), across)
    live.d_came = swapped(live.d_came, "core")
    live.out_sums = add_up(live.out_sums)
    live.gate_sums = add_up(live.gate_sums)
    settle(live)

    live.scan_sums = cut_line(live.scan_sums)
    settle(live)
    live.scan_sums = move(live.scan_sums, "z")
    live.grad_in, live.g_gain_in = input_rows(
        bounds, live.own_in, live.own_grad, live.d_own, live.d_came, live.back_own, live.back_came, live.gain_in
    )
    def spread_half(value, width):
        parts = value.reshape(value.shape[:-1] + (nx, 1, width // (2 * nx)))
        zero = jnp.zeros_like(parts)
        first = core == 0
        both = jnp.concatenate([jnp.where(first, parts, zero), jnp.where(first, zero, parts)], axis=-2)
        return both.reshape(value.shape[:-1] + (width,))

    taps_sum = jnp.sum(live.g_taps, axis=0)
    own_sum = jnp.sum(live.g_own, axis=0)
    nothing = jnp.zeros_like(own_sum)
    taps_sum = jnp.concatenate(
        [
            spread_half(taps_sum, E),
            jnp.where(core == 0, own_sum, nothing),
            jnp.where(core == 0, nothing, own_sum),
        ],
        axis=1,
    )
    head_sum = spread_half(jnp.sum(live.g_heads, axis=0)[:3, :HC], H)
    live.known = jnp.concatenate(
        [taps_sum[: CONV + 1].reshape(-1), spread_half(live.g_gain_out[0], E), head_sum.reshape(-1), live.stats[0, :3]]
    )
    del live.g_taps, live.g_own, live.g_heads, live.g_gain_out, live.stats

    settle(live)

    packed = jnp.concatenate([live.known, live.g_gain_in[0]])
    packed = sum_everywhere(jnp.pad(packed, (0, -packed.shape[0] % 1024)).reshape(-1, NS)).reshape(-1)
    grad_keep, grad_send = by_slots(live.grad_in)
    grad_in = by_index("y", grad_keep, swapped(grad_send, "y"))
    block_out = by_index("y", live.block_keep, live.block_send)
    g_out = live.out_sums.reshape(thin, features)

    def row_share(value):
        return take(value, core, 0), swapped(take(value, 1 - core, 0), "core")

    gate_mine, gate_came = row_share(live.gate_sums)
    scan_mine, scan_came = row_share(add_up(live.scan_sums))
    place_at = [0]
    for size in ((CONV + 1) * CH, E, 3 * H, 3, features):
        place_at.append(place_at[-1] + size)
    device = ((ix * 2 + core) * nz + iz) * ny + iy
    taps_total = packed[: place_at[1]].reshape(CONV + 1, CH)
    taps_mine = lax.dynamic_slice_in_dim(taps_total, device * chan, chan, 1)
    gain_out_mine = lax.dynamic_slice_in_dim(packed[place_at[1] : place_at[2]], device * thin, thin)
    gain_in_mine = lax.dynamic_slice_in_dim(packed[place_at[4] : place_at[5]], device * deep, deep)
    head_total = packed[place_at[2] : place_at[3]].reshape(3, H)
    valid_sums = packed[place_at[3] : place_at[4]]

    def both_halves(mine_part, came_part):
        pair = by_index("core", mine_part, came_part)
        width = mine_part.shape[-1]
        return pair.reshape(2, deep, nx, width // nx).transpose(1, 2, 0, 3).reshape(deep, 2 * width)

    own_pair = by_index("core", scan_mine[:, OWN:STEP], scan_came[:, OWN:STEP])
    g_in_weight = jnp.concatenate(
        [
            both_halves(gate_mine, gate_came),
            both_halves(scan_mine[:, :EC], scan_came[:, :EC]),
            own_pair[0],
            own_pair[1],
            both_halves(scan_mine[:, STEP : STEP + HC], scan_came[:, STEP : STEP + HC]),
        ],
        axis=1,
    )
    token_total = jnp.sum(lengths).astype(F32) * features
    rms_stats = jnp.sqrt(valid_sums / token_total)
    return (
        block_out,
        grad_in,
        gain_in_mine,
        g_in_weight,
        taps_mine[:CONV],
        taps_mine[CONV],
        head_total[0],
        head_total[1],
        head_total[2],
        gain_out_mine,
        g_out,
        rms_stats,
    )


def solution(mesh):
    nb, ns = mesh.shape["batch"], mesh.shape["seq"]
    fine = Mesh(mesh.devices.reshape(nb // 2, 2, ns // 2, 2), ("x", "core", "z", "y"))
    batch, seq = ("x", "core"), ("z", "y")
    every = batch + seq
    act = P(batch, seq, None)
    return jax.shard_map(
        shards,
        mesh=fine,
        in_specs=(
            act, P(), P(every), P(every, None), P(None, every), P(every), P(), P(), P(), P(every), P(every, None), act,
        ),
        out_specs=(
            act, act, P(every), P(every, None), P(None, every), P(every), P(), P(), P(), P(every), P(every, None), P(),
        ),
        check_vma=False,
    )
```

```python
import functools
import types

import jax
import jax.numpy as jnp
from jax import lax
from jax.experimental import pallas as pl
from jax.experimental.pallas import tpu as pltpu
from jax.sharding import Mesh
from jax.sharding import PartitionSpec as P

H = 48
P_SIZE = 64
NS = 128
CONV = 4
SPAN = 256
E = 3072
CH = 3328

HC = H // 2
EC = E // 2
HALO = 16
OWN = EC
STEP = EC + NS
OTHER = EC + 2 * NS
WIDE = EC + 3 * NS
BACK = EC + 2 * NS

EPSILON = 1e-05
BF16 = jnp.bfloat16
VM = 60
UNROLL = 6
F32 = jnp.float32


def settle(live):
    live.__dict__.update(lax.optimization_barrier(dict(live.__dict__)))


def others(piece, axis):
    size = lax.axis_size(axis)
    here = lax.axis_index(axis)
    moved = []
    for step in range(1, size):
        route = [(i, (i + step) % size) for i in range(size)]
        moved.append((lax.rem(here - step + size, size), lax.ppermute(piece, axis, route)))
    return moved


def everyone(piece, axis):
    return [(lax.axis_index(axis), piece)] + others(piece, axis)


def shared(value, axes):
    count = 1
    for axis in axes:
        count *= lax.axis_size(axis)
    return lax.all_to_all(jnp.broadcast_to(value, (count,) + value.shape), axes, 0, 0, tiled=True)


def by_index(axis, mine, other):
    first = lax.axis_index(axis) == 0
    return jnp.where(first, jnp.stack([mine, other]), jnp.stack([other, mine]))


def swapped(piece, axis):
    return lax.ppermute(piece, axis, [(0, 1), (1, 0)])


def take(value, index, axis):
    return lax.dynamic_index_in_dim(value, index, axis, keepdims=False)


def copy_plan(items):
    values, scalars, plan = [], [], []
    for piece, source, out, target in items:
        known = [i for i, v in enumerate(values) if v is piece]
        if not known:
            values.append(piece)
            known = [len(values) - 1]
        at = []
        for index in target:
            if index is None or isinstance(index, int):
                at.append(index)
            else:
                scalars.append(index)
                at.append((len(scalars) - 1,))
        plan.append((known[0], source, out, at))
    return values, jnp.stack(scalars).astype(jnp.int32), plan


def copy_all(plan, table, inputs, results, sems):
    copies = []
    for number, (known, source, out, at) in enumerate(plan):
        here = tuple(slice(None) if i is None else i for i in source)
        there = tuple(slice(None) if i is None else (table[i[0]] if isinstance(i, tuple) else i) for i in at)
        origin = inputs[known].at[here] if here else inputs[known]
        copies.append(pltpu.make_async_copy(origin, results[out].at[there], sems.at[number]))
    for copy in copies:
        copy.start()
    for copy in copies:
        copy.wait()


ANYWHERE = pl.BlockSpec(memory_space=pltpu.HBM)
NO_COST = pl.CostEstimate(flops=0, bytes_accessed=1024, transcendentals=0)


def assemble(outs, items, dtype):
    values, table, plan = copy_plan(items)
    count = len(values)

    def kernel(table_ref, *refs):
        copy_all(plan, table_ref, refs[:count], refs[count:-1], refs[-1])

    return pl.pallas_call(
        kernel,
        in_specs=[pl.BlockSpec(memory_space=pltpu.SMEM)] + [ANYWHERE] * count,
        out_specs=[pl.BlockSpec(memory_space=pltpu.VMEM)] * len(outs),
        out_shape=[jax.ShapeDtypeStruct(dims, dtype) for dims in outs],
        scratch_shapes=[pltpu.SemaphoreType.DMA((len(plan),))],
        compiler_params=pltpu.CompilerParams(vmem_limit_bytes=16 * 1024 * 1024),
        cost_estimate=NO_COST,
    )(table, *values)


ORDERS = (("y", "x"), ("x", "y"))


def join_line(everybody):
    _, rows, columns = everybody[0][1].shape
    items = [(piece, (half,), half, (index,)) for index, piece in everybody for half in range(2)]
    return assemble([(len(everybody), rows, columns)] * 2, items, everybody[0][1].dtype)


def plane_first(line):
    return [everyone(line[half], ORDERS[half][0]) for half in range(2)]


def plane_stack(held):
    items, outs = [], []
    for half, pieces in enumerate(held):
        outs.append((len(pieces),) + pieces[0][1].shape)
        items += [(piece, (), half, (index,)) for index, piece in pieces]
    return assemble(outs, items, held[0][0][1].dtype)


def plane_second(both):
    return [everyone(both[half], ORDERS[half][1]) for half in range(2)]


def plane_items(held, inner):
    nx, ny = lax.axis_size("x"), lax.axis_size("y")
    _, nz, rows, columns = held[0][0][1].shape
    dims = (nx, nz, ny, 2, rows, columns) if inner else (nx, 2, nz, ny, rows, columns)
    items = []
    for half, pieces in enumerate(held):
        for index, piece in pieces:
            for k in range(piece.shape[0]):
                at_x, at_y = (index, k) if half == 0 else (k, index)
                items.append((piece, (k,), 0, (at_x, None, at_y, half) if inner else (at_x, half, None, at_y)))
    return dims, items


def cut(value, axis, dim):
    size = lax.axis_size(axis)
    here = lax.axis_index(axis)
    return take(value, here, dim), [take(value, lax.rem(here + step, size), dim) for step in range(1, size)]


def move(held, axis):
    mine, going = held
    size = lax.axis_size(axis)
    came = []
    for step, piece in enumerate(going, 1):
        came.append(lax.ppermute(piece, axis, [(i, (i + step) % size) for i in range(size)]))
    return mine, came


def add_up(held):
    mine, came = held
    total = mine.astype(F32)
    for piece in came:
        total = total + piece.astype(F32)
    return total


def cut_first(whole, inner):
    return [
        cut(whole[:, :, :, half] if inner else whole[:, half], axis, 0 if axis == "x" else 2)
        for half, (_, axis) in enumerate(ORDERS)
    ]


def move_first(held):
    return [move(one, axis) for one, (_, axis) in zip(held, ORDERS)]


def cut_second(held):
    return [cut(add_up(one).astype(BF16), axis, 0 if axis == "x" else 1) for one, (axis, _) in zip(held, ORDERS)]


def move_second(held):
    return [move(one, axis) for one, (axis, _) in zip(held, ORDERS)]


def cut_line(held):
    return cut(jnp.stack([add_up(one).astype(BF16) for one in held]), "z", 1)


def sum_everywhere(value):
    for axis in ("core", "x", "z", "y"):
        size = lax.axis_size(axis)
        step = 1
        while step < size:
            route = [(i, i ^ step) for i in range(size)]
            value = value + lax.ppermute(value, axis, route)
            step *= 2
    return value


def nn(a, b):
    return lax.dot_general(a, b, (((1,), (0,)), ((), ())), preferred_element_type=F32)


def nt(a, b):
    return lax.dot_general(a, b, (((1,), (1,)), ((), ())), preferred_element_type=F32)


def tn(a, b):
    return lax.dot_general(a, b, (((0,), (0,)), ((), ())), preferred_element_type=F32)


def pieces_of(value, count):
    parts = []
    rest = value
    for index in range(count):
        part = rest.astype(BF16)
        parts.append(part)
        if index < count - 1:
            rest = rest - part.astype(F32)
    return parts


PIECE = 32


def nt_fine(a, b):
    a_high, a_low = pieces_of(a, 2)
    b_high, b_low = pieces_of(b, 2)
    return nt(jnp.concatenate([a_high, a_low, a_high], axis=1), jnp.concatenate([b_high, b_high, b_low], axis=1))


def head_map():
    row = lax.rem(lax.broadcasted_iota(jnp.int32, (NS, EC), 0), PIECE)
    lane = lax.broadcasted_iota(jnp.int32, (NS, EC), 1)
    inside = (lane >= row * P_SIZE) & (lane < row * P_SIZE + P_SIZE)
    return jnp.where(inside, 1.0, 0.0).astype(BF16)


def head_sums():
    row = lax.broadcasted_iota(jnp.int32, (EC, NS), 0)
    lane = lax.broadcasted_iota(jnp.int32, (EC, NS), 1)
    inside = (row >= lane * P_SIZE) & (row < lane * P_SIZE + P_SIZE)
    return jnp.where(inside, 1.0, 0.0).astype(BF16)


def packed(value):
    lane = lax.broadcasted_iota(jnp.int32, value.shape, 1)
    high, mid, low = (p.astype(F32) for p in pieces_of(jnp.where(lane < HC, value, 0.0), 3))
    return (high + pltpu.roll(mid, PIECE, 1) + pltpu.roll(low, 2 * PIECE, 1)).astype(BF16)


def spread(value, heads):
    return nn(packed(value), heads)


def gathered_heads(value, sums, count=1):
    return sum(nn(part, sums) for part in pieces_of(value, count))


def triangle(kind):
    row = lax.broadcasted_iota(jnp.int32, (SPAN, SPAN), 0)
    col = lax.broadcasted_iota(jnp.int32, (SPAN, SPAN), 1)
    keep = {"ge": row >= col, "gt": row > col, "le": row <= col}[kind]
    return jnp.where(keep, 1.0, 0.0)


def exact_sum(matrix, value):
    low = matrix.astype(BF16)
    return sum(nn(low, part) for part in pieces_of(value, 3))


def sigmoid(v):
    return 0.5 * jnp.tanh(0.5 * v) + 0.5


def softplus(v):
    return jnp.maximum(v, 0.0) + jnp.log1p(jnp.exp(-jnp.abs(v)))


def call(kernel, grid, in_specs, out_specs, out_shape, scratch=(), vmem=VM, **more):
    return pl.pallas_call(
        kernel,
        grid=grid,
        in_specs=in_specs,
        out_specs=out_specs,
        out_shape=out_shape,
        scratch_shapes=list(scratch),
        compiler_params=pltpu.CompilerParams(vmem_limit_bytes=vmem * 1024 * 1024),
        cost_estimate=NO_COST,
        **more,
    )


def shape(*dims, dtype=F32):
    return jax.ShapeDtypeStruct(dims, dtype)


def fixed(*dims):
    return pl.BlockSpec(dims, lambda *_: (0,) * len(dims))


def conv_kernel(rows, nz, proj, taps, heads_par, x_out, bc_out, step_out, cum_out, state_out, local_out):
    heads = head_map()
    spans = rows // SPAN
    lower = triangle("ge")
    state = jnp.zeros((NS, EC), F32)
    total = jnp.zeros((1, NS), F32)
    core_one = heads_par[3:4, :] > 0.5
    for span in range(spans):
        start = HALO + span * SPAN

        def activated(first, width):
            running = taps[4:5, first : first + width]
            for k in range(CONV):
                at = start - (CONV - 1) + k
                running = running + taps[k : k + 1, first : first + width] * proj[0, at : at + SPAN, first : first + width]
            return running * sigmoid(running)

        own = activated(OWN, NS)
        other = activated(OTHER, NS)
        write_full = jnp.where(core_one, other, own)
        write = write_full.astype(BF16)
        here = slice(span * SPAN, span * SPAN + SPAN)
        bc_out[0, here, :NS] = write_full
        bc_out[0, here, NS:] = jnp.where(core_one, own, other)
        raw = proj[0, start : start + SPAN, STEP : STEP + NS] + heads_par[0:1, :]
        step = softplus(raw)
        cum = exact_sum(lower, -step * heads_par[1:2, :])
        step_out[0, here] = step
        cum_out[0, here] = cum
        last = cum[SPAN - 1 : SPAN]
        tail_low = packed(jnp.exp(last - cum) * step)
        local_out[0, span] = state.astype(BF16)
        decay = spread(jnp.broadcast_to(jnp.exp(last), (8, NS)), heads)[0:1]
        wide = EC // 2
        fresh = []
        for half in range(2):
            cols = slice(half * wide, half * wide + wide)
            x = activated(half * wide, wide)
            x_out[0, here, cols] = x
            fresh.append(tn(write, (x * nn(tail_low, heads[:, cols])).astype(BF16)))
        state = state * decay + jnp.concatenate(fresh, axis=1)
        total = total + last
    depth = NS // nz
    for group in range(nz):
        state_out[group, 0, :, :EC] = state[group * depth : (group + 1) * depth].astype(BF16)
    row = lax.broadcasted_iota(jnp.int32, (depth, NS), 0)
    high, mid, low = (part.astype(F32) for part in pieces_of(total, 3))
    total_rows = jnp.where(row == 0, high, jnp.where(row == 1, mid, jnp.where(row == 2, low, 0.0))).astype(BF16)
    for group in range(nz):
        state_out[group, 0, :, EC:] = total_rows


def intra_kernel(x_ref, bc_ref, step_ref, cum_ref, heads_par, out_ref, xs_ref, cross_ref, cumt_ref):
    heads = head_map()
    step_wide = spread(step_ref[0], heads)
    xs_ref[...] = (x_ref[0] * step_wide).astype(BF16)
    cum = cum_ref[0]
    cumt_ref[...] = cum.T
    cross_ref[...] = nt_fine(bc_ref[0, :, NS:], bc_ref[0, :, :NS]) * triangle("ge")
    skip = spread(jnp.broadcast_to(heads_par[2:3, :], (8, NS)), heads)[0:1]
    out_ref[0] = x_ref[0] * skip
    low = lax.broadcasted_iota(jnp.int32, (SPAN, NS), 1) < P_SIZE

    def pair(p, carry):
        lanes = pl.ds(pl.multiple_of(p * NS, NS), NS)
        xs = xs_ref[:, lanes]
        made = []
        for j in range(2):
            h = 2 * p + j
            col = pltpu.roll(cum, lax.rem(NS - h, NS), 1)[:, 0:1]
            row = cumt_ref[pl.ds(h, 1), :]
            mix = jnp.exp(jnp.minimum(col - row, 0.0)) * cross_ref[...]
            made.append(nn(mix.astype(BF16), xs))
        out_ref[0, :, lanes] += jnp.where(low, made[0], made[1])
        return carry

    lax.fori_loop(0, HC // 2, pair, 0, unroll=UNROLL)


def span_state(state_ref, local_ref, before, heads):
    whole = jnp.concatenate([state_ref[g, 0] for g in range(state_ref.shape[0])], axis=0)
    decay = spread(jnp.broadcast_to(jnp.exp(before), (8, NS)), heads)[0:1]
    return whole.astype(F32) * decay + local_ref[0, 0].astype(F32)


def finish_kernel(part_ref, bc_ref, cum_ref, before_ref, state_ref, local_ref, gate_ref, dmix_ref, gain_ref, out_ref, sums_ref):
    heads = head_map()
    state = span_state(state_ref, local_ref, before_ref[0, 0, 0:1], heads).astype(BF16)
    grown = spread(jnp.exp(cum_ref[0]), heads)
    y = part_ref[0] + grown * nn(bc_ref[0, :, NS:].astype(BF16), state)
    out_ref[0] = y
    gate = gate_ref[0]
    gated = y * gate * sigmoid(gate)
    squares = jnp.sum(gated * gated, axis=1, keepdims=True)
    slopes = jnp.sum(gated * gain_ref[0:1, :] * dmix_ref[0], axis=1, keepdims=True)
    lane = lax.broadcasted_iota(jnp.int32, (SPAN, NS), 1)
    sums_ref[0] = jnp.where(lane == 0, squares, jnp.where(lane == 1, slopes, 0.0))


def gate_kernel(
    spans, nz, y_ref, gate_ref, dmix_ref, sums_ref, gain_ref, bc_ref, cum_ref,
    mix_out, dy_out, dgate_out, ggain_out, state_out, local_out, run_ref,
):
    step = pl.program_id(1)
    heads = head_map()
    squares = sums_ref[0, :, 0:1]
    slopes = sums_ref[0, :, 1:2]
    scale = lax.rsqrt(squares / E + EPSILON)
    y = y_ref[0]
    gate = gate_ref[0]
    soft = sigmoid(gate)
    silu = gate * soft
    gated = y * silu
    gain = gain_ref[0:1, :]
    dmix = dmix_ref[0]
    mix_out[0] = (gated * scale * gain).astype(BF16)
    dgated = scale * (gain * dmix - gated * (scale * scale * slopes / E))
    dy = dgated * silu
    dy_out[0] = dy
    dgate_out[0] = (dgated * y * (soft * (1.0 + gate * (1.0 - soft)))).astype(BF16)

    @pl.when((step == 0) & (pl.program_id(0) == 0))
    def _():
        ggain_out[...] = jnp.zeros_like(ggain_out)

    ggain_out[...] += jnp.broadcast_to(jnp.sum(gated * scale * dmix, axis=0, keepdims=True), (8, EC))

    @pl.when(step == 0)
    def _():
        run_ref[...] = jnp.zeros_like(run_ref)

    cum = cum_ref[0]
    grown = spread(jnp.exp(cum), heads)
    fresh = tn(bc_ref[0, :, NS:].astype(BF16), (dy * grown).astype(BF16))
    local_out[0, 0] = run_ref[...].astype(BF16)
    run_ref[...] = fresh + run_ref[...] * grown[SPAN - 1 : SPAN]

    @pl.when(step == spans - 1)
    def _():
        depth = NS // nz
        for group in range(nz):
            state_out[group, 0] = run_ref[group * depth : (group + 1) * depth].astype(BF16)


def back_kernel(kept, x_ref, bc_ref, step_ref, cum_ref, before_ref, dy_ref, state_ref, local_ref, *refs):
    dxs_out, dbc_out, dcum_out, dstep_out, cross_ref, dcross_ref, cumt_ref, rows_ref = refs[kept:]
    heads = head_map()
    sums = head_sums()
    cum = cum_ref[0]
    step = step_ref[0]
    cumt_ref[...] = cum.T
    write = bc_ref[0, :, :NS].astype(BF16)
    read = bc_ref[0, :, NS:].astype(BF16)
    mask = triangle("le")
    cross_ref[...] = nt_fine(bc_ref[0, :, :NS], bc_ref[0, :, NS:]) * mask
    dcross_ref[...] = jnp.zeros_like(dcross_ref)
    rows_ref[...] = jnp.zeros_like(rows_ref)
    lane = lax.broadcasted_iota(jnp.int32, (SPAN, NS), 1)
    low = lane < P_SIZE

    def pair(p, cols):
        lanes = pl.ds(pl.multiple_of(p * NS, NS), NS)
        x_high, x_low = (part.astype(F32) for part in pieces_of(x_ref[0, :, lanes], 2))
        dy, dy_low = pieces_of(dy_ref[0, :, lanes], 2)
        right = jnp.concatenate([dy, dy, dy_low], axis=1)
        made = []
        for j in range(2):
            h = 2 * p + j
            col = pltpu.roll(cum, lax.rem(NS - h, NS), 1)[:, 0:1]
            step_col = pltpu.roll(step, lax.rem(NS - h, NS), 1)[:, 0:1]
            row = cumt_ref[pl.ds(h, 1), :]
            decay = jnp.exp(jnp.minimum(row - col, 0.0))
            mine = low if j == 0 else ~low
            high = jnp.where(mine, x_high, 0.0).astype(BF16)
            rest = jnp.where(mine, x_low, 0.0).astype(BF16)
            slope = nt(jnp.concatenate([high, rest, high], axis=1), right) * decay
            cross = cross_ref[...]
            cols = jnp.where(lane == h, jnp.sum(slope * cross, axis=1, keepdims=True), cols)
            slope = slope * step_col
            dcross_ref[...] += slope
            rows_ref[pl.ds(h, 1), :] = jnp.sum(slope * cross, axis=0, keepdims=True)
            made.append(nn((decay * cross).astype(BF16), dy))
        dxs_out[0, :, lanes] = jnp.where(low, made[0], made[1])
        return cols

    cols = lax.fori_loop(0, HC // 2, pair, jnp.zeros((SPAN, NS), F32))
    dcross = (dcross_ref[...] * mask).astype(BF16)
    state = span_state(state_ref, local_ref, before_ref[0, 0, 0:1], heads).astype(BF16)
    grown = spread(jnp.exp(cum), heads)
    dye = dy_ref[0] * grown
    inter = gathered_heads(dye * nn(read, state), sums)
    dstep_out[0] = cols
    dbc_out[0, :, :NS] = nn(dcross, read)
    dbc_out[0, :, NS:] = tn(dcross, write) + nt(dye.astype(BF16), state)
    dcum_out[0] = rows_ref[...].T - step * cols + inter


def close_kernel(
    rows, nz, x_ref, bc_ref, step_ref, cum_ref, dy_ref, proj_ref, taps, heads_par, dxs_ref, dbc_ref, dcum_ref, dstep_ref,
    state_ref, local_ref, back_ref, blocal_ref, dproj_out, mine_out, theirs_out, gtaps_out, ghead_out, dpre_ref,
):
    core_one = heads_par[3:4, :] > 0.5
    heads = head_map()
    sums = head_sums()
    spans = rows // SPAN
    upper = triangle("le")
    below = triangle("gt")
    whole_in = jnp.concatenate([state_ref[g, 0] for g in range(nz)], axis=0).astype(F32)
    whole_back = jnp.concatenate([back_ref[g, 0] for g in range(nz)], axis=0).astype(F32)
    lasts = [cum_ref[0, (c + 1) * SPAN - 1 : (c + 1) * SPAN] for c in range(spans)]
    skip = spread(jnp.broadcast_to(heads_par[2:3, :], (8, NS)), heads)[0:1]
    real = lax.broadcasted_iota(jnp.int32, (SPAN, NS), 1) < HC
    dpre_ref[:HALO] = jnp.zeros((HALO, EC), F32)
    dpre_ref[HALO + rows :] = jnp.zeros((HALO, EC), F32)
    zero_row = jnp.zeros((1, NS), F32)
    gbias, gdecay, gskip = zero_row, zero_row, zero_row
    for span in range(spans):
        here = slice(span * SPAN, span * SPAN + SPAN)
        before = sum(lasts[:span], zero_row)
        after = sum(lasts[span + 1 :], zero_row)
        both = spread(jnp.exp(jnp.concatenate([before, after, lasts[span], jnp.zeros((5, NS), F32)], axis=0)), heads)
        state = whole_in * both[0:1] + local_ref[0, span].astype(F32)
        back = whole_back * both[1:2] + blocal_ref[0, span].astype(F32)
        back_low = back.astype(BF16)
        at_last = gathered_heads(
            jnp.broadcast_to(jnp.sum(state * back, axis=0, keepdims=True) * both[2:3], (8, EC)), sums, 2
        )[0:1]
        write = bc_ref[0, here, :NS].astype(BF16)
        cum = cum_ref[0, here]
        step = step_ref[0, here]
        x = x_ref[0, here]
        dy = dy_ref[0, here]
        tail = spread(jnp.exp(lasts[span] - cum), heads)
        step_wide = spread(step, heads)
        from_back = tail * nn(write, back_low)
        dxs = dxs_ref[0, here] + from_back
        later = gathered_heads(x * from_back, sums)
        dstep = dstep_ref[0, here] + later
        moved = step * later
        dwrite = dbc_ref[0, here, :NS] + nt((x * tail * step_wide).astype(BF16), back_low)
        dread = dbc_ref[0, here, NS:]
        mine_out[0, here] = jnp.where(core_one, dread, dwrite)
        theirs_out[0, here] = jnp.where(core_one, dwrite, dread)
        dlog = exact_sum(upper, dcum_ref[0, here]) + exact_sum(below, moved) + at_last
        raw = proj_ref[0, HALO + span * SPAN : HALO + span * SPAN + SPAN, STEP : STEP + NS] + heads_par[0:1, :]
        draw = jnp.where(real, (dstep - heads_par[1:2, :] * dlog) * sigmoid(raw), 0.0)
        dproj_out[0, HALO + span * SPAN : HALO + span * SPAN + SPAN, STEP : STEP + NS] = draw.astype(BF16)
        gbias = gbias + jnp.sum(draw, axis=0, keepdims=True)
        gdecay = gdecay + jnp.sum(jnp.where(real, dlog * (-step * heads_par[1:2, :]), 0.0), axis=0, keepdims=True)
        gskip = gskip + gathered_heads(jnp.broadcast_to(jnp.sum(dy * x, axis=0, keepdims=True), (8, EC)), sums, 3)[0:1]
        dx = dxs * step_wide + skip * dy
        start = HALO + span * SPAN
        pre = taps[4:5, :EC]
        for k in range(CONV):
            at = start - (CONV - 1) + k
            pre = pre + taps[k : k + 1, :EC] * proj_ref[0, at : at + SPAN, :EC]
        soft = sigmoid(pre)
        dpre_ref[start : start + SPAN] = dx * (soft * (1.0 + pre * (1.0 - soft)))
    conv_back(rows, dpre_ref, proj_ref, taps, 0, EC, dproj_out, 0, gtaps_out)
    dproj_out[0, :HALO, STEP : STEP + NS] = jnp.zeros((HALO, NS), BF16)
    ghead_out[0] = jnp.concatenate([gbias, gdecay, gskip, jnp.zeros((5, NS), F32)], axis=0)


def conv_back(rows, dpre_ref, proj_ref, taps, first, width, dproj_out, out_first, gtaps_out):
    sums = [jnp.zeros((1, width), F32)] * (CONV + 1)
    blocks = [(0, HALO)] + [(HALO + s * SPAN, SPAN) for s in range(rows // SPAN)]
    for start, count in blocks:
        running = jnp.zeros((count, width), F32)
        for k in range(CONV):
            at = start + (CONV - 1) - k
            running = running + taps[k : k + 1, first : first + width] * dpre_ref[at : at + count]
        dproj_out[0, start : start + count, out_first : out_first + width] = running.astype(BF16)
        if count == SPAN:
            dpre = dpre_ref[start : start + count]
            for k in range(CONV):
                at = start - (CONV - 1) + k
                sums[k] = sums[k] + jnp.sum(dpre * proj_ref[0, at : at + count, first : first + width], axis=0, keepdims=True)
            sums[CONV] = sums[CONV] + jnp.sum(dpre, axis=0, keepdims=True)
    gtaps_out[0, :, :width] = jnp.concatenate(sums + [jnp.zeros((3, width), F32)], axis=0)


def own_kernel(rows, dproj_in, mine_ref, came_ref, proj_ref, taps, dproj_out, gtaps_out, dpre_ref):
    dpre_ref[:HALO] = jnp.zeros((HALO, NS), F32)
    dpre_ref[HALO + rows :] = jnp.zeros((HALO, NS), F32)
    for span in range(rows // SPAN):
        start = HALO + span * SPAN
        pre = taps[4:5, :]
        for k in range(CONV):
            at = start - (CONV - 1) + k
            pre = pre + taps[k : k + 1, :] * proj_ref[0, at : at + SPAN]
        soft = sigmoid(pre)
        here = slice(span * SPAN, span * SPAN + SPAN)
        dconv = mine_ref[0, here] + came_ref[0, here]
        dpre_ref[start : start + SPAN] = dconv * (soft * (1.0 + pre * (1.0 - soft)))
    conv_back(rows, dpre_ref, proj_ref, taps, 0, NS, dproj_out, 0, gtaps_out)


def outer_kernel(halo, a_ref, b_ref, out_ref):
    slots, _, width = a_ref.shape
    left = a_ref[...][:, halo:].reshape(-1, width)
    right = b_ref[...].reshape(left.shape[0], -1)
    out_ref[...] = tn(left, right).astype(BF16)


def outer(a, b, halo=0):
    slots, tall, left = a.shape
    rows, right = b.shape[1:]
    tile = 256
    return call(
        functools.partial(outer_kernel, halo),
        (left // tile,),
        [pl.BlockSpec((slots, tall, tile), lambda i: (0, 0, i)), fixed(slots, rows, right)],
        pl.BlockSpec((tile, right), lambda i: (i, 0)),
        shape(left, right, dtype=BF16),
    )(a, b)


def outer_cut(a, b, inner, halo=0):
    nx, nz, ny = lax.axis_size("x"), lax.axis_size("z"), lax.axis_size("y")
    slots, tall, left = a.shape
    rows, right = b.shape[1:]
    deep = left // (2 * nx * nz * ny)
    if nx != 2 or nz % 2 or deep % 16:
        dims = (nx, nz, ny, 2, deep, right) if inner else (nx, 2, nz, ny, deep, right)
        return cut_first(outer(a, b, halo).reshape(dims), inner)
    tile = left // 4
    few = nz // 2

    def kernel(place_ref, a_ref, b_ref, stay0, go0, stay1, go1):
        at = pl.program_id(0)
        x = at // 2
        here = place_ref[0] == x
        low = place_ref[1] == 0
        part = a_ref[...][:, halo:].reshape(-1, tile)
        made = tn(part, b_ref[...].reshape(part.shape[0], -1)).astype(BF16)

        def split(value):
            return jnp.where(low, value[:, 0], value[:, 1]), jnp.where(low, value[:, 1], value[:, 0])

        if inner:
            made = made.reshape(few, ny, 2, deep, right)
            group = pl.ds((at % 2) * few, few)

            @pl.when(here)
            def _():
                stay0[group] = made[:, :, 0]

            @pl.when(jnp.logical_not(here))
            def _():
                go0[group] = made[:, :, 0]

            stay1[x, group], go1[x, group] = split(made[:, :, 1])
        else:
            made = made.reshape(nz, ny, deep, right)
            first = at % 2 == 0

            @pl.when(first & here)
            def _():
                stay0[...] = made

            @pl.when(first & jnp.logical_not(here))
            def _():
                go0[...] = made

            @pl.when(jnp.logical_not(first))
            def _():
                stay1[x], go1[x] = split(made)

    half0, half1 = (nz, ny, deep, right), (nx, nz, deep, right)
    stay0, go0, stay1, go1 = call(
        kernel,
        (4,),
        [
            pl.BlockSpec(memory_space=pltpu.SMEM), pl.BlockSpec((slots, tall, tile), lambda i: (0, 0, i)),
            fixed(slots, rows, right),
        ],
        [fixed(*half0), fixed(*half0), fixed(*half1), fixed(*half1)],
        [shape(*d, dtype=BF16) for d in (half0, half0, half1, half1)],
    )(jnp.stack([lax.axis_index("x"), lax.axis_index("y")]), a, b)
    return [(stay0, [go0]), (stay1, [go1])]


def rows_kernel(turned, halo, a_ref, b_ref, out_ref):
    value = a_ref[0, halo:]
    out_ref[0] = (nt if turned else nn)(value, b_ref[...])


def by_rows(a, b, turned=False, halo=0):
    slots, tall, depth = a.shape
    right = b.shape[0 if turned else 1]
    return call(
        functools.partial(rows_kernel, turned, halo),
        (slots,),
        [pl.BlockSpec((1, tall, depth), lambda s: (s, 0, 0)), fixed(*b.shape)],
        pl.BlockSpec((1, tall - halo, right), lambda s: (s, 0, 0)),
        shape(slots, tall - halo, right),
    )(a, b)


def by_rows_of(a, held, inner, turned=False, halo=0):
    dims, items = plane_items(held, inner)
    wide = dims[-1]
    deep = EC if inner else dims[0] * dims[1] * dims[2] * dims[3] * dims[4]
    if dims[4] % 16:
        whole = assemble([dims], items, BF16)[0].reshape(deep, wide)
        return by_rows(a, whole, turned, halo), whole
    values, table, plan = copy_plan(items)
    count = len(values)
    slots, tall, depth = a.shape
    right = deep if turned else wide

    def kernel(table_ref, a_ref, *refs):
        pieces, out_ref, whole_ref, held_ref, sems, whole_sem = refs[:count], *refs[count:]
        store = pltpu.make_async_copy(held_ref, whole_ref, whole_sem)

        @pl.when(pl.program_id(0) == 0)
        def _():
            copy_all(plan, table_ref, pieces, [held_ref], sems)
            store.start()

        matrix = held_ref[...].reshape(deep, wide)
        out_ref[0] = (nt if turned else nn)(a_ref[0, halo:], matrix)

        @pl.when(pl.program_id(0) == slots - 1)
        def _():
            store.wait()

    out, whole = call(
        kernel,
        (slots,),
        [pl.BlockSpec(memory_space=pltpu.SMEM), pl.BlockSpec((1, tall, depth), lambda s: (s, 0, 0))]
        + [ANYWHERE] * count,
        [pl.BlockSpec((1, tall - halo, right), lambda s: (s, 0, 0)), ANYWHERE],
        [shape(slots, tall - halo, right), shape(*dims, dtype=BF16)],
        [pltpu.VMEM(dims, BF16), pltpu.SemaphoreType.DMA((len(plan),)), pltpu.SemaphoreType.DMA],
    )(table, a, *values)
    return out, whole.reshape(deep, wide)


def normed_kernel(core_ref, dproj_ref, dgate_ref, scan_ref, gate_ref, own_ref, other_ref):
    scan, gate = scan_ref[...], gate_ref[...]
    core = core_ref[0]
    for slot, out_ref in ((core, own_ref), (1 - core, other_ref)):
        out_ref[:HALO] = nt(dproj_ref[slot, :HALO], scan)
        out_ref[HALO:] = nt(dproj_ref[slot, HALO:], scan) + nt(dgate_ref[slot], gate)


SMALL = pl.BlockSpec(memory_space=pltpu.SMEM)


def to_normed(core, d_proj, d_gate, scan_weight, gate_weight):
    slots, tall, _ = d_proj.shape
    features = gate_weight.shape[0]
    tile = 256
    return call(
        normed_kernel,
        (features // tile,),
        [
            SMALL, fixed(slots, tall, BACK), fixed(slots, tall - HALO, EC),
            pl.BlockSpec((tile, BACK), lambda i: (i, 0)), pl.BlockSpec((tile, EC), lambda i: (i, 0)),
        ],
        [pl.BlockSpec((tall, tile), lambda i: (0, i))] * 2,
        [shape(tall, features)] * 2,
    )(core.reshape(1), d_proj, d_gate, scan_weight, gate_weight)


def two_kernel(core_ref, a_ref, b_ref, own_ref, other_ref):
    core = core_ref[0]
    own_ref[...] = nn(a_ref[core], b_ref[...])
    other_ref[...] = nn(a_ref[1 - core], b_ref[...])


def two_slots(core, a, b):
    slots, rows, depth = a.shape
    right = b.shape[1]
    tile = 256
    return call(
        two_kernel,
        (right // tile,),
        [SMALL, fixed(slots, rows, depth), pl.BlockSpec((depth, tile), lambda i: (0, i))],
        [pl.BlockSpec((rows, tile), lambda i: (0, i))] * 2,
        [shape(rows, right)] * 2,
    )(core.reshape(1), a, b)


def valid_rows(bounds_ref, count):
    row = lax.broadcasted_iota(jnp.int32, (count, 1), 0) + pl.program_id(0) * count + bounds_ref[0]
    return jnp.where(row < bounds_ref[1], 1.0, 0.0)


def block_kernel(bounds_ref, in_ref, own_ref, came_ref, out_ref, sums_ref):
    valid = valid_rows(bounds_ref, SPAN)
    residual = in_ref[...].astype(F32)
    mixed = own_ref[...] + came_ref[...]
    value = valid * (residual + mixed)
    out_ref[...] = value.astype(BF16)
    lane = lax.broadcasted_iota(jnp.int32, (8, NS), 1)
    total = jnp.zeros((8, NS), F32)
    for number, part in enumerate((valid * residual * residual, valid * mixed * mixed, value * value)):
        part = jnp.sum(jnp.sum(part, axis=1, keepdims=True), axis=0, keepdims=True)
        total = jnp.where(lane == number, part, total)

    @pl.when(pl.program_id(0) == 0)
    def _():
        sums_ref[...] = jnp.zeros_like(sums_ref)

    sums_ref[...] += total


def block_rows(bounds, own_in, mixer_own, mixer_came):
    rows, features = own_in.shape
    tile = pl.BlockSpec((SPAN, features), lambda i: (i, 0))
    return call(
        block_kernel,
        (rows // SPAN,),
        [SMALL, tile, tile, tile],
        [tile, fixed(8, NS)],
        [shape(rows, features, dtype=BF16), shape(8, NS)],
    )(bounds, own_in, mixer_own, mixer_came)


def input_kernel(bounds_ref, in_ref, grad_ref, own_ref, came_ref, later_ref, across_ref, gain_ref, out_ref, gain_out):
    valid = valid_rows(bounds_ref, SPAN)
    at = pl.program_id(0)
    start = pl.multiple_of(HALO + at * SPAN, HALO)
    slope = own_ref[pl.ds(start, SPAN)] + came_ref[pl.ds(start, SPAN)]
    tail = jnp.where(at == pl.num_programs(0) - 1, later_ref[...] + across_ref[...], 0.0)
    slope = jnp.concatenate([slope[: SPAN - HALO], slope[SPAN - HALO :] + tail], axis=0)
    residual = in_ref[...].astype(F32)
    features = residual.shape[1]
    scale = lax.rsqrt(jnp.sum(residual * residual, axis=1, keepdims=True) / features + EPSILON)
    unit = residual * scale
    along = slope * gain_ref[...]
    mean = jnp.sum(along * unit, axis=1, keepdims=True) / features
    out_ref[...] = (valid * grad_ref[...].astype(F32) + scale * (along - unit * mean)).astype(BF16)

    @pl.when(at == 0)
    def _():
        gain_out[...] = jnp.zeros_like(gain_out)

    gain_out[...] += jnp.broadcast_to(jnp.sum(slope * unit, axis=0, keepdims=True), gain_out.shape)


def input_rows(bounds, own_in, own_grad, d_own, d_came, back_own, back_came, gain):
    rows, features = own_in.shape
    tile = pl.BlockSpec((SPAN, features), lambda i: (i, 0))
    return call(
        input_kernel,
        (rows // SPAN,),
        [
            SMALL, tile, tile, fixed(*d_own.shape), fixed(*d_came.shape), fixed(HALO, features), fixed(HALO, features),
            fixed(1, features),
        ],
        [tile, fixed(8, features)],
        [shape(rows, features, dtype=BF16), shape(8, features)],
    )(bounds, own_in, own_grad, d_own, d_came, back_own, back_came, gain)


def start_kernel(ends_ref, starts_out, decays_out):
    heads = head_map()
    nz, slots, depth, _ = starts_out.shape
    for slot in range(slots):
        running = jnp.zeros((depth, EC), F32)
        for k in range(nz):
            starts_out[k, slot] = running.astype(BF16)
            pieces = ends_ref[k, slot, :, EC:].astype(F32)
            total = pieces[0:1] + pieces[1:2] + pieces[2:3]
            decay = spread(jnp.broadcast_to(jnp.exp(total), (8, NS)), heads)
            decays_out[k, slot] = decay
            running = running * decay[0:1] + ends_ref[k, slot, :, :EC].astype(F32)


def start_states(ends):
    nz, slots, depth, _ = ends.shape
    return pl.pallas_call(
        start_kernel,
        out_shape=[shape(nz, slots, depth, EC, dtype=BF16), shape(nz, slots, 8, EC)],
        compiler_params=pltpu.CompilerParams(vmem_limit_bytes=VM * 1024 * 1024),
        cost_estimate=NO_COST,
    )(ends)


def later_kernel(tails_ref, decays_ref, backs_out):
    nz, slots, depth, _ = backs_out.shape
    for slot in range(slots):
        running = jnp.zeros((depth, EC), F32)
        for k in reversed(range(nz)):
            backs_out[k, slot] = running.astype(BF16)
            running = running * decays_ref[k, slot, 0:1] + tails_ref[k, slot].astype(F32)


def later_states(tails, decays):
    return pl.pallas_call(
        later_kernel,
        out_shape=shape(*tails.shape, dtype=BF16),
        compiler_params=pltpu.CompilerParams(vmem_limit_bytes=VM * 1024 * 1024),
        cost_estimate=NO_COST,
    )(tails, decays)


def shards(
    block_in,
    lengths,
    norm_gain,
    in_weight,
    conv_weight,
    conv_bias,
    step_bias,
    decay_log,
    skip_gain,
    out_gain,
    out_weight,
    grad_out,
):
    slot_count, row_count, features = block_in.shape
    nx, nz, ny = lax.axis_size("x"), lax.axis_size("z"), lax.axis_size("y")
    ix, iz, iy = lax.axis_index("x"), lax.axis_index("z"), lax.axis_index("y")
    core = lax.axis_index("core")
    rows = ny * row_count
    spans = rows // SPAN
    deep = in_weight.shape[0]
    thin = out_weight.shape[0]

    def half_of(value, width, which):
        parts = value.reshape(value.shape[:-1] + (nx, 2, width // (2 * nx)))
        chosen = take(parts, which, value.ndim)
        return chosen.reshape(value.shape[:-1] + (width // 2,))

    def one_slot(block):
        return by_index("y", take(block, iy, 0), swapped(take(block, 1 - iy, 0), "y")).reshape(rows, features)

    def by_slots(value):
        parts = value.reshape(ny, row_count, features)
        return take(parts, iy, 0), take(parts, 1 - iy, 0)

    def exchange(value):
        return lax.all_to_all(value, "z", 0, 0, tiled=True)

    def scaled(value):
        wide = value.astype(F32)
        return wide * lax.rsqrt(jnp.mean(wide * wide, axis=-1, keepdims=True) + EPSILON)

    tall = HALO + rows
    own_length = take(lengths, (ix * 2 + core) * slot_count + iy, 0)
    bounds = jnp.stack([iz * rows, own_length]).astype(jnp.int32)
    live = types.SimpleNamespace()

    def columns_of(which):
        heads_in = half_of(in_weight[:, E : 2 * E], E, which)
        write = in_weight[:, 2 * E : 2 * E + NS]
        read = in_weight[:, 2 * E + NS : E + CH]
        first = which == 0
        steps = jnp.pad(half_of(in_weight[:, E + CH :], H, which), ((0, 0), (0, NS - HC)))
        gate = half_of(in_weight[:, :E], E, which)
        return jnp.concatenate(
            [heads_in, jnp.where(first, write, read), steps, jnp.where(first, read, write), gate], axis=1
        )

    live.mine = columns_of(core)
    live.came = swapped(columns_of(1 - core), "core")
    live.block_in, live.grad_out = block_in, grad_out
    live.small = jnp.concatenate([norm_gain, conv_weight.reshape(-1), conv_bias, out_gain])
    settle(live)

    pieces = by_index("core", live.mine, live.came)
    live.scan = everyone(pieces[:, :, :WIDE], "z")
    live.gate = pieces[:, :, WIDE:]
    live.own_in = one_slot(live.block_in)
    live.own_grad = one_slot(live.grad_out)
    live.small = shared(jnp.pad(live.small, (0, -live.small.shape[0] % 1024)).reshape(-1, NS), ("x", "core", "z", "y"))
    del live.mine, live.came, live.block_in, live.grad_out
    settle(live)

    live.scan = join_line(live.scan)
    settle(live)
    live.scan = plane_first(live.scan)
    last_rows = live.own_in[rows - HALO :]
    live.other_in = swapped(live.own_in, "core")
    live.before_own = lax.ppermute(last_rows, "z", [(i, i + 1) for i in range(nz - 1)])
    across = [(c * nz + i, (1 - c) * nz + i + 1) for c in range(2) for i in range(nz - 1)]
    live.before_other = lax.ppermute(last_rows, ("core", "z"), across)
    small = live.small.reshape(2 * nx * nz * ny, -1)
    chan = CH // (2 * nx * nz * ny)
    gain_in = small[:, :deep].reshape(1, features).astype(F32)
    taps_all = small[:, deep : deep + CONV * chan].reshape(-1, CONV, chan).transpose(1, 0, 2).reshape(CONV, CH)
    at = deep + CONV * chan
    bias_all = small[:, at : at + chan].reshape(1, CH)
    gain_out_all = small[:, at + chan : at + chan + thin].reshape(E)
    taps_all = jnp.concatenate([taps_all, bias_all, jnp.zeros((3, CH), BF16)], axis=0).astype(F32)
    own_taps = jnp.where(core == 0, taps_all[:, E : E + NS], taps_all[:, E + NS :])
    other_taps = jnp.where(core == 0, taps_all[:, E + NS :], taps_all[:, E : E + NS])
    taps = jnp.concatenate(
        [half_of(taps_all[:, :E], E, core), own_taps, jnp.zeros((8, NS), F32), other_taps], axis=1
    )
    gain_out = jnp.broadcast_to(half_of(gain_out_all, E, core).astype(F32), (8, EC))

    def head_row(value):
        return jnp.pad(half_of(value, H, core), (0, NS - HC))

    heads_par = jnp.stack(
        [
            head_row(step_bias),
            head_row(jnp.exp(decay_log)),
            head_row(skip_gain),
            jnp.full((NS,), core, F32),
        ]
        + [jnp.zeros((NS,), F32)] * 4
    )

    live.gain_in, live.taps, live.own_taps, live.gain_out, live.heads_par = gain_in, taps, own_taps, gain_out, heads_par
    del live.small
    settle(live)

    live.scan = plane_stack(live.scan)
    settle(live)
    live.scan = plane_second(live.scan)
    live.gate = everyone(live.gate, "z")
    joined = jnp.concatenate(
        [by_index("core", live.before_own, live.before_other), by_index("core", live.own_in, live.other_in)], axis=1
    )
    live.normed = (scaled(joined) * live.gain_in).astype(BF16)
    del live.before_own, live.before_other, live.other_in
    settle(live)

    live.gate = join_line(live.gate)
    settle(live)
    live.gate = plane_first(live.gate)
    live.other_grad = swapped(live.own_grad, "core")
    live.proj, live.scan_weight = by_rows_of(live.normed, live.scan, False)
    del live.scan
    settle(live)

    live.gate = plane_stack(live.gate)
    live.out_rows = out_weight.reshape(2, thin // 2, features)
    settle(live)
    live.gate = plane_second(live.gate)
    live.out_rows = everyone(live.out_rows, "z")
    proj, taps, heads_par = live.proj, live.taps, live.heads_par
    whole_row = lambda *dims: pl.BlockSpec((1,) + dims, lambda s: (s,) + (0,) * len(dims))
    x, bc, step, cum, state_part, local = call(
        functools.partial(conv_kernel, rows, nz),
        (2,),
        [whole_row(tall, WIDE), fixed(8, WIDE), fixed(8, NS)],
        [
            whole_row(rows, EC), whole_row(rows, 2 * NS), whole_row(rows, NS), whole_row(rows, NS),
            pl.BlockSpec((nz, 1, NS // nz, EC + NS), lambda s: (0, s, 0, 0)), whole_row(spans, NS, EC),
        ],
        [
            shape(2, rows, EC), shape(2, rows, 2 * NS), shape(2, rows, NS), shape(2, rows, NS),
            shape(nz, 2, NS // nz, EC + NS, dtype=BF16), shape(2, spans, NS, EC, dtype=BF16),
        ],
    )(proj, taps, heads_par)

    live.state_part, live.x, live.bc, live.step, live.cum, live.local = state_part, x, bc, step, cum, local
    settle(live)

    live.out_rows = join_line(live.out_rows)
    settle(live)
    live.ends = exchange(live.state_part)
    live.out_rows = plane_first(live.out_rows)
    x, bc, step, cum, heads_par = live.x, live.bc, live.step, live.cum, live.heads_par
    in_span = lambda *dims: pl.BlockSpec((1, SPAN) + dims, lambda s, c: (s, c) + (0,) * len(dims))
    local_span = pl.BlockSpec((1, 1, NS, EC), lambda s, c: (s, c, 0, 0))
    state_spec = pl.BlockSpec((nz, 1, NS // nz, EC), lambda s, c: (0, s, 0, 0))
    before_spec = pl.BlockSpec((1, 1, 8, NS), lambda s, c: (s, c, 0, 0))
    part = call(
        intra_kernel,
        (2, spans),
        [in_span(EC), in_span(2 * NS), in_span(NS), in_span(NS), fixed(8, NS)],
        in_span(EC),
        shape(2, rows, EC),
        [
            pltpu.VMEM((SPAN, EC), BF16), pltpu.VMEM((SPAN, SPAN), F32), pltpu.VMEM((NS, SPAN), F32),
        ],
    )(x, bc, step, cum, heads_par)

    live.part = part
    del live.state_part
    settle(live)

    live.starts, live.decays = start_states(live.ends)
    live.out_rows = plane_stack(live.out_rows)
    del live.ends
    settle(live)
    live.state_in = exchange(live.starts)
    live.out_rows = plane_second(live.out_rows)
    live.gate, live.gate_weight = by_rows_of(live.normed, live.gate, False, halo=HALO)

    positions = iz * rows + jnp.arange(rows, dtype=jnp.int32)
    slot_lengths = jnp.stack(
        [take(lengths, (ix * 2 + s) * slot_count + iy, 0) for s in range(2)]
    )
    all_valid = positions[None, :] < slot_lengths[:, None]

    all_grad = by_index("core", live.own_grad, live.other_grad)
    live.d_mix = jnp.where(all_valid[:, :, None], all_grad, jnp.zeros_like(all_grad))
    del live.starts, live.other_grad
    settle(live)

    d_mixer_in, live.back_weight = by_rows_of(live.d_mix, live.out_rows, True, turned=True)
    span_ends = live.cum.reshape(2, spans, SPAN, NS)[:, :, SPAN - 1]
    before = jnp.cumsum(span_ends, axis=1) - span_ends
    live.before = jnp.broadcast_to(before[:, :, None], (2, spans, 8, NS))
    part, bc, cum, before, state_in, local, gate, gain_out = (
        live.part, live.bc, live.cum, live.before, live.state_in, live.local, live.gate, live.gain_out
    )
    ssm_out, sums = call(
        finish_kernel,
        (2, spans),
        [
            in_span(EC), in_span(2 * NS), in_span(NS), before_spec, state_spec, local_span, in_span(EC), in_span(EC),
            fixed(8, EC),
        ],
        [in_span(EC), in_span(NS)],
        [shape(2, rows, EC), shape(2, rows, NS)],
    )(part, bc, cum, before, state_in, local, gate, d_mixer_in, gain_out)
    sums = sums + swapped(sums, "core")
    rev = lambda *dims: pl.BlockSpec((1, SPAN) + dims, lambda s, c: (s, spans - 1 - c) + (0,) * len(dims))
    rev_local = pl.BlockSpec((1, 1, NS, EC), lambda s, c: (s, spans - 1 - c, 0, 0))
    mixer_in, d_ssm, d_gate, g_gain_out, back_part, back_local = call(
        functools.partial(gate_kernel, spans, nz),
        (2, spans),
        [rev(EC), rev(EC), rev(EC), rev(NS), fixed(8, EC), rev(2 * NS), rev(NS)],
        [rev(EC), rev(EC), rev(EC), fixed(8, EC), state_spec, rev_local],
        [
            shape(2, rows, EC, dtype=BF16), shape(2, rows, EC), shape(2, rows, EC, dtype=BF16), shape(8, EC),
            shape(nz, 2, NS // nz, EC, dtype=BF16), shape(2, spans, NS, EC, dtype=BF16),
        ],
        [pltpu.VMEM((NS, EC), F32)],
    )(ssm_out, gate, d_mixer_in, sums, gain_out, bc, cum)
    live.mixer_in, live.d_ssm, live.d_gate, live.back_part, live.back_local = mixer_in, d_ssm, d_gate, back_part, back_local
    live.g_gain_out = g_gain_out
    del live.part, live.gate, live.out_rows, live.gain_out
    settle(live)

    live.tails = exchange(live.back_part)
    live.out_sums = outer_cut(live.mixer_in, live.d_mix, True)
    live.gate_sums = outer_cut(live.normed, live.d_gate, False, HALO)
    live.mixer_own, live.mixer_part = two_slots(core, live.mixer_in, live.back_weight)
    del live.back_part, live.d_mix, live.mixer_in, live.back_weight
    settle(live)

    live.backs = later_states(live.tails, live.decays)
    del live.tails, live.decays
    settle(live)
    live.back_in = exchange(live.backs)
    live.out_sums = move_first(live.out_sums)

    def back_call(slot, kept):
        one = lambda *dims: pl.BlockSpec((1, SPAN) + dims, lambda c: (slot, c) + (0,) * len(dims))
        anywhere = [pl.BlockSpec(memory_space=pl.ANY)] * len(kept)
        return call(
            functools.partial(back_kernel, len(kept)),
            (spans,),
            [
                one(EC), one(2 * NS), one(NS), one(NS), pl.BlockSpec((1, 1, 8, NS), lambda c: (slot, c, 0, 0)), one(EC),
                pl.BlockSpec((nz, 1, NS // nz, EC), lambda c: (0, slot, 0, 0)),
                pl.BlockSpec((1, 1, NS, EC), lambda c: (slot, c, 0, 0)),
            ]
            + anywhere,
            [one(EC), one(2 * NS), one(NS), one(NS)],
            [shape(2, rows, EC), shape(2, rows, 2 * NS), shape(2, rows, NS), shape(2, rows, NS)],
            [
                pltpu.VMEM((SPAN, SPAN), F32), pltpu.VMEM((SPAN, SPAN), F32), pltpu.VMEM((NS, SPAN), F32),
                pltpu.VMEM((NS, SPAN), F32),
            ],
            input_output_aliases={8 + i: i for i in range(len(kept))},
        )(live.x, live.bc, live.step, live.cum, live.before, live.d_ssm, live.state_in, live.local, *kept)

    live.first_slot = back_call(0, ())
    del live.backs
    settle(live)

    live.gate_sums = move_first(live.gate_sums)
    live.mixer_part = swapped(live.mixer_part, "core")
    live.dxs, live.d_bc, live.d_cum, live.d_step = back_call(1, live.first_slot)
    del live.first_slot, live.before
    settle(live)

    live.out_sums = cut_second(live.out_sums)
    live.gate_sums = cut_second(live.gate_sums)
    settle(live)
    live.out_sums = move_second(live.out_sums)
    live.gate_sums = move_second(live.gate_sums)
    slot_state = pl.BlockSpec((nz, 1, NS // nz, EC), lambda s: (0, s, 0, 0))
    d_proj, mine, theirs, g_taps, g_heads = call(
        functools.partial(close_kernel, rows, nz),
        (2,),
        [
            whole_row(rows, EC), whole_row(rows, 2 * NS), whole_row(rows, NS), whole_row(rows, NS), whole_row(rows, EC),
            whole_row(tall, WIDE), fixed(8, WIDE), fixed(8, NS), whole_row(rows, EC), whole_row(rows, 2 * NS),
            whole_row(rows, NS), whole_row(rows, NS), slot_state, whole_row(spans, NS, EC), slot_state,
            whole_row(spans, NS, EC),
        ],
        [whole_row(tall, BACK), whole_row(rows, NS), whole_row(rows, NS), whole_row(8, EC), whole_row(8, NS)],
        [shape(2, tall, BACK, dtype=BF16), shape(2, rows, NS), shape(2, rows, NS), shape(2, 8, EC), shape(2, 8, NS)],
        [pltpu.VMEM((HALO + rows + HALO, EC), F32)],
    )(live.x, live.bc, live.step, live.cum, live.d_ssm, live.proj, live.taps, live.heads_par, live.dxs, live.d_bc, live.d_cum, live.d_step, live.state_in, live.local, live.back_in, live.back_local)

    live.d_proj, live.bc_mine, live.bc_theirs, live.g_taps, live.g_heads = d_proj, mine, theirs, g_taps, g_heads
    del live.x, live.bc, live.step, live.cum, live.d_ssm, live.taps, live.heads_par, live.dxs, live.d_bc, live.d_cum
    del live.d_step, live.state_in, live.local, live.back_in, live.back_local
    settle(live)

    live.out_sums = cut_line(live.out_sums)
    settle(live)
    live.out_sums = move(live.out_sums, "z")
    mine, theirs, d_proj, proj, own_taps = (
        live.bc_mine, swapped(live.bc_theirs, "core"), live.d_proj, live.proj, live.own_taps
    )
    column = pl.BlockSpec((1, tall, NS), lambda s: (s, 0, OWN // NS))
    d_proj, g_own = call(
        functools.partial(own_kernel, rows),
        (2,),
        [pl.BlockSpec(memory_space=pl.ANY), whole_row(rows, NS), whole_row(rows, NS), column, fixed(8, NS)],
        [column, whole_row(8, NS)],
        [shape(2, tall, BACK, dtype=BF16), shape(2, 8, NS)],
        [pltpu.VMEM((HALO + rows + HALO, NS), F32)],
        input_output_aliases={0: 0},
    )(d_proj, mine, theirs, proj, own_taps)

    live.d_proj, live.g_own = d_proj, g_own
    live.scan_sums = outer_cut(live.normed, d_proj, False)
    del live.bc_mine, live.bc_theirs, live.proj, live.own_taps, live.normed
    settle(live)

    live.gate_sums = cut_line(live.gate_sums)
    settle(live)
    live.scan_sums = move_first(live.scan_sums)
    live.gate_sums = move(live.gate_sums, "z")
    live.d_own, live.d_came = to_normed(core, live.d_proj, live.d_gate, live.scan_weight, live.gate_weight)
    del live.d_proj, live.d_gate, live.scan_weight, live.gate_weight
    settle(live)

    live.scan_sums = cut_second(live.scan_sums)
    halo_own, halo_came = live.d_own[:HALO], live.d_came[:HALO]
    settle(live)
    live.scan_sums = move_second(live.scan_sums)
    live.block_out, live.stats = block_rows(bounds, live.own_in, live.mixer_own, live.mixer_part)
    del live.mixer_own, live.mixer_part
    live.back_own = lax.ppermute(halo_own, "z", [(i + 1, i) for i in range(nz - 1)])
    across = [(c * nz + i + 1, (1 - c) * nz + i) for c in range(2) for i in range(nz - 1)]
    live.back_came = lax.ppermute(halo_came, ("core", "z"), across)
    live.d_came = swapped(live.d_came, "core")
    live.out_sums = add_up(live.out_sums)
    live.gate_sums = add_up(live.gate_sums)
    settle(live)

    live.scan_sums = cut_line(live.scan_sums)
    live.block_keep, live.block_send = by_slots(live.block_out)
    del live.block_out
    settle(live)
    live.scan_sums = move(live.scan_sums, "z")
    live.block_send = swapped(live.block_send, "y")
    live.grad_in, live.g_gain_in = input_rows(
        bounds, live.own_in, live.own_grad, live.d_own, live.d_came, live.back_own, live.back_came, live.gain_in
    )
    def spread_half(value, width):
        parts = value.reshape(value.shape[:-1] + (nx, 1, width // (2 * nx)))
        zero = jnp.zeros_like(parts)
        first = core == 0
        both = jnp.concatenate([jnp.where(first, parts, zero), jnp.where(first, zero, parts)], axis=-2)
        return both.reshape(value.shape[:-1] + (width,))

    taps_sum = jnp.sum(live.g_taps, axis=0)
    own_sum = jnp.sum(live.g_own, axis=0)
    nothing = jnp.zeros_like(own_sum)
    taps_sum = jnp.concatenate(
        [
            spread_half(taps_sum, E),
            jnp.where(core == 0, own_sum, nothing),
            jnp.where(core == 0, nothing, own_sum),
        ],
        axis=1,
    )
    head_sum = spread_half(jnp.sum(live.g_heads, axis=0)[:3, :HC], H)
    live.known = jnp.concatenate(
        [taps_sum[: CONV + 1].reshape(-1), spread_half(live.g_gain_out[0], E), head_sum.reshape(-1), live.stats[0, :3]]
    )
    del live.g_taps, live.g_own, live.g_heads, live.g_gain_out, live.stats

    settle(live)

    packed = jnp.concatenate([live.known, live.g_gain_in[0]])
    packed = sum_everywhere(jnp.pad(packed, (0, -packed.shape[0] % 1024)).reshape(-1, NS)).reshape(-1)
    grad_keep, grad_send = by_slots(live.grad_in)
    grad_in = by_index("y", grad_keep, swapped(grad_send, "y"))
    block_out = by_index("y", live.block_keep, live.block_send)
    g_out = live.out_sums.reshape(thin, features)

    def row_share(value):
        return take(value, core, 0), swapped(take(value, 1 - core, 0), "core")

    gate_mine, gate_came = row_share(live.gate_sums)
    scan_mine, scan_came = row_share(add_up(live.scan_sums))
    place_at = [0]
    for size in ((CONV + 1) * CH, E, 3 * H, 3, features):
        place_at.append(place_at[-1] + size)
    device = ((ix * 2 + core) * nz + iz) * ny + iy
    taps_total = packed[: place_at[1]].reshape(CONV + 1, CH)
    taps_mine = lax.dynamic_slice_in_dim(taps_total, device * chan, chan, 1)
    gain_out_mine = lax.dynamic_slice_in_dim(packed[place_at[1] : place_at[2]], device * thin, thin)
    gain_in_mine = lax.dynamic_slice_in_dim(packed[place_at[4] : place_at[5]], device * deep, deep)
    head_total = packed[place_at[2] : place_at[3]].reshape(3, H)
    valid_sums = packed[place_at[3] : place_at[4]]

    def both_halves(mine_part, came_part):
        pair = by_index("core", mine_part, came_part)
        width = mine_part.shape[-1]
        return pair.reshape(2, deep, nx, width // nx).transpose(1, 2, 0, 3).reshape(deep, 2 * width)

    own_pair = by_index("core", scan_mine[:, OWN:STEP], scan_came[:, OWN:STEP])
    g_in_weight = jnp.concatenate(
        [
            both_halves(gate_mine, gate_came),
            both_halves(scan_mine[:, :EC], scan_came[:, :EC]),
            own_pair[0],
            own_pair[1],
            both_halves(scan_mine[:, STEP : STEP + HC], scan_came[:, STEP : STEP + HC]),
        ],
        axis=1,
    )
    token_total = jnp.sum(lengths).astype(F32) * features
    rms_stats = jnp.sqrt(valid_sums / token_total)
    return (
        block_out,
        grad_in,
        gain_in_mine,
        g_in_weight,
        taps_mine[:CONV],
        taps_mine[CONV],
        head_total[0],
        head_total[1],
        head_total[2],
        gain_out_mine,
        g_out,
        rms_stats,
    )


def solution(mesh):
    nb, ns = mesh.shape["batch"], mesh.shape["seq"]
    fine = Mesh(mesh.devices.reshape(nb // 2, 2, ns // 2, 2), ("x", "core", "z", "y"))
    batch, seq = ("x", "core"), ("z", "y")
    every = batch + seq
    act = P(batch, seq, None)
    return jax.shard_map(
        shards,
        mesh=fine,
        in_specs=(
            act, P(), P(every), P(every, None), P(None, every), P(every), P(), P(), P(), P(every), P(every, None), act,
        ),
        out_specs=(
            act, act, P(every), P(every, None), P(None, every), P(every), P(), P(), P(), P(every), P(every, None), P(),
        ),
        check_vma=False,
    )
```
